256 devices in a mesh: pipe: 4 (over y), dp: 64 (over x, z, core).
Axes of the slice: x: 4, y: 4, z: 8, core: 2. Of those that a mesh axis runs over, the one named last changes fastest.
Arguments:
- features: bfloat16 [1024, 12, 12, 512], P('dp'), may hold values from -16 to 16
- labels: int32 [1024], P('dp'), may hold values from 0 to 999
- micro_count: int32 [64], P('dp'), may hold values from 1 to 8, as said below
- cells_per_section: int32 [4], replicated, may hold values from 1 to 3, as said below
- point_weight: bfloat16 [4, 3, 512, 512], P('pipe'), may hold values from -0.125 to 0.125
- depth_three: bfloat16 [4, 3, 3, 512], P('pipe'), may hold values from -2 to 2
- depth_five: bfloat16 [4, 5, 5, 512], P('pipe'), may hold values from -1.25 to 1.25
- depth_seven: bfloat16 [4, 7, 7, 512], P('pipe'), may hold values from -0.875 to 0.875
- head_weight: float32 [512, 1000], replicated, may hold values from -9 to 9
Outputs:
- loss: float32 [], replicated
- point_grad: float32 [4, 3, 512, 512], P('pipe')
- three_grad: float32 [4, 3, 3, 512], P('pipe')
- five_grad: float32 [4, 5, 5, 512], P('pipe')
- seven_grad: float32 [4, 7, 7, 512], P('pipe')
The draws below stay inside these ranges and needn't reach their ends.
Inputs may be any that keep to these rules, and one draw needn't show every extreme that they name: Replica r's live micro-batches are its first micro_count[r] ones; some replica has 8. Section q holds cells_per_section[q] cells; some section holds 3.
All inputs are finite; a program needn't handle non-finite values.
Results may differ from the reference program's by a relative error of at most 0.013.
Values may be sent and summed in bfloat16 or wider, within the bound.
A program may use at most 192 MiB of HBM per device.

```python
import jax
import jax.numpy as jnp
from jax import lax

C = 512
CLASSES = 1000
SIDE = 12
MB_IMG = 2
MICRO = 8
CELLS_MAX = 3
BATCH = 1024
N_PIPE = 4
N_DP = 64


def draw_micro_count(key, part):
    key_counts, key_fullest = jax.random.split(jax.random.fold_in(key, 11))
    counts = jax.random.randint(key_counts, (N_DP,), 1, MICRO + 1)
    fullest = jax.random.randint(key_fullest, (), 0, N_DP)
    return jnp.where(jnp.arange(N_DP) == fullest, MICRO, counts).astype(jnp.int32)


def draw_cells_per_section(key, part):
    key_counts, key_fullest = jax.random.split(jax.random.fold_in(key, 23))
    counts = jax.random.randint(key_counts, (N_PIPE,), 1, CELLS_MAX + 1)
    fullest = jax.random.randint(key_fullest, (), 0, N_PIPE)
    return jnp.where(jnp.arange(N_PIPE) == fullest, CELLS_MAX, counts).astype(jnp.int32)


def plant(entries, stream_key, low, largest):
    longest = entries.shape.index(max(entries.shape))
    spots = []
    for shift in (0, 1):
        where = [jax.random.randint(jax.random.fold_in(stream_key, axis), (), 0, length) for axis, length in enumerate(entries.shape)]
        where[longest] = (where[longest] + shift) % entries.shape[longest]
        spots.append(tuple(where))
    return entries.at[spots[0]].set(low).at[spots[1]].set(largest)


def strengthened(array, key, source, target, blocks, factor):
    owner, partner = [(jnp.arange(array.shape[axis_at]) // (array.shape[axis_at] // blocks)).reshape([-1 if axis == axis_at else 1 for axis in range(array.ndim)]) for axis_at in (source, target)]
    chosen = jax.random.permutation(key, blocks)[partner]
    strong = (owner == chosen) | (owner == (partner + blocks // 2) % blocks)
    return jnp.where(strong, factor * array, array)


def level_of(own_key, shape, cuts, low, high):
    gain, own = 1.0, jax.random.fold_in(own_key, 6)
    for dim, shards_of in cuts:
        heights = jnp.exp(jax.random.uniform(jax.random.fold_in(own, dim), (shards_of,), jnp.float32, low / len(cuts), high / len(cuts)))
        gain = gain * jnp.repeat(heights, shape[dim] // shards_of).reshape([-1 if axis == dim else 1 for axis in range(len(shape))])
    return gain


def normal_values(key, dims, width, limit, cuts=(), dtype=jnp.bfloat16):
    values = width * jax.random.normal(key, dims, jnp.float32)
    if cuts:
        values = values * level_of(key, dims, cuts, -0.22, 0.18)
    return jnp.clip(values, -limit, limit).astype(dtype)


def gaussian_with(key, extent, width, reach, pieces, heavy, held_as=jnp.bfloat16):
    values = width * jax.random.normal(key, extent, jnp.float32)
    if pieces:
        values = values * level_of(key, extent, pieces, -0.22, 0.18)
    return jnp.clip(strengthened(values, jax.random.fold_in(key, 3), *heavy), -reach, reach).astype(held_as)


def setup_inputs(seed: int = 0) -> dict:
    key_list = jax.random.split(jax.random.key(seed), 10)
    return {
        "features": gaussian_with(key_list[0], (BATCH, SIDE, SIDE, C), 1.0, 16.0, ((0, 64),), (0, 3, 64, 4.0)),
        "labels": plant(jax.random.randint(key_list[1], (BATCH,), 0, CLASSES), jax.random.fold_in(key_list[1], 1), 0, CLASSES - 1).astype(jnp.int32),
        "micro_count": draw_micro_count(jax.random.fold_in(key_list[9], 71), 0),
        "cells_per_section": draw_cells_per_section(jax.random.fold_in(key_list[9], 71), 0),
        "point_weight": normal_values(key_list[4], (N_PIPE, CELLS_MAX, C, C), (4 * C) ** -0.5, 0.125, ((0, 4),)),
        "depth_three": normal_values(key_list[5], (N_PIPE, 3, 3, C), 9 ** -0.5, 2.0, ((0, 4),)),
        "depth_five": normal_values(key_list[6], (N_PIPE, 5, 5, C), 25 ** -0.5, 1.25, ((0, 4),)),
        "depth_seven": normal_values(key_list[7], (N_PIPE, 7, 7, C), 49 ** -0.5, 0.875, ((0, 4),)),
        "head_weight": normal_values(key_list[8], (C, CLASSES), 1.5, 9.0, (), jnp.float32),
    }


LOGIT_CAP = 30.0


def depth_conv(rectified, kernel):
    kernel_size = kernel.shape[0]
    half_size = (kernel_size - 1) // 2
    side_rows = rectified.shape[1]
    side_cols = rectified.shape[2]
    padded = jnp.pad(rectified, ((0, 0), (half_size, half_size), (half_size, half_size), (0, 0)))
    running = jnp.zeros_like(rectified)
    for offset_row in range(kernel_size):
        for offset_col in range(kernel_size):
            running = running + padded[:, offset_row:offset_row + side_rows, offset_col:offset_col + side_cols, :] * kernel[offset_row, offset_col]
    return running


def depth_back(cotangent, kernel):
    kernel_size = kernel.shape[0]
    half_size = (kernel_size - 1) // 2
    side_rows = cotangent.shape[1]
    side_cols = cotangent.shape[2]
    padded = jnp.pad(cotangent, ((0, 0), (half_size, half_size), (half_size, half_size), (0, 0)))
    running = jnp.zeros_like(cotangent)
    for offset_row in range(kernel_size):
        for offset_col in range(kernel_size):
            flip_row = kernel_size - 1 - offset_row
            flip_col = kernel_size - 1 - offset_col
            running = running + padded[:, flip_row:flip_row + side_rows, flip_col:flip_col + side_cols, :] * kernel[offset_row, offset_col]
    return running


def kernel_terms(rectified, cotangent, kernel_size):
    half_size = (kernel_size - 1) // 2
    side_rows = rectified.shape[1]
    side_cols = rectified.shape[2]
    padded = jnp.pad(rectified, ((0, 0), (half_size, half_size), (half_size, half_size), (0, 0)))
    kernel_rows = []
    for offset_row in range(kernel_size):
        row_terms = []
        for offset_col in range(kernel_size):
            window = padded[:, offset_row:offset_row + side_rows, offset_col:offset_col + side_cols, :]
            row_terms.append(jnp.sum(window * cotangent, axis=(0, 1, 2)))
        kernel_rows.append(jnp.stack(row_terms))
    return jnp.stack(kernel_rows)


def make_deep(inputs, kernel):
    rectified = jnp.maximum(inputs, 0).astype(jnp.float32)
    return depth_conv(rectified, kernel.astype(jnp.float32)).astype(jnp.bfloat16)


def forward_cell(inputs, kernel, weight):
    channels = inputs.shape[-1]
    depthwise = make_deep(inputs, kernel)
    mixed = jnp.dot(depthwise.reshape(-1, channels), weight, preferred_element_type=jnp.float32)
    result = inputs.astype(jnp.float32) + mixed.reshape(inputs.shape)
    return result.astype(jnp.bfloat16), depthwise


def backward_cell(inputs, depthwise, kernel, weight, cotangent):
    channels = inputs.shape[-1]
    flat_cot = cotangent.reshape(-1, channels)
    point_part = lax.dot_general(depthwise.reshape(-1, channels), flat_cot, (((0,), (0,)), ((), ())), preferred_element_type=jnp.float32)
    deep_cot = lax.dot_general(flat_cot, weight, (((1,), (1,)), ((), ())), preferred_element_type=jnp.float32).reshape(inputs.shape)
    rectified = jnp.maximum(inputs, 0).astype(jnp.float32)
    kernel_part = kernel_terms(rectified, deep_cot, kernel.shape[0])
    rect_cot = depth_back(deep_cot, kernel.astype(jnp.float32))
    backward = (cotangent.astype(jnp.float32) + jnp.where(inputs > 0, rect_cot, 0.0)).astype(jnp.bfloat16)
    return backward, point_part, kernel_part


def head_loss(final_act, head_weight, targets, live_mask):
    pooled = jnp.mean(final_act.astype(jnp.float32), axis=(1, 2))
    scores = jnp.dot(pooled, head_weight, precision=lax.Precision.HIGHEST)
    capped = jnp.tanh(scores / LOGIT_CAP)
    logits = LOGIT_CAP * capped
    exponent = jnp.exp(logits)
    softmax_total = jnp.sum(exponent, axis=-1, keepdims=True)
    classes = lax.broadcasted_iota(jnp.int32, logits.shape, 1)
    onehot = (classes == targets.astype(jnp.int32)[:, None]).astype(jnp.float32)
    row_loss = (jnp.log(softmax_total[:, 0]) - jnp.sum(logits * onehot, axis=-1)) * live_mask
    logit_cot = (exponent / softmax_total - onehot) * live_mask[:, None]
    score_cot = logit_cot * (1.0 - capped * capped)
    pooled_cot = lax.dot_general(score_cot, head_weight, (((1,), (1,)), ((), ())), precision=lax.Precision.HIGHEST)
    positions = final_act.shape[1] * final_act.shape[2]
    spread = jnp.broadcast_to((pooled_cot / positions)[:, None, None, :], final_act.shape)
    return jnp.sum(row_loss), spread.astype(jnp.bfloat16)


def reference(features, labels, micro_count, cells_per_section, point_weight, depth_three, depth_five, depth_seven, head_weight):
    kernels = (depth_three, depth_five, depth_seven)
    group_rows = MICRO * MB_IMG
    shaped = features.reshape(N_DP, group_rows, SIDE, SIDE, C)
    label_rows = labels.reshape(N_DP, group_rows)

    def replica(state_carry, slices):
        loss_sum, point_sum, three_sum, five_sum, seven_sum = state_carry
        kernel_sums = [three_sum, five_sum, seven_sum]
        images, targets, live_count = slices
        live_mask = ((jnp.arange(group_rows) // MB_IMG) < live_count).astype(jnp.float32)
        current = images
        record = []
        for section_q in range(N_PIPE):
            for cell_slot in range(CELLS_MAX):
                active = cell_slot < cells_per_section[section_q]
                result, depthwise = forward_cell(current, kernels[cell_slot][section_q], point_weight[section_q, cell_slot])
                record.append((section_q, cell_slot, active, current, depthwise))
                current = jnp.where(active, result, current)
        part_loss, cotangent = head_loss(current, head_weight, targets, live_mask)
        for section_q, cell_slot, active, inputs, depthwise in reversed(record):
            backward, point_part, kernel_part = backward_cell(inputs, depthwise, kernels[cell_slot][section_q], point_weight[section_q, cell_slot], cotangent)
            active_scale = active.astype(jnp.float32)
            point_sum = point_sum.at[section_q, cell_slot].add(point_part * active_scale)
            kernel_sums[cell_slot] = kernel_sums[cell_slot].at[section_q].add(kernel_part * active_scale)
            cotangent = jnp.where(active, backward, cotangent)
        return (loss_sum + part_loss, point_sum, kernel_sums[0], kernel_sums[1], kernel_sums[2]), None

    start_state = (
        jnp.zeros((), jnp.float32),
        jnp.zeros((N_PIPE, CELLS_MAX, C, C), jnp.float32),
        jnp.zeros((N_PIPE, 3, 3, C), jnp.float32),
        jnp.zeros((N_PIPE, 5, 5, C), jnp.float32),
        jnp.zeros((N_PIPE, 7, 7, C), jnp.float32),
    )
    finished, spent = lax.scan(replica, start_state, (shaped, label_rows, micro_count))
    return (finished[0], finished[1], finished[2], finished[3], finished[4])
```

```python
import functools

import jax
import jax.numpy as jnp
import ml_dtypes
import numpy as np
from jax import lax
from jax.experimental import pallas as pl
from jax.experimental.pallas import tpu as pltpu
from jax.sharding import PartitionSpec as P

SIDE = 12
AREA = SIDE * SIDE
MB_IMG = 2
CELLS_MAX = 3
TAPS = 7
TAP_ROWS = 64
LOGIT_CAP = 30.0
CYCLE = SIDE + TAPS // 2
HALF = 128
IMAGES = 4


def transform_tables():
    slots = [(0, 0)]
    seen = {(0, 0)}
    for u in range(CYCLE):
        for v in range(CYCLE):
            if (u, v) in seen:
                continue
            seen.add((u, v))
            seen.add(((-u) % CYCLE, (-v) % CYCLE))
            slots.append((u, v))
    count = len(slots)
    waves = np.array(slots, np.float64)
    sites = np.array([(i, j) for i in range(SIDE) for j in range(SIDE)], np.float64)
    reach = TAPS // 2
    shifts = np.array(
        [(u - reach, v - reach) for u in range(TAPS) for v in range(TAPS)], np.float64
    )
    weight = np.where((waves == 0).all(1), 1.0, 2.0)[:, None] / CYCLE**2
    site_angle = 2 * np.pi * ((waves @ sites.T) % CYCLE) / CYCLE
    tap_angle = 2 * np.pi * ((waves @ shifts.T) % CYCLE) / CYCLE
    into = np.zeros((2 * HALF, AREA))
    into[:count] = np.cos(site_angle)
    into[HALF : HALF + count] = -np.sin(site_angle)
    back = np.zeros((AREA, 2 * HALF))
    back[:, :count] = (np.cos(site_angle) * weight).T
    back[:, HALF : HALF + count] = -(np.sin(site_angle) * weight).T
    tap_into = np.zeros((2 * HALF, TAP_ROWS))
    tap_into[:count, : TAPS * TAPS] = np.cos(tap_angle)
    tap_into[HALF : HALF + count, : TAPS * TAPS] = np.sin(tap_angle)
    tap_back = np.zeros((TAP_ROWS, 2 * HALF))
    tap_back[: TAPS * TAPS, :count] = (np.cos(tap_angle) * weight).T
    tap_back[: TAPS * TAPS, HALF : HALF + count] = -(np.sin(tap_angle) * weight).T
    return [pair_of(table) for table in (into, back, tap_into, tap_back)]


def pair_of(table):
    high = table.astype(ml_dtypes.bfloat16)
    low = (table - high.astype(np.float64)).astype(ml_dtypes.bfloat16)
    return np.stack([high, low])


def mul(a, b):
    return jnp.dot(a, b, preferred_element_type=jnp.float32)


def halves(values):
    high = values.astype(jnp.bfloat16)
    low = (values - high.astype(jnp.float32)).astype(jnp.bfloat16)
    return high, low


def cells_kernel(
    cells_ref,
    features_ref,
    targets_ref,
    live_ref,
    weight_ref,
    taps_ref,
    head_ref,
    into_ref,
    back_ref,
    tap_into_ref,
    tap_back_ref,
    point_ref,
    kernel_ref,
    loss_ref,
    order_ref,
    acts_ref,
    deep_ref,
    wave_ref,
    cot_ref,
    deep_cot_ref,
    total_ref,
):
    sections = weight_ref.shape[0] // CELLS_MAX
    count = jnp.int32(0)
    for section in range(sections):
        held = cells_ref[section]
        for slot in range(CELLS_MAX):
            order_ref[count + slot] = section * CELLS_MAX + slot
        for slot in range(1, CELLS_MAX):

            @pl.when(slot >= held)
            def _(cell=section * CELLS_MAX + slot):
                point_ref[cell] = jnp.zeros(point_ref.shape[1:], point_ref.dtype)
                kernel_ref[cell] = jnp.zeros(kernel_ref.shape[1:], kernel_ref.dtype)

        count = count + held

    acts_ref[0] = features_ref[...]

    def rows_of(image):
        return pl.ds(image * AREA, AREA)

    def forward(step, _):
        cell = order_ref[step]
        taps = taps_ref[cell]
        wave = mul(tap_into_ref[0], taps) + mul(tap_into_ref[1], taps)
        wave_ref[step] = wave
        wave_re, wave_im = wave[:HALF], wave[HALF:]
        for image in range(IMAGES):
            site = jnp.maximum(acts_ref[step, rows_of(image)], 0)
            seen = mul(into_ref[0], site) + mul(into_ref[1], site)
            seen_re, seen_im = seen[:HALF], seen[HALF:]
            mixed = jnp.concatenate(
                [
                    seen_re * wave_re - seen_im * wave_im,
                    seen_re * wave_im + seen_im * wave_re,
                ],
                axis=0,
            )
            high, low = halves(mixed)
            deep = mul(back_ref[0], high) + mul(back_ref[0], low) + mul(back_ref[1], high)
            deep_ref[step, rows_of(image)] = deep.astype(jnp.bfloat16)
        mixed = mul(deep_ref[step], weight_ref[cell])
        acts_ref[step + 1] = (acts_ref[step].astype(jnp.float32) + mixed).astype(jnp.bfloat16)
        return 0

    lax.fori_loop(0, count, forward, 0)

    means = [
        jnp.sum(acts_ref[count, rows_of(image)].astype(jnp.float32), axis=0, keepdims=True)
        for image in range(IMAGES)
    ]
    spare = jnp.zeros((8 - IMAGES, features_ref.shape[1]), jnp.float32)
    pooled = jnp.concatenate(means + [spare], axis=0) / AREA
    head = head_ref[...]
    scores = jnp.dot(
        pooled, head, precision=lax.Precision.HIGHEST, preferred_element_type=jnp.float32
    )
    capped = jnp.tanh(scores / LOGIT_CAP)
    logits = LOGIT_CAP * capped
    exponent = jnp.exp(logits)
    total = jnp.sum(exponent, axis=1, keepdims=True)
    classes = lax.broadcasted_iota(jnp.int32, logits.shape, 1)
    onehot = (classes == targets_ref[...]).astype(jnp.float32)
    live = live_ref[...]
    row_loss = (jnp.log(total) - jnp.sum(logits * onehot, axis=1, keepdims=True)) * live
    loss_ref[...] = jnp.broadcast_to(
        jnp.sum(row_loss, axis=0, keepdims=True), loss_ref.shape
    )
    score_cot = (exponent / total - onehot) * live * (1.0 - capped * capped)
    pooled_cot = lax.dot_general(
        score_cot,
        head,
        (((1,), (1,)), ((), ())),
        precision=lax.Precision.HIGHEST,
        preferred_element_type=jnp.float32,
    )
    spread = pooled_cot / AREA
    for image in range(IMAGES):
        cot_ref[rows_of(image)] = jnp.broadcast_to(
            spread[image : image + 1], (AREA, spread.shape[1])
        ).astype(jnp.bfloat16)

    def backward(turn, _):
        step = count - 1 - turn
        cell = order_ref[step]
        cot = cot_ref[...]
        point_ref[cell] = lax.dot_general(
            deep_ref[step], cot, (((0,), (0,)), ((), ())), preferred_element_type=jnp.float32
        )
        deep_cot_ref[...] = lax.dot_general(
            cot, weight_ref[cell], (((1,), (1,)), ((), ())), preferred_element_type=jnp.float32
        ).astype(jnp.bfloat16)
        wave_re, wave_im = wave_ref[step, :HALF], wave_ref[step, HALF:]
        for image in range(IMAGES):
            acts = acts_ref[step, rows_of(image)]
            seen = mul(into_ref[0], jnp.maximum(acts, 0))
            seen_re, seen_im = seen[:HALF], seen[HALF:]
            sent = mul(into_ref[0], deep_cot_ref[rows_of(image)])
            sent_re, sent_im = sent[:HALF], sent[HALF:]
            part_re = seen_re * sent_re + seen_im * sent_im
            part_im = seen_im * sent_re - seen_re * sent_im
            if image == 0:
                total_ref[:HALF] = part_re
                total_ref[HALF:] = part_im
            else:
                total_ref[:HALF] += part_re
                total_ref[HALF:] += part_im
            mixed = jnp.concatenate(
                [
                    sent_re * wave_re + sent_im * wave_im,
                    sent_im * wave_re - sent_re * wave_im,
                ],
                axis=0,
            ).astype(jnp.bfloat16)
            rect_cot = mul(back_ref[0], mixed)
            cot_ref[rows_of(image)] = (
                cot_ref[rows_of(image)].astype(jnp.float32)
                + jnp.where(acts.astype(jnp.float32) > 0, rect_cot, 0.0)
            ).astype(jnp.bfloat16)
        high, low = halves(total_ref[...])
        kernel_ref[cell] = (
            mul(tap_back_ref[0], high) + mul(tap_back_ref[0], low) + mul(tap_back_ref[1], high)
        )
        return 0

    lax.fori_loop(0, count, backward, 0)


def run_cells(cells, features, targets, live, weights, taps, head):
    slots, channels = weights.shape[0], weights.shape[-1]
    tables = [jnp.asarray(table) for table in transform_tables()]
    vmem = pl.BlockSpec(memory_space=pltpu.VMEM)
    rows = IMAGES * AREA
    return pl.pallas_call(
        cells_kernel,
        out_shape=(
            jax.ShapeDtypeStruct((slots, channels, channels), jnp.float32),
            jax.ShapeDtypeStruct((slots, TAP_ROWS, channels), jnp.float32),
            jax.ShapeDtypeStruct((8, 128), jnp.float32),
        ),
        in_specs=[pl.BlockSpec(memory_space=pltpu.SMEM)] + [vmem] * 10,
        out_specs=(vmem, vmem, vmem),
        scratch_shapes=[
            pltpu.SMEM((slots + CELLS_MAX,), jnp.int32),
            pltpu.VMEM((slots + 1, rows, channels), jnp.bfloat16),
            pltpu.VMEM((slots, rows, channels), jnp.bfloat16),
            pltpu.VMEM((slots, 2 * HALF, channels), jnp.float32),
            pltpu.VMEM((rows, channels), jnp.bfloat16),
            pltpu.VMEM((rows, channels), jnp.bfloat16),
            pltpu.VMEM((2 * HALF, channels), jnp.float32),
        ],
        compiler_params=pltpu.CompilerParams(vmem_limit_bytes=60 * 1024 * 1024),
        name="cells",
    )(cells, features, targets, live, weights, taps, head, *tables)


def padded_taps(kernel):
    edge = (TAPS - kernel.shape[1]) // 2
    wide = jnp.pad(kernel, ((0, 0), (edge, edge), (edge, edge), (0, 0)))
    flat = wide.reshape(kernel.shape[0], TAPS * TAPS, kernel.shape[-1])
    return jnp.pad(flat, ((0, 0), (0, TAP_ROWS - TAPS * TAPS), (0, 0)))


def own_taps(rows, size):
    edge = (TAPS - size) // 2
    window = rows[: TAPS * TAPS].reshape(TAPS, TAPS, rows.shape[-1])
    return window[edge : edge + size, edge : edge + size]


def shards(
    features,
    labels,
    micro_count,
    cells_per_section,
    point_weight,
    depth_three,
    depth_five,
    depth_seven,
    head_weight,
):
    sections = lax.axis_size("pipe")
    section_index = lax.axis_index("pipe")
    channels = point_weight.shape[-1]
    weights = lax.all_gather(point_weight[0], "pipe")
    taps = jnp.concatenate(
        [padded_taps(kernel) for kernel in (depth_three, depth_five, depth_seven)], axis=0
    )
    taps = lax.all_gather(taps, "pipe")
    slots = sections * CELLS_MAX

    per_replica = features.shape[0]
    share = per_replica // sections
    grouped = features.reshape(share, sections, AREA, channels)
    own = lax.dynamic_index_in_dim(grouped, section_index, 1, keepdims=False)
    own = own.reshape(share * AREA, channels)
    image = section_index + sections * lax.iota(jnp.int32, share)
    own_live = (image // MB_IMG < micro_count[0]).astype(jnp.float32)
    own_labels = labels[image]
    live = jnp.pad(own_live, (0, 8 - share))[:, None]
    targets = jnp.pad(own_labels, (0, 8 - share))[:, None]

    point_part, kernel_part, loss_part = run_cells(
        cells_per_section,
        own,
        targets,
        live,
        weights.reshape(slots, channels, channels),
        taps.reshape(slots, TAP_ROWS, channels),
        head_weight,
    )
    point_part = point_part.reshape(sections, CELLS_MAX, channels, channels)
    kernel_part = kernel_part.reshape(sections, CELLS_MAX, TAP_ROWS, channels)
    point_sum = lax.psum_scatter(point_part, "pipe")
    kernel_sum = lax.psum_scatter(kernel_part, "pipe")
    point_sum, kernel_sum = lax.psum((point_sum, kernel_sum), "dp")
    total_loss = lax.psum(loss_part[0, 0], ("pipe", "dp"))
    return (
        total_loss,
        point_sum[None],
        own_taps(kernel_sum[0], 3)[None],
        own_taps(kernel_sum[1], 5)[None],
        own_taps(kernel_sum[2], 7)[None],
    )


def solution(mesh):
    return jax.shard_map(
        shards,
        mesh=mesh,
        in_specs=(
            P("dp", None, None, None),
            P("dp"),
            P("dp"),
            P(),
            P("pipe", None, None, None),
            P("pipe", None, None, None),
            P("pipe", None, None, None),
            P("pipe", None, None, None),
            P(),
        ),
        out_specs=(
            P(),
            P("pipe", None, None, None),
            P("pipe", None, None, None),
            P("pipe", None, None, None),
            P("pipe", None, None, None),
        ),
        check_vma=False,
    )
```

```python
import functools

import jax
import jax.numpy as jnp
import ml_dtypes
import numpy as np
from jax import lax
from jax.experimental import pallas as pl
from jax.experimental.pallas import tpu as pltpu
from jax.sharding import PartitionSpec as P

SIDE = 12
AREA = SIDE * SIDE
MB_IMG = 2
CELLS_MAX = 3
TAPS = 7
TAP_ROWS = 64
LOGIT_CAP = 30.0
CYCLE = SIDE + TAPS // 2
HALF = 128
IMAGES = 4
CHIPS_X = 4
CHIPS_Z = 8
CORES = 2
LANES = 128
MESH = pl.DeviceIdType.MESH
TAP_SPANS = (16, 32, 64)
TAP_STARTS = (0, 16, 48)
TAP_BLOCK = 112
CHUNK = 112
CHUNK_A = 64
CHUNK_B = CHUNK - CHUNK_A
BLOCK = CORES * CHIPS_Z * CHUNK
WEIGHT_A = 96


def transform_tables():
    slots = [(0, 0)]
    seen = {(0, 0)}
    for u in range(CYCLE):
        for v in range(CYCLE):
            if (u, v) in seen:
                continue
            seen.add((u, v))
            seen.add(((-u) % CYCLE, (-v) % CYCLE))
            slots.append((u, v))
    count = len(slots)
    waves = np.array(slots, np.float64)
    sites = np.array([(i, j) for i in range(SIDE) for j in range(SIDE)], np.float64)
    weight = np.where((waves == 0).all(1), 1.0, 2.0)[:, None] / CYCLE**2
    site_angle = 2 * np.pi * ((waves @ sites.T) % CYCLE) / CYCLE
    into = np.zeros((2 * HALF, AREA))
    into[:count] = np.cos(site_angle)
    into[HALF : HALF + count] = -np.sin(site_angle)
    back = np.zeros((AREA, 2 * HALF))
    back[:, :count] = (np.cos(site_angle) * weight).T
    back[:, HALF : HALF + count] = -(np.sin(site_angle) * weight).T
    tap_into = np.zeros((CELLS_MAX, 2 * HALF, TAP_ROWS))
    tap_back = np.zeros((CELLS_MAX, TAP_ROWS, 2 * HALF))
    for slot in range(CELLS_MAX):
        size = 2 * slot + 3
        reach = size // 2
        shifts = np.array(
            [(u - reach, v - reach) for u in range(size) for v in range(size)], np.float64
        )
        taps = size * size
        tap_angle = 2 * np.pi * ((waves @ shifts.T) % CYCLE) / CYCLE
        tap_into[slot, :count, :taps] = np.cos(tap_angle)
        tap_into[slot, HALF : HALF + count, :taps] = np.sin(tap_angle)
        tap_back[slot, :taps, :count] = (np.cos(tap_angle) * weight).T
        tap_back[slot, :taps, HALF : HALF + count] = -(np.sin(tap_angle) * weight).T
    return [pair_of(table) for table in (into, back, tap_into, tap_back)]


def pair_of(table):
    high = table.astype(ml_dtypes.bfloat16)
    low = (table - high.astype(np.float64)).astype(ml_dtypes.bfloat16)
    return np.stack([high, low])


def mul(a, b):
    return jnp.dot(a, b, preferred_element_type=jnp.float32)


def halves(values):
    high = values.astype(jnp.bfloat16)
    low = (values - high.astype(jnp.float32)).astype(jnp.bfloat16)
    return high, low


def cells_kernel(
    cells_ref,
    device_ref,
    features_ref,
    targets_ref,
    live_ref,
    weight_ref,
    taps_ref,
    head_ref,
    into_ref,
    back_ref,
    tap_into_ref,
    tap_back_ref,
    grad_ref,
    order_ref,
    acts_ref,
    deep_ref,
    wave_ref,
    cot_ref,
    deep_cot_ref,
    total_ref,
):
    slots, channels = weight_ref.shape[0], weight_ref.shape[-1]
    sections = slots // CELLS_MAX
    point_rows = CELLS_MAX * channels
    loss_start = point_rows + TAP_BLOCK
    count = jnp.int32(0)
    for section in range(sections):
        held = cells_ref[section]
        for slot in range(CELLS_MAX):
            order_ref[count + slot] = section * CELLS_MAX + slot
        for slot in range(1, CELLS_MAX):

            @pl.when(slot >= held)
            def _(start=section * BLOCK, slot=slot):
                grad_ref[start + slot * channels : start + (slot + 1) * channels] = jnp.zeros(
                    (channels, channels), jnp.bfloat16
                )
                taps = start + point_rows + TAP_STARTS[slot]
                grad_ref[taps : taps + TAP_SPANS[slot]] = jnp.zeros(
                    (TAP_SPANS[slot], channels), jnp.bfloat16
                )

        count = count + held

    acts_ref[0] = features_ref[...]

    def rows_of(image):
        return pl.ds(image * AREA, AREA)

    def forward(step, _):
        cell = order_ref[step]
        slot = lax.rem(cell, CELLS_MAX)
        taps = taps_ref[cell]
        wave = mul(tap_into_ref[0, slot], taps) + mul(tap_into_ref[1, slot], taps)
        wave_ref[step] = wave
        wave_re, wave_im = wave[:HALF], wave[HALF:]
        for image in range(IMAGES):
            site = jnp.maximum(acts_ref[step, rows_of(image)], 0)
            seen = mul(into_ref[0], site) + mul(into_ref[1], site)
            seen_re, seen_im = seen[:HALF], seen[HALF:]
            mixed = jnp.concatenate(
                [
                    seen_re * wave_re - seen_im * wave_im,
                    seen_re * wave_im + seen_im * wave_re,
                ],
                axis=0,
            )
            high, low = halves(mixed)
            deep = mul(back_ref[0], high) + mul(back_ref[0], low) + mul(back_ref[1], high)
            deep_ref[step, rows_of(image)] = deep.astype(jnp.bfloat16)
        mixed = mul(deep_ref[step], weight_ref[cell])
        acts_ref[step + 1] = (acts_ref[step].astype(jnp.float32) + mixed).astype(jnp.bfloat16)
        return 0

    lax.fori_loop(0, count, forward, 0)

    means = [
        jnp.sum(acts_ref[count, rows_of(image)].astype(jnp.float32), axis=0, keepdims=True)
        for image in range(IMAGES)
    ]
    spare = jnp.zeros((8 - IMAGES, channels), jnp.float32)
    pooled = jnp.concatenate(means + [spare], axis=0) / AREA
    head = head_ref[...]
    scores = jnp.dot(
        pooled, head, precision=lax.Precision.HIGHEST, preferred_element_type=jnp.float32
    )
    capped = jnp.tanh(scores / LOGIT_CAP)
    logits = LOGIT_CAP * capped
    exponent = jnp.exp(logits)
    total = jnp.sum(exponent, axis=1, keepdims=True)
    classes = lax.broadcasted_iota(jnp.int32, logits.shape, 1)
    onehot = (classes == targets_ref[...]).astype(jnp.float32)
    live = live_ref[...]
    row_loss = (jnp.log(total) - jnp.sum(logits * onehot, axis=1, keepdims=True)) * live
    score_cot = (exponent / total - onehot) * live * (1.0 - capped * capped)
    pooled_cot = lax.dot_general(
        score_cot,
        head,
        (((1,), (1,)), ((), ())),
        precision=lax.Precision.HIGHEST,
        preferred_element_type=jnp.float32,
    )
    spread = pooled_cot / AREA
    for image in range(IMAGES):
        cot_ref[rows_of(image)] = jnp.broadcast_to(
            spread[image : image + 1], (AREA, channels)
        ).astype(jnp.bfloat16)

    loss = jnp.broadcast_to(jnp.sum(row_loss, axis=0, keepdims=True), (16, channels))
    high = loss.astype(jnp.bfloat16).astype(jnp.float32)
    middle = (loss - high).astype(jnp.bfloat16).astype(jnp.float32)
    low = loss - high - middle
    part = lax.broadcasted_iota(jnp.int32, loss.shape, 0)
    own = lax.broadcasted_iota(jnp.int32, loss.shape, 1) == device_ref[0]
    parts = jnp.where(part == 0, high, jnp.where(part == 1, middle, low))
    parts = jnp.where(own & (part < 3), parts, 0.0).astype(jnp.bfloat16)
    for section in range(sections):
        start = section * BLOCK + loss_start
        grad_ref[start : start + 16] = parts
        grad_ref[start + 16 : (section + 1) * BLOCK] = jnp.zeros(
            (BLOCK - loss_start - 16, channels), jnp.bfloat16
        )

    def backward(turn, _):
        step = count - 1 - turn
        cell = order_ref[step]
        section = lax.div(cell, CELLS_MAX)
        slot = lax.rem(cell, CELLS_MAX)
        start = pl.multiple_of(section * BLOCK, 16)
        cot = cot_ref[...]
        point = pl.multiple_of(start + slot * channels, 16)
        grad_ref[pl.ds(point, channels)] = lax.dot_general(
            deep_ref[step], cot, (((0,), (0,)), ((), ())), preferred_element_type=jnp.float32
        ).astype(jnp.bfloat16)
        deep_cot_ref[...] = lax.dot_general(
            cot, weight_ref[cell], (((1,), (1,)), ((), ())), preferred_element_type=jnp.float32
        ).astype(jnp.bfloat16)
        wave_re, wave_im = wave_ref[step, :HALF], wave_ref[step, HALF:]
        for image in range(IMAGES):
            acts = acts_ref[step, rows_of(image)]
            seen = mul(into_ref[0], jnp.maximum(acts, 0))
            seen_re, seen_im = seen[:HALF], seen[HALF:]
            sent = mul(into_ref[0], deep_cot_ref[rows_of(image)])
            sent_re, sent_im = sent[:HALF], sent[HALF:]
            part_re = seen_re * sent_re + seen_im * sent_im
            part_im = seen_im * sent_re - seen_re * sent_im
            if image == 0:
                total_ref[:HALF] = part_re
                total_ref[HALF:] = part_im
            else:
                total_ref[:HALF] += part_re
                total_ref[HALF:] += part_im
            mixed = jnp.concatenate(
                [
                    sent_re * wave_re + sent_im * wave_im,
                    sent_im * wave_re - sent_re * wave_im,
                ],
                axis=0,
            ).astype(jnp.bfloat16)
            rect_cot = mul(back_ref[0], mixed)
            cot_ref[rows_of(image)] = (
                cot_ref[rows_of(image)].astype(jnp.float32)
                + jnp.where(acts.astype(jnp.float32) > 0, rect_cot, 0.0)
            ).astype(jnp.bfloat16)
        high, low = halves(total_ref[...])
        taps = (
            mul(tap_back_ref[0, slot], high)
            + mul(tap_back_ref[0, slot], low)
            + mul(tap_back_ref[1, slot], high)
        ).astype(jnp.bfloat16)
        for kind in range(CELLS_MAX):

            @pl.when(slot == kind)
            def _(kind=kind):
                row = pl.multiple_of(start + point_rows + TAP_STARTS[kind], 16)
                grad_ref[pl.ds(row, TAP_SPANS[kind])] = taps[: TAP_SPANS[kind]]

        return 0

    lax.fori_loop(0, count, backward, 0)


def run_cells(cells, device, features, targets, live, weights, taps, head):
    slots, channels = weights.shape[0], weights.shape[-1]
    tables = [jnp.asarray(table) for table in transform_tables()]
    vmem = pl.BlockSpec(memory_space=pltpu.VMEM)
    smem = pl.BlockSpec(memory_space=pltpu.SMEM)
    rows = IMAGES * AREA
    return pl.pallas_call(
        cells_kernel,
        out_shape=jax.ShapeDtypeStruct((slots // CELLS_MAX * BLOCK, channels), jnp.bfloat16),
        in_specs=[smem, smem] + [vmem] * 10,
        out_specs=vmem,
        scratch_shapes=[
            pltpu.SMEM((slots + CELLS_MAX,), jnp.int32),
            pltpu.VMEM((slots + 1, rows, channels), jnp.bfloat16),
            pltpu.VMEM((slots, rows, channels), jnp.bfloat16),
            pltpu.VMEM((slots, 2 * HALF, channels), jnp.float32),
            pltpu.VMEM((rows, channels), jnp.bfloat16),
            pltpu.VMEM((rows, channels), jnp.bfloat16),
            pltpu.VMEM((2 * HALF, channels), jnp.float32),
        ],
        compiler_params=pltpu.CompilerParams(vmem_limit_bytes=60 * 1024 * 1024),
        name="cells",
    )(cells, device, features, targets, live, weights, taps, head, *tables)


class Place:
    def __init__(self, sections):
        self.sections = sections
        self.pipe = lax.axis_index("pipe")
        place = lax.axis_index("dp")
        self.core = lax.rem(place, CORES)
        self.z = lax.rem(lax.div(place, CORES), CHIPS_Z)
        self.x = lax.div(place, CORES * CHIPS_Z)

    def device(self, pipe=0, x=0, z=0, core=0):
        pipe = lax.rem(self.pipe + pipe, self.sections)
        x = lax.rem(self.x + x, CHIPS_X)
        z = lax.rem(self.z + z, CHIPS_Z)
        core = lax.rem(self.core + core, CORES)
        return (pipe, (x * CHIPS_Z + z) * CORES + core)

    def greet(self, partners):
        barrier = pltpu.get_barrier_semaphore()
        for partner in partners:
            pl.semaphore_signal(barrier, inc=1, device_id=partner, device_id_type=MESH)
        pl.semaphore_wait(barrier, len(partners))


def start_remote(source, target, send_sems, recv_sems, index, device):
    copy = pltpu.make_async_remote_copy(
        src_ref=source,
        dst_ref=target,
        send_sem=send_sems.at[index],
        recv_sem=recv_sems.at[index],
        device_id=device,
        device_id_type=MESH,
    )
    copy.start()
    return copy


def start_local(source, target, sems, index):
    copy = pltpu.make_async_copy(source, target, sems.at[index])
    copy.start()
    return copy


def gather_kernel(
    sections,
    weight_ref,
    taps_ref,
    weights_ref,
    all_taps_ref,
    direct_send,
    direct_recv,
    split_send,
    split_recv,
    spread_send,
    spread_recv,
    taps_send,
    taps_recv,
    core_send,
    core_recv,
    local_sem,
):
    at = Place(sections)
    others_y = range(1, sections)
    others_x = range(1, CHIPS_X)
    at.greet(
        [at.device(pipe=d) for d in others_y]
        + [at.device(x=d) for d in others_x]
        + [at.device(core=1)]
    )
    core = at.core
    lanes = pl.ds(pl.multiple_of(at.x * LANES, LANES), LANES)
    cells = pl.ds(0, CELLS_MAX)
    near = pl.ds(0, WEIGHT_A)
    far = pl.ds(WEIGHT_A, weight_ref.shape[2] - WEIGHT_A)
    split = [
        start_remote(
            weight_ref.at[cells, core, far, lanes],
            weights_ref.at[at.pipe, cells, core, far, lanes],
            split_send,
            split_recv,
            d - 1,
            at.device(pipe=d),
        )
        for d in others_y
    ]
    direct = [
        start_remote(
            weight_ref.at[cells, core, near],
            weights_ref.at[at.pipe, cells, core, near],
            direct_send,
            direct_recv,
            d - 1,
            at.device(pipe=d),
        )
        for d in others_y
    ]
    tap_copies = [
        start_remote(
            taps_ref, all_taps_ref.at[at.pipe], taps_send, taps_recv, d - 1, at.device(pipe=d)
        )
        for d in others_y
    ]
    local = [
        start_local(weight_ref, weights_ref.at[at.pipe], local_sem, 0),
        start_local(taps_ref, all_taps_ref.at[at.pipe], local_sem, 1),
    ]
    spread = []
    for d in others_y:
        split[d - 1].wait_recv()
        source = lax.rem(at.pipe + sections - d, sections)
        piece = weights_ref.at[source, cells, core, far, lanes]
        spread.append(
            [
                start_remote(
                    piece,
                    piece,
                    spread_send,
                    spread_recv,
                    (d - 1) * (CHIPS_X - 1) + e - 1,
                    at.device(x=e),
                )
                for e in others_x
            ]
        )
    shared = []
    for d in others_y:
        direct[d - 1].wait_recv()
        for copy in spread[d - 1]:
            copy.wait_recv()
        source = lax.rem(at.pipe + sections - d, sections)
        piece = weights_ref.at[source, cells, core]
        shared.append(start_remote(piece, piece, core_send, core_recv, d - 1, at.device(core=1)))
    for copy in local:
        copy.wait()
    for copy in tap_copies + shared:
        copy.wait()
    for copy in split + direct + [copy for copies in spread for copy in copies]:
        copy.wait_send()


def gather_weights(weight, taps, sections):
    cells, channels = weight.shape[0], weight.shape[-1]
    weight = weight.reshape(cells, CORES, channels // CORES, channels)
    anywhere = pl.BlockSpec(memory_space=pl.ANY)
    dma = pltpu.SemaphoreType.DMA
    ys, xs = sections - 1, CHIPS_X - 1
    weights, all_taps = pl.pallas_call(
        functools.partial(gather_kernel, sections),
        out_shape=(
            jax.ShapeDtypeStruct((sections,) + weight.shape, weight.dtype),
            jax.ShapeDtypeStruct((sections,) + taps.shape, taps.dtype),
        ),
        in_specs=[anywhere, anywhere],
        out_specs=(anywhere, anywhere),
        scratch_shapes=[
            dma((ys,)),
            dma((ys,)),
            dma((ys,)),
            dma((ys,)),
            dma((ys * xs,)),
            dma((ys * xs,)),
            dma((ys,)),
            dma((ys,)),
            dma((ys,)),
            dma((ys,)),
            dma((2,)),
        ],
        compiler_params=pltpu.CompilerParams(collective_id=0, has_side_effects=True),
        name="gather",
    )(weight, taps)
    return weights.reshape(sections * cells, channels, channels), all_taps


def reduce_kernel(
    sections,
    grad_ref,
    out_ref,
    own_ref,
    pair_ref,
    part_a_ref,
    part_b_ref,
    in_a1_ref,
    in_b1_ref,
    mid_a_ref,
    mid_b_ref,
    in_a2_ref,
    in_b2_ref,
    small_ref,
    in_z_ref,
    line_ref,
    plane_ref,
    pair_send,
    pair_recv,
    a1_send,
    a1_recv,
    b1_send,
    b1_recv,
    a2_send,
    a2_recv,
    b2_send,
    b2_recv,
    z_send,
    z_recv,
    line_send,
    line_recv,
    plane_send,
    plane_recv,
    core_send,
    core_recv,
    local_sem,
):
    at = Place(sections)
    others_y = range(1, sections)
    others_x = range(1, CHIPS_X)
    others_z = range(1, CHIPS_Z)
    partner = at.device(core=1)
    at.greet(
        [partner]
        + [at.device(pipe=d) for d in others_y]
        + [at.device(x=d) for d in others_x]
        + [at.device(z=d) for d in others_z]
    )
    f32 = jnp.float32
    bf16 = jnp.bfloat16

    def lanes(x):
        return pl.ds(pl.multiple_of(x * LANES, LANES), LANES)

    order = [lax.rem(at.pipe + d, sections) for d in (2, 1, 3, 0)]
    paired, local = [], []
    for k, section in enumerate(order):
        paired.append(
            start_remote(
                grad_ref.at[section, lax.rem(at.core + 1, CORES)],
                pair_ref.at[section],
                pair_send,
                pair_recv,
                k,
                partner,
            )
        )
        local.append(start_local(grad_ref.at[section, at.core], own_ref.at[section], local_sem, k))
    a1, b1 = {}, []
    for k, section in enumerate(order):
        local[k].wait()
        paired[k].wait_recv()

        def add_pair(z, _, section=section):
            total = own_ref[section, z].astype(f32) + pair_ref[section, z].astype(f32)
            part_a_ref[section, z] = total[:CHUNK_A].astype(bf16)
            part_b_ref[section, z] = total[CHUNK_A:].astype(bf16)
            return 0

        lax.fori_loop(0, CHIPS_Z, add_pair, 0)
        d = (2, 1, 3, 0)[k]
        if d:
            a1[d] = start_remote(
                part_a_ref.at[section],
                in_a1_ref.at[d - 1],
                a1_send,
                a1_recv,
                d - 1,
                at.device(pipe=d),
            )
        for e in others_x:
            b1.append(
                start_remote(
                    part_b_ref.at[
                        section,
                        pl.ds(0, CHIPS_Z),
                        pl.ds(0, CHUNK_B),
                        lanes(lax.rem(at.x + e, CHIPS_X)),
                    ],
                    in_b1_ref.at[e - 1, section],
                    b1_send,
                    b1_recv,
                    k * (CHIPS_X - 1) + e - 1,
                    at.device(x=e),
                )
            )
    b2 = {}
    for k, section in enumerate(order):
        for e in others_x:
            b1[k * (CHIPS_X - 1) + e - 1].wait_recv()

        def add_b1(z, _, section=section):
            total = part_b_ref[section, z, :, lanes(at.x)].astype(f32)
            for e in others_x:
                total = total + in_b1_ref[e - 1, section, z].astype(f32)
            mid_b_ref[section, z] = total.astype(bf16)
            return 0

        lax.fori_loop(0, CHIPS_Z, add_b1, 0)
        d = (2, 1, 3, 0)[k]
        if d:
            b2[d] = start_remote(
                mid_b_ref.at[section],
                in_b2_ref.at[d - 1],
                b2_send,
                b2_recv,
                d - 1,
                at.device(pipe=d),
            )
    for d in others_y:
        a1[d].wait_recv()

    def add_a1(z, _):
        total = part_a_ref[at.pipe, z].astype(f32)
        for d in others_y:
            total = total + in_a1_ref[d - 1, z].astype(f32)
        mid_a_ref[z] = total.astype(bf16)
        return 0

    lax.fori_loop(0, CHIPS_Z, add_a1, 0)
    a2 = [
        start_remote(
            mid_a_ref.at[
                pl.ds(0, CHIPS_Z), pl.ds(0, CHUNK_A), lanes(lax.rem(at.x + e, CHIPS_X))
            ],
            in_a2_ref.at[e - 1],
            a2_send,
            a2_recv,
            e - 1,
            at.device(x=e),
        )
        for e in others_x
    ]
    for d in others_y:
        b2[d].wait_recv()
    for copy in a2:
        copy.wait_recv()

    def add_second(z, _):
        total_a = mid_a_ref[z, :, lanes(at.x)].astype(f32)
        total_b = mid_b_ref[at.pipe, z].astype(f32)
        for e in others_x:
            total_a = total_a + in_a2_ref[e - 1, z].astype(f32)
        for d in others_y:
            total_b = total_b + in_b2_ref[d - 1, z].astype(f32)
        small_ref[z, :CHUNK_A] = total_a.astype(bf16)
        small_ref[z, CHUNK_A:] = total_b.astype(bf16)
        return 0

    lax.fori_loop(0, CHIPS_Z, add_second, 0)
    to_z = [
        start_remote(
            small_ref.at[lax.rem(at.z + d, CHIPS_Z)],
            in_z_ref.at[d - 1],
            z_send,
            z_recv,
            d - 1,
            at.device(z=d),
        )
        for d in others_z
    ]
    for copy in to_z:
        copy.wait_recv()
    total = small_ref[at.z].astype(f32)
    for d in others_z:
        total = total + in_z_ref[d - 1].astype(f32)
    line_ref[at.z] = total.astype(bf16)
    piece = line_ref.at[at.z]
    line = [
        start_remote(piece, piece, line_send, line_recv, d - 1, at.device(z=d)) for d in others_z
    ]
    for copy in line:
        copy.wait_recv()
    column = plane_ref.at[pl.ds(0, CHIPS_Z), pl.ds(0, CHUNK), lanes(at.x)]
    plane = [
        start_remote(line_ref, column, plane_send, plane_recv, e - 1, at.device(x=e))
        for e in others_x
    ]
    own_column = start_local(line_ref, column, local_sem, 0)
    own_column.wait()
    for copy in plane:
        copy.wait_recv()
    half = out_ref.at[at.core]
    last = start_remote(plane_ref, half, core_send, core_recv, 0, partner)
    own_half = start_local(plane_ref, half, local_sem, 1)
    own_half.wait()
    last.wait()
    for copy in paired + b1 + list(a1.values()) + list(b2.values()) + a2 + to_z + line + plane:
        copy.wait_send()


def reduce_grads(grads, sections):
    channels = grads.shape[-1]
    grads = grads.reshape(sections, CORES, CHIPS_Z, CHUNK, channels)
    anywhere = pl.BlockSpec(memory_space=pl.ANY)
    dma = pltpu.SemaphoreType.DMA
    ys, xs, zs = sections - 1, CHIPS_X - 1, CHIPS_Z - 1

    def vmem(*shape):
        return pltpu.VMEM(shape, jnp.bfloat16)

    out = pl.pallas_call(
        functools.partial(reduce_kernel, sections),
        out_shape=jax.ShapeDtypeStruct((CORES, CHIPS_Z, CHUNK, channels), jnp.bfloat16),
        in_specs=[anywhere],
        out_specs=anywhere,
        scratch_shapes=[
            vmem(sections, CHIPS_Z, CHUNK, channels),
            vmem(sections, CHIPS_Z, CHUNK, channels),
            vmem(sections, CHIPS_Z, CHUNK_A, channels),
            vmem(sections, CHIPS_Z, CHUNK_B, channels),
            vmem(ys, CHIPS_Z, CHUNK_A, channels),
            vmem(xs, sections, CHIPS_Z, CHUNK_B, LANES),
            vmem(CHIPS_Z, CHUNK_A, channels),
            vmem(sections, CHIPS_Z, CHUNK_B, LANES),
            vmem(xs, CHIPS_Z, CHUNK_A, LANES),
            vmem(ys, CHIPS_Z, CHUNK_B, LANES),
            vmem(CHIPS_Z, CHUNK, LANES),
            vmem(zs, CHUNK, LANES),
            vmem(CHIPS_Z, CHUNK, LANES),
            vmem(CHIPS_Z, CHUNK, channels),
            dma((sections,)),
            dma((sections,)),
            dma((ys,)),
            dma((ys,)),
            dma((sections * xs,)),
            dma((sections * xs,)),
            dma((xs,)),
            dma((xs,)),
            dma((ys,)),
            dma((ys,)),
            dma((zs,)),
            dma((zs,)),
            dma((zs,)),
            dma((zs,)),
            dma((xs,)),
            dma((xs,)),
            dma((1,)),
            dma((1,)),
            dma((sections,)),
        ],
        compiler_params=pltpu.CompilerParams(
            collective_id=1, has_side_effects=True, vmem_limit_bytes=40 * 1024 * 1024
        ),
        name="reduce",
    )(grads)
    return out.reshape(BLOCK, channels)


def padded_taps(kernel):
    flat = kernel[0].reshape(-1, kernel.shape[-1])
    return jnp.pad(flat, ((0, TAP_ROWS - flat.shape[0]), (0, 0)))


def own_taps(block, slot, start):
    size = 2 * slot + 3
    rows = block[start + TAP_STARTS[slot] :][: size * size].astype(jnp.float32)
    return rows.reshape(1, size, size, block.shape[-1])


def shards(
    features,
    labels,
    micro_count,
    cells_per_section,
    point_weight,
    depth_three,
    depth_five,
    depth_seven,
    head_weight,
):
    sections = lax.axis_size("pipe")
    section_index = lax.axis_index("pipe")
    channels = point_weight.shape[-1]
    taps = jnp.stack([padded_taps(kernel) for kernel in (depth_three, depth_five, depth_seven)])
    weights, taps = gather_weights(point_weight[0], taps, sections)

    per_replica = features.shape[0]
    share = per_replica // sections
    grouped = features.reshape(share, sections, AREA, channels)
    own = lax.dynamic_index_in_dim(grouped, section_index, 1, keepdims=False)
    own = own.reshape(share * AREA, channels)
    image = section_index + sections * lax.iota(jnp.int32, share)
    own_live = (image // MB_IMG < micro_count[0]).astype(jnp.float32)
    own_labels = labels[image]
    live = jnp.pad(own_live, (0, 8 - share))[:, None]
    targets = jnp.pad(own_labels, (0, 8 - share))[:, None]
    device = (lax.axis_index("dp") * sections + section_index)[None]

    grads = run_cells(
        cells_per_section,
        device,
        own,
        targets,
        live,
        weights,
        taps.reshape(sections * CELLS_MAX, TAP_ROWS, channels),
        head_weight,
    )
    block = reduce_grads(grads, sections)
    taps_start = CELLS_MAX * channels
    loss_start = taps_start + TAP_BLOCK
    total_loss = jnp.sum(block[loss_start : loss_start + 3].astype(jnp.float32))
    point_sum = block[:taps_start].astype(jnp.float32)
    return (
        total_loss,
        point_sum.reshape(1, CELLS_MAX, channels, channels),
        own_taps(block, 0, taps_start),
        own_taps(block, 1, taps_start),
        own_taps(block, 2, taps_start),
    )


def solution(mesh):
    return jax.shard_map(
        shards,
        mesh=mesh,
        in_specs=(
            P("dp", None, None, None),
            P("dp"),
            P("dp"),
            P(),
            P("pipe", None, None, None),
            P("pipe", None, None, None),
            P("pipe", None, None, None),
            P("pipe", None, None, None),
            P(),
        ),
        out_specs=(
            P(),
            P("pipe", None, None, None),
            P("pipe", None, None, None),
            P("pipe", None, None, None),
            P("pipe", None, None, None),
        ),
        check_vma=False,
    )
```

```python
import functools

import jax
import jax.numpy as jnp
import ml_dtypes
import numpy as np
from jax import lax
from jax.experimental import pallas as pl
from jax.experimental.pallas import tpu as pltpu
from jax.sharding import PartitionSpec as P

SIDE = 12
AREA = SIDE * SIDE
MB_IMG = 2
CELLS_MAX = 3
TAPS = 7
TAP_ROWS = 64
LOGIT_CAP = 30.0
CYCLE = SIDE + TAPS // 2
HALF = 128
IMAGES = 4
GROUP = 16
CHIPS_X = 4
CHIPS_Z = 8
CORES = 2
LANES = 128
MESH = pl.DeviceIdType.MESH
TAP_HALVES = (0, 0, 1)
TAP_STARTS = (0, 16, 0)
TAP_SPANS = (16, 32, 64)
CHUNK = 112
CHUNK_A = 64
CHUNK_B = CHUNK - CHUNK_A
HALF_ROWS = CHIPS_Z * CHUNK
LOSS_ROWS = 16
WEIGHT_A = 272
CELLS_MB = 32


def transform_tables():
    slots = [(0, 0)]
    seen = {(0, 0)}
    for u in range(CYCLE):
        for v in range(CYCLE):
            if (u, v) in seen:
                continue
            seen.add((u, v))
            seen.add(((-u) % CYCLE, (-v) % CYCLE))
            slots.append((u, v))
    count = len(slots)
    waves = np.array(slots, np.float64)
    sites = np.array([(i, j) for i in range(SIDE) for j in range(SIDE)], np.float64)
    weight = np.where((waves == 0).all(1), 1.0, 2.0)[:, None] / CYCLE**2
    site_angle = 2 * np.pi * ((waves @ sites.T) % CYCLE) / CYCLE
    into = np.zeros((2 * HALF, AREA))
    into[:count] = np.cos(site_angle)
    into[HALF : HALF + count] = -np.sin(site_angle)
    back = np.zeros((AREA, 2 * HALF))
    back[:, :count] = (np.cos(site_angle) * weight).T
    back[:, HALF : HALF + count] = -(np.sin(site_angle) * weight).T
    tap_into = np.zeros((CELLS_MAX, 2 * HALF, TAP_ROWS))
    tap_back = np.zeros((CELLS_MAX, TAP_ROWS, 2 * HALF))
    for slot in range(CELLS_MAX):
        size = 2 * slot + 3
        reach = size // 2
        shifts = np.array(
            [(u - reach, v - reach) for u in range(size) for v in range(size)], np.float64
        )
        taps = slice(TAP_STARTS[slot], TAP_STARTS[slot] + size * size)
        tap_angle = 2 * np.pi * ((waves @ shifts.T) % CYCLE) / CYCLE
        tap_into[slot, :count, taps] = np.cos(tap_angle)
        tap_into[slot, HALF : HALF + count, taps] = np.sin(tap_angle)
        tap_back[slot, taps, :count] = (np.cos(tap_angle) * weight).T
        tap_back[slot, taps, HALF : HALF + count] = -(np.sin(tap_angle) * weight).T
    return [pair_of(table) for table in (into, back, tap_into, tap_back)]


def pair_of(table):
    high = table.astype(ml_dtypes.bfloat16)
    low = (table - high.astype(np.float64)).astype(ml_dtypes.bfloat16)
    return np.stack([high, low])


def mul(a, b):
    return jnp.dot(a, b, preferred_element_type=jnp.float32)


def halves(values):
    high = values.astype(jnp.bfloat16)
    low = (values - high.astype(jnp.float32)).astype(jnp.bfloat16)
    return high, low


def cells_kernel(
    cells_ref,
    labels_ref,
    live_count_ref,
    features_ref,
    weight_ref,
    head_ref,
    into_ref,
    back_ref,
    tap_into_ref,
    tap_back_ref,
    grad_ref,
    order_ref,
    acts_ref,
    deep_ref,
    wave_ref,
    cot_ref,
    deep_cot_ref,
    total_ref,
):
    sections, channels = weight_ref.shape[0], weight_ref.shape[-1]
    span = channels // CORES
    point_rows = CELLS_MAX * span
    loss_start = point_rows + TAP_ROWS
    pipe = lax.axis_index("pipe")
    count = jnp.int32(0)
    for section in range(sections):
        held = cells_ref[section]
        for slot in range(CELLS_MAX):
            order_ref[count + slot] = section * CELLS_MAX + slot
        for slot in range(1, CELLS_MAX):

            @pl.when(slot >= held)
            def _(section=section, slot=slot):
                for core in range(CORES):
                    grad_ref[section, core, slot * span : (slot + 1) * span] = jnp.zeros(
                        (span, channels), jnp.bfloat16
                    )
                row = point_rows + TAP_STARTS[slot]
                grad_ref[section, TAP_HALVES[slot], row : row + TAP_SPANS[slot]] = jnp.zeros(
                    (TAP_SPANS[slot], channels), jnp.bfloat16
                )

        count = count + held

    acts_ref[0] = features_ref[...]

    def rows_of(image):
        return pl.ds(image * AREA, AREA)

    def forward(step, _):
        cell = order_ref[step]
        section = lax.div(cell, CELLS_MAX)
        slot = lax.rem(cell, CELLS_MAX)
        taps = weight_ref[section, lax.div(slot, CELLS_MAX - 1), point_rows:]
        wave = mul(tap_into_ref[0, slot], taps) + mul(tap_into_ref[1, slot], taps)
        wave_ref[step] = wave
        wave_re, wave_im = wave[:HALF], wave[HALF:]
        for image in range(IMAGES):
            site = jnp.maximum(acts_ref[step, rows_of(image)], 0)
            seen = mul(into_ref[0], site) + mul(into_ref[1], site)
            seen_re, seen_im = seen[:HALF], seen[HALF:]
            mixed = jnp.concatenate(
                [
                    seen_re * wave_re - seen_im * wave_im,
                    seen_re * wave_im + seen_im * wave_re,
                ],
                axis=0,
            )
            high, low = halves(mixed)
            deep = mul(back_ref[0], high) + mul(back_ref[0], low) + mul(back_ref[1], high)
            deep_ref[step, rows_of(image)] = deep.astype(jnp.bfloat16)
        rows = pl.ds(pl.multiple_of(slot * span, span), span)
        mixed = mul(deep_ref[step, :, :span], weight_ref[section, 0, rows]) + mul(
            deep_ref[step, :, span:], weight_ref[section, 1, rows]
        )
        acts_ref[step + 1] = (acts_ref[step].astype(jnp.float32) + mixed).astype(jnp.bfloat16)
        return 0

    lax.fori_loop(0, count, forward, 0)

    means = [
        jnp.sum(acts_ref[count, rows_of(image)].astype(jnp.float32), axis=0, keepdims=True)
        for image in range(IMAGES)
    ]
    spare = jnp.zeros((8 - IMAGES, channels), jnp.float32)
    pooled = jnp.concatenate(means + [spare], axis=0) / AREA
    head = head_ref[...]
    scores = lax.dot_general(
        pooled,
        head,
        (((1,), (1,)), ((), ())),
        precision=lax.Precision.HIGHEST,
        preferred_element_type=jnp.float32,
    )
    capped = jnp.tanh(scores / LOGIT_CAP)
    logits = LOGIT_CAP * capped
    exponent = jnp.exp(logits)
    total = jnp.sum(exponent, axis=1, keepdims=True)
    classes = lax.broadcasted_iota(jnp.int32, logits.shape, 1)
    image_row = lax.broadcasted_iota(jnp.int32, (8, 1), 0)
    targets = jnp.zeros((8, 1), jnp.int32)
    live = jnp.zeros((8, 1), jnp.float32)
    for image in range(IMAGES):
        place = pipe + sections * image
        is_live = (lax.div(place, MB_IMG) < live_count_ref[0]).astype(jnp.float32)
        targets = jnp.where(image_row == image, labels_ref[place], targets)
        live = jnp.where(image_row == image, is_live, live)
    onehot = (classes == targets).astype(jnp.float32)
    row_loss = (jnp.log(total) - jnp.sum(logits * onehot, axis=1, keepdims=True)) * live
    score_cot = (exponent / total - onehot) * live * (1.0 - capped * capped)
    pooled_cot = jnp.dot(
        score_cot, head, precision=lax.Precision.HIGHEST, preferred_element_type=jnp.float32
    )
    spread = pooled_cot / AREA
    for image in range(IMAGES):
        cot_ref[rows_of(image)] = jnp.broadcast_to(
            spread[image : image + 1], (AREA, channels)
        ).astype(jnp.bfloat16)

    loss = jnp.broadcast_to(jnp.sum(row_loss, axis=0, keepdims=True), (LOSS_ROWS, channels))
    high = loss.astype(jnp.bfloat16).astype(jnp.float32)
    middle = (loss - high).astype(jnp.bfloat16).astype(jnp.float32)
    low = loss - high - middle
    device = lax.axis_index("dp") * sections + pipe
    part = lax.broadcasted_iota(jnp.int32, loss.shape, 0)
    own = lax.broadcasted_iota(jnp.int32, loss.shape, 1) == device
    parts = jnp.where(part == 0, high, jnp.where(part == 1, middle, low))
    parts = jnp.where(own & (part < 3), parts, 0.0).astype(jnp.bfloat16)
    for section in range(sections):
        for core in range(CORES):
            grad_ref[section, core, loss_start : loss_start + LOSS_ROWS] = parts
            grad_ref[section, core, loss_start + LOSS_ROWS :] = jnp.zeros(
                (HALF_ROWS - loss_start - LOSS_ROWS, channels), jnp.bfloat16
            )

    def backward(turn, _):
        step = count - 1 - turn
        cell = order_ref[step]
        section = lax.div(cell, CELLS_MAX)
        slot = lax.rem(cell, CELLS_MAX)
        rows = pl.ds(pl.multiple_of(slot * span, span), span)
        cot = cot_ref[...]
        for core in range(CORES):
            columns = slice(core * span, (core + 1) * span)
            grad_ref[section, core, rows] = lax.dot_general(
                deep_ref[step, :, columns],
                cot,
                (((0,), (0,)), ((), ())),
                preferred_element_type=jnp.float32,
            ).astype(jnp.bfloat16)
            deep_cot_ref[:, columns] = lax.dot_general(
                cot,
                weight_ref[section, core, rows],
                (((1,), (1,)), ((), ())),
                preferred_element_type=jnp.float32,
            ).astype(jnp.bfloat16)
        wave_re, wave_im = wave_ref[step, :HALF], wave_ref[step, HALF:]
        for image in range(IMAGES):
            acts = acts_ref[step, rows_of(image)]
            seen = mul(into_ref[0], jnp.maximum(acts, 0))
            seen_re, seen_im = seen[:HALF], seen[HALF:]
            sent = mul(into_ref[0], deep_cot_ref[rows_of(image)])
            sent_re, sent_im = sent[:HALF], sent[HALF:]
            part_re = seen_re * sent_re + seen_im * sent_im
            part_im = seen_im * sent_re - seen_re * sent_im
            if image == 0:
                total_ref[:HALF] = part_re
                total_ref[HALF:] = part_im
            else:
                total_ref[:HALF] += part_re
                total_ref[HALF:] += part_im
            mixed = jnp.concatenate(
                [
                    sent_re * wave_re + sent_im * wave_im,
                    sent_im * wave_re - sent_re * wave_im,
                ],
                axis=0,
            ).astype(jnp.bfloat16)
            rect_cot = mul(back_ref[0], mixed)
            cot_ref[rows_of(image)] = (
                cot_ref[rows_of(image)].astype(jnp.float32)
                + jnp.where(acts.astype(jnp.float32) > 0, rect_cot, 0.0)
            ).astype(jnp.bfloat16)
        high, low = halves(total_ref[...])
        taps = (
            mul(tap_back_ref[0, slot], high)
            + mul(tap_back_ref[0, slot], low)
            + mul(tap_back_ref[1, slot], high)
        ).astype(jnp.bfloat16)
        for kind in range(CELLS_MAX):

            @pl.when(slot == kind)
            def _(kind=kind):
                first, last = TAP_STARTS[kind], TAP_STARTS[kind] + TAP_SPANS[kind]
                grad_ref[section, TAP_HALVES[kind], point_rows + first : point_rows + last] = taps[
                    first:last
                ]

        return 0

    lax.fori_loop(0, count, backward, 0)


def run_cells(cells, labels, live_count, features, weights, head):
    sections, channels = weights.shape[0], weights.shape[-1]
    slots = sections * CELLS_MAX
    tables = [jnp.asarray(table) for table in transform_tables()]
    vmem = pl.BlockSpec(memory_space=pltpu.VMEM)
    smem = pl.BlockSpec(memory_space=pltpu.SMEM)
    rows = IMAGES * AREA
    return pl.pallas_call(
        cells_kernel,
        out_shape=jax.ShapeDtypeStruct((sections, CORES, HALF_ROWS, channels), jnp.bfloat16),
        in_specs=[smem] * 3 + [vmem] * 7,
        out_specs=vmem,
        scratch_shapes=[
            pltpu.SMEM((slots + CELLS_MAX,), jnp.int32),
            pltpu.VMEM((slots + 1, rows, channels), jnp.bfloat16),
            pltpu.VMEM((slots, rows, channels), jnp.bfloat16),
            pltpu.VMEM((slots, 2 * HALF, channels), jnp.float32),
            pltpu.VMEM((rows, channels), jnp.bfloat16),
            pltpu.VMEM((rows, channels), jnp.bfloat16),
            pltpu.VMEM((2 * HALF, channels), jnp.float32),
        ],
        compiler_params=pltpu.CompilerParams(vmem_limit_bytes=CELLS_MB * 1024 * 1024),
        name="cells",
    )(cells, labels, live_count, features, weights, head, *tables)


class Place:
    def __init__(self, sections):
        self.sections = sections
        self.pipe = lax.axis_index("pipe")
        place = lax.axis_index("dp")
        self.core = lax.rem(place, CORES)
        self.z = lax.rem(lax.div(place, CORES), CHIPS_Z)
        self.x = lax.div(place, CORES * CHIPS_Z)

    def device(self, pipe=0, x=0, z=0, core=0):
        pipe = lax.rem(self.pipe + pipe, self.sections)
        x = lax.rem(self.x + x, CHIPS_X)
        z = lax.rem(self.z + z, CHIPS_Z)
        core = lax.rem(self.core + core, CORES)
        return (pipe, (x * CHIPS_Z + z) * CORES + core)

    def signal(self, partners):
        barrier = pltpu.get_barrier_semaphore()
        for partner in partners:
            pl.semaphore_signal(barrier, inc=1, device_id=partner, device_id_type=MESH)

    def wait(self, partners):
        pl.semaphore_wait(pltpu.get_barrier_semaphore(), partners)


def start_remote(source, target, send_sems, recv_sems, index, device):
    copy = pltpu.make_async_remote_copy(
        src_ref=source,
        dst_ref=target,
        send_sem=send_sems.at[index],
        recv_sem=recv_sems.at[index],
        device_id=device,
        device_id_type=MESH,
    )
    copy.start()
    return copy


def start_local(source, target, sems, index):
    copy = pltpu.make_async_copy(source, target, sems.at[index])
    copy.start()
    return copy


def gather_kernel(
    sections,
    weight_ref,
    three_ref,
    five_ref,
    seven_ref,
    features_ref,
    weights_ref,
    own_ref,
    taps_ref,
    direct_send,
    direct_recv,
    split_send,
    split_recv,
    spread_send,
    spread_recv,
    core_send,
    core_recv,
    weight_sem,
):
    at = Place(sections)
    others_y = range(1, sections)
    others_x = range(1, CHIPS_X)
    core = at.core
    channels = weights_ref.shape[-1]
    span = channels // CORES
    point_rows = CELLS_MAX * span
    at.signal(
        [at.device(pipe=d) for d in others_y]
        + [at.device(x=d) for d in others_x]
        + [at.device(core=1)]
    )
    loads = []
    for half in (core, lax.rem(core + 1, CORES)):
        for cell in range(CELLS_MAX):
            loads.append(
                start_local(
                    weight_ref.at[cell, half],
                    weights_ref.at[at.pipe, half, pl.ds(cell * span, span)],
                    weight_sem,
                    len(loads),
                )
            )
    taps_ref[...] = jnp.zeros_like(taps_ref)
    for slot, ref in enumerate((three_ref, five_ref, seven_ref)):
        size = 2 * slot + 3
        for u in range(size):
            row = TAP_STARTS[slot] + u * size
            taps_ref[TAP_HALVES[slot], row : row + size] = ref[u].astype(jnp.float32)
    for half in range(CORES):
        weights_ref[at.pipe, half, point_rows:] = taps_ref[half].astype(jnp.bfloat16)
    for copy in loads[:CELLS_MAX]:
        copy.wait()
    at.wait((sections - 1) + (CHIPS_X - 1) + 1)

    near = pl.ds(0, WEIGHT_A)
    far = pl.ds(WEIGHT_A, point_rows + TAP_ROWS - WEIGHT_A)

    def lanes(x):
        return pl.ds(pl.multiple_of(x * LANES, LANES), LANES)

    split, direct = [], []
    for d in others_y:
        piece = weights_ref.at[at.pipe, core, far, lanes(at.x)]
        split.append(
            start_remote(piece, piece, split_send, split_recv, d - 1, at.device(pipe=d))
        )
    for d in others_y:
        piece = weights_ref.at[at.pipe, core, near]
        direct.append(
            start_remote(piece, piece, direct_send, direct_recv, d - 1, at.device(pipe=d))
        )
    per_replica = features_ref.shape[0] // AREA
    group = (GROUP * IMAGES, GROUP * per_replica)
    row = lax.broadcasted_iota(jnp.int32, group, 0)
    column = lax.broadcasted_iota(jnp.int32, group, 1)
    wanted = lax.rem(row, GROUP) * per_replica + lax.div(row, GROUP) * sections + at.pipe
    pick = (column == wanted).astype(jnp.float32).astype(jnp.bfloat16)
    for g in range(AREA // GROUP):
        picked = mul(pick, features_ref[g * group[1] : (g + 1) * group[1]]).astype(jnp.bfloat16)
        for k in range(IMAGES):
            row = k * AREA + g * GROUP
            own_ref[row : row + GROUP] = picked[k * GROUP : (k + 1) * GROUP]

    spread, shared = [], []

    def share(piece):
        k = len(shared)
        shared.append(start_remote(piece, piece, core_send, core_recv, k, at.device(core=1)))

    def source(d):
        return lax.rem(at.pipe + sections - d, sections)

    for d in others_y:
        split[d - 1].wait_recv()
        piece = weights_ref.at[source(d), core, far, lanes(at.x)]
        for e in others_x:
            k = (d - 1) * (CHIPS_X - 1) + e - 1
            spread.append(
                start_remote(piece, piece, spread_send, spread_recv, k, at.device(x=e))
            )
        share(piece)
    for d in others_y:
        direct[d - 1].wait_recv()
        share(weights_ref.at[source(d), core, near])
    for d in others_y:
        for e in others_x:
            spread[(d - 1) * (CHIPS_X - 1) + e - 1].wait_recv()
            x = lax.rem(at.x + CHIPS_X - e, CHIPS_X)
            share(weights_ref.at[source(d), core, far, lanes(x)])
    for copy in loads[CELLS_MAX:]:
        copy.wait()
    for copy in shared:
        copy.wait_recv()
    for copy in shared + split + direct + spread:
        copy.wait_send()


def gather_weights(weight, three, five, seven, features, sections):
    cells, channels = weight.shape[0], weight.shape[-1]
    weight = weight.reshape(cells, CORES, channels // CORES, channels)
    vmem = pl.BlockSpec(memory_space=pltpu.VMEM)
    anywhere = pl.BlockSpec(memory_space=pl.ANY)
    dma = pltpu.SemaphoreType.DMA
    ys, xs = sections - 1, CHIPS_X - 1
    rows = cells * channels // CORES + TAP_ROWS
    return pl.pallas_call(
        functools.partial(gather_kernel, sections),
        out_shape=(
            jax.ShapeDtypeStruct((sections, CORES, rows, channels), weight.dtype),
            jax.ShapeDtypeStruct((IMAGES * AREA, channels), features.dtype),
        ),
        in_specs=[anywhere, vmem, vmem, vmem, vmem],
        out_specs=(vmem, vmem),
        scratch_shapes=[
            pltpu.VMEM((CORES, TAP_ROWS, channels), jnp.float32),
            dma((ys,)),
            dma((ys,)),
            dma((ys,)),
            dma((ys,)),
            dma((ys * xs,)),
            dma((ys * xs,)),
            dma((2 * ys + ys * xs,)),
            dma((2 * ys + ys * xs,)),
            dma((CORES * cells,)),
        ],
        compiler_params=pltpu.CompilerParams(
            collective_id=0, has_side_effects=True, vmem_limit_bytes=24 * 1024 * 1024
        ),
        name="gather",
    )(weight, three, five, seven, features)


def reduce_kernel(
    sections,
    grad_ref,
    out_ref,
    own_ref,
    pair_ref,
    part_a_ref,
    part_b_ref,
    in_a1_ref,
    in_b1_ref,
    mid_a_ref,
    mid_b_ref,
    in_a2_ref,
    in_b2_ref,
    small_ref,
    in_z_ref,
    line_ref,
    plane_ref,
    pair_send,
    pair_recv,
    a1_send,
    a1_recv,
    b1_send,
    b1_recv,
    a2_send,
    a2_recv,
    b2_send,
    b2_recv,
    z_send,
    z_recv,
    line_send,
    line_recv,
    plane_send,
    plane_recv,
    core_send,
    core_recv,
    local_sem,
):
    at = Place(sections)
    others_y = range(1, sections)
    others_x = range(1, CHIPS_X)
    others_z = range(1, CHIPS_Z)
    partner = at.device(core=1)
    at.signal(
        [partner]
        + [at.device(pipe=d) for d in others_y]
        + [at.device(x=d) for d in others_x]
        + [at.device(z=d) for d in others_z]
    )
    at.wait(1 + len(others_y) + len(others_x) + len(others_z))
    f32 = jnp.float32
    bf16 = jnp.bfloat16

    def lanes(x):
        return pl.ds(pl.multiple_of(x * LANES, LANES), LANES)

    order = [lax.rem(at.pipe + d, sections) for d in (2, 1, 3, 0)]
    paired, local = [], []
    for k, section in enumerate(order):
        paired.append(
            start_remote(
                grad_ref.at[section, lax.rem(at.core + 1, CORES)],
                pair_ref.at[section],
                pair_send,
                pair_recv,
                k,
                partner,
            )
        )
        local.append(start_local(grad_ref.at[section, at.core], own_ref.at[section], local_sem, k))
    a1, b1 = {}, []
    for k, section in enumerate(order):
        local[k].wait()
        paired[k].wait_recv()

        def add_pair(z, _, section=section):
            total = own_ref[section, z].astype(f32) + pair_ref[section, z].astype(f32)
            part_a_ref[section, z] = total[:CHUNK_A].astype(bf16)
            part_b_ref[section, z] = total[CHUNK_A:].astype(bf16)
            return 0

        lax.fori_loop(0, CHIPS_Z, add_pair, 0)
        d = (2, 1, 3, 0)[k]
        if d:
            a1[d] = start_remote(
                part_a_ref.at[section],
                in_a1_ref.at[d - 1],
                a1_send,
                a1_recv,
                d - 1,
                at.device(pipe=d),
            )
        for e in others_x:
            b1.append(
                start_remote(
                    part_b_ref.at[
                        section,
                        pl.ds(0, CHIPS_Z),
                        pl.ds(0, CHUNK_B),
                        lanes(lax.rem(at.x + e, CHIPS_X)),
                    ],
                    in_b1_ref.at[e - 1, section],
                    b1_send,
                    b1_recv,
                    k * (CHIPS_X - 1) + e - 1,
                    at.device(x=e),
                )
            )
    b2 = {}
    for k, section in enumerate(order):
        for e in others_x:
            b1[k * (CHIPS_X - 1) + e - 1].wait_recv()

        def add_b1(z, _, section=section):
            total = part_b_ref[section, z, :, lanes(at.x)].astype(f32)
            for e in others_x:
                total = total + in_b1_ref[e - 1, section, z].astype(f32)
            mid_b_ref[section, z] = total.astype(bf16)
            return 0

        lax.fori_loop(0, CHIPS_Z, add_b1, 0)
        d = (2, 1, 3, 0)[k]
        if d:
            b2[d] = start_remote(
                mid_b_ref.at[section],
                in_b2_ref.at[d - 1],
                b2_send,
                b2_recv,
                d - 1,
                at.device(pipe=d),
            )
    for d in others_y:
        a1[d].wait_recv()

    def add_a1(z, _):
        total = part_a_ref[at.pipe, z].astype(f32)
        for d in others_y:
            total = total + in_a1_ref[d - 1, z].astype(f32)
        mid_a_ref[z] = total.astype(bf16)
        return 0

    lax.fori_loop(0, CHIPS_Z, add_a1, 0)
    a2 = [
        start_remote(
            mid_a_ref.at[
                pl.ds(0, CHIPS_Z), pl.ds(0, CHUNK_A), lanes(lax.rem(at.x + e, CHIPS_X))
            ],
            in_a2_ref.at[e - 1],
            a2_send,
            a2_recv,
            e - 1,
            at.device(x=e),
        )
        for e in others_x
    ]
    for d in others_y:
        b2[d].wait_recv()
    for copy in a2:
        copy.wait_recv()

    def add_second(z, _):
        total_a = mid_a_ref[z, :, lanes(at.x)].astype(f32)
        total_b = mid_b_ref[at.pipe, z].astype(f32)
        for e in others_x:
            total_a = total_a + in_a2_ref[e - 1, z].astype(f32)
        for d in others_y:
            total_b = total_b + in_b2_ref[d - 1, z].astype(f32)
        small_ref[z, :CHUNK_A] = total_a.astype(bf16)
        small_ref[z, CHUNK_A:] = total_b.astype(bf16)
        return 0

    lax.fori_loop(0, CHIPS_Z, add_second, 0)
    to_z = [
        start_remote(
            small_ref.at[lax.rem(at.z + d, CHIPS_Z)],
            in_z_ref.at[d - 1],
            z_send,
            z_recv,
            d - 1,
            at.device(z=d),
        )
        for d in others_z
    ]
    for copy in to_z:
        copy.wait_recv()
    total = small_ref[at.z].astype(f32)
    for d in others_z:
        total = total + in_z_ref[d - 1].astype(f32)
    line_ref[at.z] = total.astype(bf16)
    piece = line_ref.at[at.z]
    line = [
        start_remote(piece, piece, line_send, line_recv, d - 1, at.device(z=d)) for d in others_z
    ]
    for copy in line:
        copy.wait_recv()
    column = plane_ref.at[pl.ds(0, CHIPS_Z), pl.ds(0, CHUNK), lanes(at.x)]
    plane = [
        start_remote(line_ref, column, plane_send, plane_recv, e - 1, at.device(x=e))
        for e in others_x
    ]
    own_column = start_local(line_ref, column, local_sem, 0)
    own_column.wait()
    for copy in plane:
        copy.wait_recv()
    half = out_ref.at[at.core]
    last = start_remote(plane_ref, half, core_send, core_recv, 0, partner)
    own_half = start_local(plane_ref, half, local_sem, 1)
    own_half.wait()
    last.wait()
    for copy in paired + b1 + list(a1.values()) + list(b2.values()) + a2 + to_z + line + plane:
        copy.wait_send()


def reduce_grads(grads, sections):
    rows, channels = grads.shape[2:]
    grads = grads.reshape(sections, CORES, CHIPS_Z, CHUNK, channels)
    anywhere = pl.BlockSpec(memory_space=pl.ANY)
    dma = pltpu.SemaphoreType.DMA
    ys, xs, zs = sections - 1, CHIPS_X - 1, CHIPS_Z - 1

    def vmem(*shape):
        return pltpu.VMEM(shape, jnp.bfloat16)

    out = pl.pallas_call(
        functools.partial(reduce_kernel, sections),
        out_shape=jax.ShapeDtypeStruct((CORES, CHIPS_Z, CHUNK, channels), jnp.bfloat16),
        in_specs=[anywhere],
        out_specs=anywhere,
        scratch_shapes=[
            vmem(sections, CHIPS_Z, CHUNK, channels),
            vmem(sections, CHIPS_Z, CHUNK, channels),
            vmem(sections, CHIPS_Z, CHUNK_A, channels),
            vmem(sections, CHIPS_Z, CHUNK_B, channels),
            vmem(ys, CHIPS_Z, CHUNK_A, channels),
            vmem(xs, sections, CHIPS_Z, CHUNK_B, LANES),
            vmem(CHIPS_Z, CHUNK_A, channels),
            vmem(sections, CHIPS_Z, CHUNK_B, LANES),
            vmem(xs, CHIPS_Z, CHUNK_A, LANES),
            vmem(ys, CHIPS_Z, CHUNK_B, LANES),
            vmem(CHIPS_Z, CHUNK, LANES),
            vmem(zs, CHUNK, LANES),
            vmem(CHIPS_Z, CHUNK, LANES),
            vmem(CHIPS_Z, CHUNK, channels),
            dma((sections,)),
            dma((sections,)),
            dma((ys,)),
            dma((ys,)),
            dma((sections * xs,)),
            dma((sections * xs,)),
            dma((xs,)),
            dma((xs,)),
            dma((ys,)),
            dma((ys,)),
            dma((zs,)),
            dma((zs,)),
            dma((zs,)),
            dma((zs,)),
            dma((xs,)),
            dma((xs,)),
            dma((1,)),
            dma((1,)),
            dma((sections,)),
        ],
        compiler_params=pltpu.CompilerParams(
            collective_id=1, has_side_effects=True, vmem_limit_bytes=40 * 1024 * 1024
        ),
        name="reduce",
    )(grads)
    return out.reshape(CORES, rows, channels)


def own_taps(block, slot):
    size = 2 * slot + 3
    start = CELLS_MAX * block.shape[-1] // CORES + TAP_STARTS[slot]
    rows = block[TAP_HALVES[slot], start : start + size * size].astype(jnp.float32)
    return rows.reshape(1, size, size, block.shape[-1])


def shards(
    features,
    labels,
    micro_count,
    cells_per_section,
    point_weight,
    depth_three,
    depth_five,
    depth_seven,
    head_weight,
):
    sections = lax.axis_size("pipe")
    channels = point_weight.shape[-1]
    by_position = features.transpose(1, 2, 0, 3).reshape(-1, channels)
    weights, own = gather_weights(
        point_weight[0], depth_three[0], depth_five[0], depth_seven[0], by_position, sections
    )
    grads = run_cells(cells_per_section, labels, micro_count, own, weights, head_weight.T)
    block = reduce_grads(grads, sections)
    span = channels // CORES
    point_rows = CELLS_MAX * span
    loss_start = point_rows + TAP_ROWS
    total_loss = jnp.sum(block[0, loss_start : loss_start + 3].astype(jnp.float32))
    point_sum = block[:, :point_rows].reshape(CORES, CELLS_MAX, span, channels)
    point_sum = point_sum.transpose(1, 0, 2, 3).astype(jnp.float32)
    return (
        total_loss,
        point_sum.reshape(1, CELLS_MAX, channels, channels),
        own_taps(block, 0),
        own_taps(block, 1),
        own_taps(block, 2),
    )


def solution(mesh):
    return jax.shard_map(
        shards,
        mesh=mesh,
        in_specs=(
            P("dp", None, None, None),
            P("dp"),
            P("dp"),
            P(),
            P("pipe", None, None, None),
            P("pipe", None, None, None),
            P("pipe", None, None, None),
            P("pipe", None, None, None),
            P(),
        ),
        out_specs=(
            P(),
            P("pipe", None, None, None),
            P("pipe", None, None, None),
            P("pipe", None, None, None),
            P("pipe", None, None, None),
        ),
        check_vma=False,
    )
```

```python
import functools

import jax
import jax.numpy as jnp
import ml_dtypes
import numpy as np
from jax import lax
from jax.experimental import pallas as pl
from jax.experimental.pallas import tpu as pltpu
from jax.sharding import PartitionSpec as P

SIDE = 12
AREA = SIDE * SIDE
MB_IMG = 2
CELLS_MAX = 3
TAPS = 7
TAP_ROWS = 64
LOGIT_CAP = 30.0
CYCLE = SIDE + TAPS // 2
HALF = 120
IMAGES = 4
GROUP = 16
CHIPS_X = 4
CHIPS_Z = 8
CORES = 2
LANES = 128
MESH = pl.DeviceIdType.MESH
TAP_HALVES = (0, 0, 1)
TAP_STARTS = (0, 16, 0)
TAP_SPANS = (16, 32, 64)
CHUNK = 112
STREAMS = ((0, 32), (32, 32), (64, 32), (96, 16))
TURNS = (0, 1, 2, 3, 0, 1, 0, 2, 1, 0, 0, 3, 2, 1, 0, 1, 3, 2, 1, 2, 0, 3, 2, 3, 1, 3, 2, 3)
FIRST_Z = 4
LAST_Z = CHIPS_Z - FIRST_Z
HALF_ROWS = CHIPS_Z * CHUNK
LOSS_ROWS = 16
WEIGHT_A = 320
CELLS_MB = 32


def transform_tables():
    slots = [(0, 0)]
    seen = {(0, 0)}
    for u in range(CYCLE):
        for v in range(CYCLE):
            if (u, v) in seen:
                continue
            seen.add((u, v))
            seen.add(((-u) % CYCLE, (-v) % CYCLE))
            slots.append((u, v))
    count = len(slots)
    waves = np.array(slots, np.float64)
    sites = np.array([(i, j) for i in range(SIDE) for j in range(SIDE)], np.float64)
    weight = np.where((waves == 0).all(1), 1.0, 2.0)[:, None] / CYCLE**2
    site_angle = 2 * np.pi * ((waves @ sites.T) % CYCLE) / CYCLE
    into = np.zeros((2 * HALF, AREA))
    into[:count] = np.cos(site_angle)
    into[HALF : HALF + count] = -np.sin(site_angle)
    back = np.zeros((AREA, 2 * HALF))
    back[:, :count] = (np.cos(site_angle) * weight).T
    back[:, HALF : HALF + count] = -(np.sin(site_angle) * weight).T
    tap_into = np.zeros((CELLS_MAX, 2 * HALF, TAP_ROWS))
    tap_back = np.zeros((CELLS_MAX, TAP_ROWS, 2 * HALF))
    for slot in range(CELLS_MAX):
        size = 2 * slot + 3
        reach = size // 2
        shifts = np.array(
            [(u - reach, v - reach) for u in range(size) for v in range(size)], np.float64
        )
        taps = slice(TAP_STARTS[slot], TAP_STARTS[slot] + size * size)
        tap_angle = 2 * np.pi * ((waves @ shifts.T) % CYCLE) / CYCLE
        tap_into[slot, :count, taps] = np.cos(tap_angle)
        tap_into[slot, HALF : HALF + count, taps] = np.sin(tap_angle)
        tap_back[slot, taps, :count] = (np.cos(tap_angle) * weight).T
        tap_back[slot, taps, HALF : HALF + count] = -(np.sin(tap_angle) * weight).T
    return [pair_of(into)[0], pair_of(back)[0], pair_of(tap_into), pair_of(tap_back)]


def pair_of(table):
    high = table.astype(ml_dtypes.bfloat16)
    low = (table - high.astype(np.float64)).astype(ml_dtypes.bfloat16)
    return np.stack([high, low])


def mul(a, b):
    return jnp.dot(a, b, preferred_element_type=jnp.float32)


def halves(values):
    high = values.astype(jnp.bfloat16)
    low = (values - high.astype(jnp.float32)).astype(jnp.bfloat16)
    return high, low


def cells_kernel(
    cells_ref,
    labels_ref,
    live_count_ref,
    features_ref,
    weight_ref,
    head_ref,
    into_ref,
    back_ref,
    tap_into_ref,
    tap_back_ref,
    grad_ref,
    order_ref,
    acts_ref,
    deep_ref,
    wave_ref,
    cot_ref,
    deep_cot_ref,
    total_ref,
):
    sections, channels = weight_ref.shape[0], weight_ref.shape[-1]
    span = channels // CORES
    point_rows = CELLS_MAX * span
    loss_start = point_rows + TAP_ROWS
    pipe = lax.axis_index("pipe")
    count = jnp.int32(0)
    for section in range(sections):
        held = cells_ref[section]
        for slot in range(CELLS_MAX):
            order_ref[count + slot] = section * CELLS_MAX + slot
        for slot in range(1, CELLS_MAX):

            @pl.when(slot >= held)
            def _(section=section, slot=slot):
                for core in range(CORES):
                    grad_ref[section, core, slot * span : (slot + 1) * span] = jnp.zeros(
                        (span, channels), jnp.bfloat16
                    )
                row = point_rows + TAP_STARTS[slot]
                grad_ref[section, TAP_HALVES[slot], row : row + TAP_SPANS[slot]] = jnp.zeros(
                    (TAP_SPANS[slot], channels), jnp.bfloat16
                )

        count = count + held

    acts_ref[0] = features_ref[...]

    def rows_of(image):
        return pl.ds(image * AREA, AREA)

    def lanes_of(image):
        return slice(image * channels, (image + 1) * channels)

    def abreast(ref):
        return jnp.concatenate([ref[rows_of(image)] for image in range(IMAGES)], axis=1)

    def forward(step, _):
        cell = order_ref[step]
        section = lax.div(cell, CELLS_MAX)
        slot = lax.rem(cell, CELLS_MAX)
        taps = weight_ref[section, lax.div(slot, CELLS_MAX - 1), point_rows:]
        wave = mul(tap_into_ref[0, slot], taps) + mul(tap_into_ref[1, slot], taps)
        wave_ref[step] = wave
        wave_re, wave_im = wave[:HALF], wave[HALF:]
        seen = mul(into_ref[...], jnp.maximum(abreast(acts_ref.at[step]), 0))
        mixed = []
        for image in range(IMAGES):
            lanes = lanes_of(image)
            seen_re, seen_im = seen[:HALF, lanes], seen[HALF:, lanes]
            mixed.append(
                jnp.concatenate(
                    [
                        seen_re * wave_re - seen_im * wave_im,
                        seen_re * wave_im + seen_im * wave_re,
                    ],
                    axis=0,
                ).astype(jnp.bfloat16)
            )
        deep = mul(back_ref[...], jnp.concatenate(mixed, axis=1)).astype(jnp.bfloat16)
        for image in range(IMAGES):
            deep_ref[step, rows_of(image)] = deep[:, lanes_of(image)]
        rows = pl.ds(pl.multiple_of(slot * span, span), span)
        mixed = mul(deep_ref[step, :, :span], weight_ref[section, 0, rows]) + mul(
            deep_ref[step, :, span:], weight_ref[section, 1, rows]
        )
        acts_ref[step + 1] = (acts_ref[step].astype(jnp.float32) + mixed).astype(jnp.bfloat16)
        return 0

    lax.fori_loop(0, count, forward, 0)

    means = [
        jnp.sum(acts_ref[count, rows_of(image)].astype(jnp.float32), axis=0, keepdims=True)
        for image in range(IMAGES)
    ]
    spare = jnp.zeros((8 - IMAGES, channels), jnp.float32)
    pooled = jnp.concatenate(means + [spare], axis=0) / AREA
    head = head_ref[...]
    scores = lax.dot_general(
        pooled,
        head,
        (((1,), (1,)), ((), ())),
        precision=lax.Precision.HIGHEST,
        preferred_element_type=jnp.float32,
    )
    capped = jnp.tanh(scores / LOGIT_CAP)
    logits = LOGIT_CAP * capped
    exponent = jnp.exp(logits)
    total = jnp.sum(exponent, axis=1, keepdims=True)
    classes = lax.broadcasted_iota(jnp.int32, logits.shape, 1)
    image_row = lax.broadcasted_iota(jnp.int32, (8, 1), 0)
    targets = jnp.zeros((8, 1), jnp.int32)
    live = jnp.zeros((8, 1), jnp.float32)
    for image in range(IMAGES):
        place = pipe + sections * image
        is_live = (lax.div(place, MB_IMG) < live_count_ref[0]).astype(jnp.float32)
        targets = jnp.where(image_row == image, labels_ref[place], targets)
        live = jnp.where(image_row == image, is_live, live)
    onehot = (classes == targets).astype(jnp.float32)
    row_loss = (jnp.log(total) - jnp.sum(logits * onehot, axis=1, keepdims=True)) * live
    score_cot = (exponent / total - onehot) * live * (1.0 - capped * capped)
    pooled_cot = jnp.dot(
        score_cot, head, precision=lax.Precision.HIGHEST, preferred_element_type=jnp.float32
    )
    spread = pooled_cot / AREA
    for image in range(IMAGES):
        cot_ref[rows_of(image)] = jnp.broadcast_to(
            spread[image : image + 1], (AREA, channels)
        ).astype(jnp.bfloat16)

    loss = jnp.broadcast_to(jnp.sum(row_loss, axis=0, keepdims=True), (LOSS_ROWS, channels))
    high = loss.astype(jnp.bfloat16).astype(jnp.float32)
    middle = (loss - high).astype(jnp.bfloat16).astype(jnp.float32)
    low = loss - high - middle
    device = lax.axis_index("dp") * sections + pipe
    part = lax.broadcasted_iota(jnp.int32, loss.shape, 0)
    own = lax.broadcasted_iota(jnp.int32, loss.shape, 1) == device
    parts = jnp.where(part == 0, high, jnp.where(part == 1, middle, low))
    parts = jnp.where(own & (part < 3), parts, 0.0).astype(jnp.bfloat16)
    for section in range(sections):
        for core in range(CORES):
            grad_ref[section, core, loss_start : loss_start + LOSS_ROWS] = parts
            grad_ref[section, core, loss_start + LOSS_ROWS :] = jnp.zeros(
                (HALF_ROWS - loss_start - LOSS_ROWS, channels), jnp.bfloat16
            )

    def backward(turn, _):
        step = count - 1 - turn
        cell = order_ref[step]
        section = lax.div(cell, CELLS_MAX)
        slot = lax.rem(cell, CELLS_MAX)
        rows = pl.ds(pl.multiple_of(slot * span, span), span)
        cot = cot_ref[...]
        for core in range(CORES):
            columns = slice(core * span, (core + 1) * span)
            grad_ref[section, core, rows] = lax.dot_general(
                deep_ref[step, :, columns],
                cot,
                (((0,), (0,)), ((), ())),
                preferred_element_type=jnp.float32,
            ).astype(jnp.bfloat16)
            deep_cot_ref[:, columns] = lax.dot_general(
                cot,
                weight_ref[section, core, rows],
                (((1,), (1,)), ((), ())),
                preferred_element_type=jnp.float32,
            ).astype(jnp.bfloat16)
        wave_re, wave_im = wave_ref[step, :HALF], wave_ref[step, HALF:]
        acts = abreast(acts_ref.at[step])
        seen = mul(into_ref[...], jnp.maximum(acts, 0))
        sent = mul(into_ref[...], abreast(deep_cot_ref))
        mixed = []
        for image in range(IMAGES):
            lanes = lanes_of(image)
            seen_re, seen_im = seen[:HALF, lanes], seen[HALF:, lanes]
            sent_re, sent_im = sent[:HALF, lanes], sent[HALF:, lanes]
            part_re = seen_re * sent_re + seen_im * sent_im
            part_im = seen_im * sent_re - seen_re * sent_im
            if image == 0:
                total_ref[:HALF] = part_re
                total_ref[HALF:] = part_im
            else:
                total_ref[:HALF] += part_re
                total_ref[HALF:] += part_im
            mixed.append(
                jnp.concatenate(
                    [
                        sent_re * wave_re + sent_im * wave_im,
                        sent_im * wave_re - sent_re * wave_im,
                    ],
                    axis=0,
                ).astype(jnp.bfloat16)
            )
        rect_cot = mul(back_ref[...], jnp.concatenate(mixed, axis=1))
        for image in range(IMAGES):
            lanes = lanes_of(image)
            passed = jnp.where(acts[:, lanes].astype(jnp.float32) > 0, rect_cot[:, lanes], 0.0)
            cot_ref[rows_of(image)] = (
                cot_ref[rows_of(image)].astype(jnp.float32) + passed
            ).astype(jnp.bfloat16)
        high, low = halves(total_ref[...])
        taps = (
            mul(tap_back_ref[0, slot], high)
            + mul(tap_back_ref[0, slot], low)
            + mul(tap_back_ref[1, slot], high)
        ).astype(jnp.bfloat16)
        for kind in range(CELLS_MAX):

            @pl.when(slot == kind)
            def _(kind=kind):
                first, last = TAP_STARTS[kind], TAP_STARTS[kind] + TAP_SPANS[kind]
                grad_ref[section, TAP_HALVES[kind], point_rows + first : point_rows + last] = taps[
                    first:last
                ]

        return 0

    lax.fori_loop(0, count, backward, 0)


def run_cells(cells, labels, live_count, features, weights, head):
    sections, channels = weights.shape[0], weights.shape[-1]
    slots = sections * CELLS_MAX
    tables = [jnp.asarray(table) for table in transform_tables()]
    vmem = pl.BlockSpec(memory_space=pltpu.VMEM)
    smem = pl.BlockSpec(memory_space=pltpu.SMEM)
    rows = IMAGES * AREA
    return pl.pallas_call(
        cells_kernel,
        out_shape=jax.ShapeDtypeStruct((sections, CORES, HALF_ROWS, channels), jnp.bfloat16),
        in_specs=[smem] * 3 + [vmem] * 7,
        out_specs=vmem,
        scratch_shapes=[
            pltpu.SMEM((slots + CELLS_MAX,), jnp.int32),
            pltpu.VMEM((slots + 1, rows, channels), jnp.bfloat16),
            pltpu.VMEM((slots, rows, channels), jnp.bfloat16),
            pltpu.VMEM((slots, 2 * HALF, channels), jnp.float32),
            pltpu.VMEM((rows, channels), jnp.bfloat16),
            pltpu.VMEM((rows, channels), jnp.bfloat16),
            pltpu.VMEM((2 * HALF, channels), jnp.float32),
        ],
        compiler_params=pltpu.CompilerParams(vmem_limit_bytes=CELLS_MB * 1024 * 1024),
        name="cells",
    )(cells, labels, live_count, features, weights, head, *tables)


class Place:
    def __init__(self, sections):
        self.sections = sections
        self.pipe = lax.axis_index("pipe")
        place = lax.axis_index("dp")
        self.core = lax.rem(place, CORES)
        self.z = lax.rem(lax.div(place, CORES), CHIPS_Z)
        self.x = lax.div(place, CORES * CHIPS_Z)

    def device(self, pipe=0, x=0, z=0, core=0):
        pipe = lax.rem(self.pipe + pipe, self.sections)
        x = lax.rem(self.x + x, CHIPS_X)
        z = lax.rem(self.z + z, CHIPS_Z)
        core = lax.rem(self.core + core, CORES)
        return (pipe, (x * CHIPS_Z + z) * CORES + core)

    def signal(self, partners):
        barrier = pltpu.get_barrier_semaphore()
        for partner in partners:
            pl.semaphore_signal(barrier, inc=1, device_id=partner, device_id_type=MESH)

    def wait(self, partners):
        pl.semaphore_wait(pltpu.get_barrier_semaphore(), partners)


def start_remote(source, target, send_sems, recv_sems, index, device):
    copy = pltpu.make_async_remote_copy(
        src_ref=source,
        dst_ref=target,
        send_sem=send_sems.at[index],
        recv_sem=recv_sems.at[index],
        device_id=device,
        device_id_type=MESH,
    )
    copy.start()
    return copy


def start_local(source, target, sems, index):
    copy = pltpu.make_async_copy(source, target, sems.at[index])
    copy.start()
    return copy


def gather_kernel(
    sections,
    weight_ref,
    three_ref,
    five_ref,
    seven_ref,
    features_ref,
    weights_ref,
    own_ref,
    taps_ref,
    direct_send,
    direct_recv,
    split_send,
    split_recv,
    spread_send,
    spread_recv,
    core_send,
    core_recv,
    weight_sem,
):
    at = Place(sections)
    others_y = range(1, sections)
    others_x = range(1, CHIPS_X)
    core = at.core
    channels = weights_ref.shape[-1]
    span = channels // CORES
    point_rows = CELLS_MAX * span
    at.signal(
        [at.device(pipe=d) for d in others_y]
        + [at.device(x=d) for d in others_x]
        + [at.device(core=1)]
    )
    loads = []
    for half in (core, lax.rem(core + 1, CORES)):
        for cell in range(CELLS_MAX):
            loads.append(
                start_local(
                    weight_ref.at[cell, half],
                    weights_ref.at[at.pipe, half, pl.ds(cell * span, span)],
                    weight_sem,
                    len(loads),
                )
            )
    taps_ref[...] = jnp.zeros_like(taps_ref)
    for slot, ref in enumerate((three_ref, five_ref, seven_ref)):
        size = 2 * slot + 3
        for u in range(size):
            row = TAP_STARTS[slot] + u * size
            taps_ref[TAP_HALVES[slot], row : row + size] = ref[u].astype(jnp.float32)
    for half in range(CORES):
        weights_ref[at.pipe, half, point_rows:] = taps_ref[half].astype(jnp.bfloat16)
    for copy in loads[:CELLS_MAX]:
        copy.wait()
    at.wait((sections - 1) + (CHIPS_X - 1) + 1)

    near = pl.ds(0, WEIGHT_A)
    far = pl.ds(WEIGHT_A, point_rows + TAP_ROWS - WEIGHT_A)

    def lanes(x):
        return pl.ds(pl.multiple_of(x * LANES, LANES), LANES)

    split, direct = [], []
    for d in others_y:
        piece = weights_ref.at[at.pipe, core, far, lanes(at.x)]
        split.append(
            start_remote(piece, piece, split_send, split_recv, d - 1, at.device(pipe=d))
        )
    for d in others_y:
        piece = weights_ref.at[at.pipe, core, near]
        direct.append(
            start_remote(piece, piece, direct_send, direct_recv, d - 1, at.device(pipe=d))
        )
    per_replica = features_ref.shape[0] // AREA
    group = (GROUP * IMAGES, GROUP * per_replica)
    row = lax.broadcasted_iota(jnp.int32, group, 0)
    column = lax.broadcasted_iota(jnp.int32, group, 1)
    wanted = lax.rem(row, GROUP) * per_replica + lax.div(row, GROUP) * sections + at.pipe
    pick = (column == wanted).astype(jnp.float32).astype(jnp.bfloat16)
    for g in range(AREA // GROUP):
        picked = mul(pick, features_ref[g * group[1] : (g + 1) * group[1]]).astype(jnp.bfloat16)
        for k in range(IMAGES):
            row = k * AREA + g * GROUP
            own_ref[row : row + GROUP] = picked[k * GROUP : (k + 1) * GROUP]

    spread, shared = [], []

    def share(piece):
        k = len(shared)
        shared.append(start_remote(piece, piece, core_send, core_recv, k, at.device(core=1)))

    def source(d):
        return lax.rem(at.pipe + sections - d, sections)

    for d in others_y:
        split[d - 1].wait_recv()
        piece = weights_ref.at[source(d), core, far, lanes(at.x)]
        for e in others_x:
            k = (d - 1) * (CHIPS_X - 1) + e - 1
            spread.append(
                start_remote(piece, piece, spread_send, spread_recv, k, at.device(x=e))
            )
        share(piece)
    for d in others_y:
        direct[d - 1].wait_recv()
        share(weights_ref.at[source(d), core, near])
    for d in others_y:
        for e in others_x:
            spread[(d - 1) * (CHIPS_X - 1) + e - 1].wait_recv()
            x = lax.rem(at.x + CHIPS_X - e, CHIPS_X)
            share(weights_ref.at[source(d), core, far, lanes(x)])
    for copy in loads[CELLS_MAX:]:
        copy.wait()
    for copy in shared:
        copy.wait_recv()
    for copy in shared + split + direct + spread:
        copy.wait_send()


def gather_weights(weight, three, five, seven, features, sections):
    cells, channels = weight.shape[0], weight.shape[-1]
    weight = weight.reshape(cells, CORES, channels // CORES, channels)
    vmem = pl.BlockSpec(memory_space=pltpu.VMEM)
    anywhere = pl.BlockSpec(memory_space=pl.ANY)
    dma = pltpu.SemaphoreType.DMA
    ys, xs = sections - 1, CHIPS_X - 1
    rows = cells * channels // CORES + TAP_ROWS
    return pl.pallas_call(
        functools.partial(gather_kernel, sections),
        out_shape=(
            jax.ShapeDtypeStruct((sections, CORES, rows, channels), weight.dtype),
            jax.ShapeDtypeStruct((IMAGES * AREA, channels), features.dtype),
        ),
        in_specs=[anywhere, vmem, vmem, vmem, vmem],
        out_specs=(vmem, vmem),
        scratch_shapes=[
            pltpu.VMEM((CORES, TAP_ROWS, channels), jnp.float32),
            dma((ys,)),
            dma((ys,)),
            dma((ys,)),
            dma((ys,)),
            dma((ys * xs,)),
            dma((ys * xs,)),
            dma((2 * ys + ys * xs,)),
            dma((2 * ys + ys * xs,)),
            dma((CORES * cells,)),
        ],
        compiler_params=pltpu.CompilerParams(
            collective_id=0, has_side_effects=True, vmem_limit_bytes=24 * 1024 * 1024
        ),
        name="gather",
    )(weight, three, five, seven, features)


def reduce_kernel(
    sections,
    grad_ref,
    out_ref,
    pair_ref,
    part_ref,
    in_a1_ref,
    in_b1_ref,
    mid_a_ref,
    mid_b_ref,
    in_a2_ref,
    in_b2_ref,
    small_ref,
    in_z_ref,
    line_ref,
    plane_ref,
    pair_send,
    pair_recv,
    a1_send,
    a1_recv,
    b1_send,
    b1_recv,
    a2_send,
    a2_recv,
    b2_send,
    b2_recv,
    z_send,
    z_recv,
    line_send,
    line_recv,
    plane_send,
    plane_recv,
    core_send,
    core_recv,
    column_sem,
    half_sem,
):
    at = Place(sections)
    others_y = range(1, sections)
    others_x = range(1, CHIPS_X)
    others_z = range(1, CHIPS_Z)
    partner = at.device(core=1)
    at.signal(
        [partner]
        + [at.device(pipe=d) for d in others_y]
        + [at.device(x=d) for d in others_x]
        + [at.device(z=d) for d in others_z]
    )
    at.wait(1 + len(others_y) + len(others_x) + len(others_z))
    f32 = jnp.float32
    bf16 = jnp.bfloat16
    order = (2, 1, 3, 0)
    other_core = lax.rem(at.core + 1, CORES)
    all_z = pl.ds(0, CHIPS_Z)
    first_z = pl.ds(0, FIRST_Z)
    last_z = pl.ds(FIRST_Z, LAST_Z)
    last_all = pl.ds(0, LAST_Z)

    def lanes(x):
        return pl.ds(pl.multiple_of(x * LANES, LANES), LANES)

    def section_at(d):
        return lax.rem(at.pipe + d, sections)

    def stream(turn, start, size):
        rows = pl.ds(start, size)
        paired, a1, b1, a2, b2 = {}, {}, {}, {}, {}
        for k, d in enumerate(order):
            section = section_at(d)
            paired[d] = start_remote(
                grad_ref.at[section, other_core, all_z, rows],
                pair_ref.at[section, all_z, rows],
                pair_send,
                pair_recv,
                turn * sections + k,
                partner,
            )
        yield
        for d in order:
            section = section_at(d)
            paired[d].wait_recv()

            def add_pair(z, _, section=section):
                total = grad_ref[section, at.core, z, rows].astype(f32)
                total = total + pair_ref[section, z, rows].astype(f32)
                part_ref[section, z, rows] = total.astype(bf16)
                return 0

            lax.fori_loop(0, CHIPS_Z, add_pair, 0)
            if d:
                a1[d] = start_remote(
                    part_ref.at[section, first_z, rows],
                    in_a1_ref.at[d - 1, first_z, rows],
                    a1_send,
                    a1_recv,
                    turn * len(others_y) + d - 1,
                    at.device(pipe=d),
                )
            for e in others_x:
                b1[d, e] = start_remote(
                    part_ref.at[section, last_z, rows, lanes(lax.rem(at.x + e, CHIPS_X))],
                    in_b1_ref.at[e - 1, section, last_all, rows],
                    b1_send,
                    b1_recv,
                    (turn * sections + d) * len(others_x) + e - 1,
                    at.device(x=e),
                )
        yield
        for d in order:
            section = section_at(d)
            for e in others_x:
                b1[d, e].wait_recv()

            def add_b1(z, _, section=section):
                total = part_ref[section, FIRST_Z + z, rows, lanes(at.x)].astype(f32)
                for e in others_x:
                    total = total + in_b1_ref[e - 1, section, z, rows].astype(f32)
                mid_b_ref[section, z, rows] = total.astype(bf16)
                return 0

            lax.fori_loop(0, LAST_Z, add_b1, 0)
            if d:
                b2[d] = start_remote(
                    mid_b_ref.at[section, last_all, rows],
                    in_b2_ref.at[d - 1, last_all, rows],
                    b2_send,
                    b2_recv,
                    turn * len(others_y) + d - 1,
                    at.device(pipe=d),
                )
        for d in others_y:
            a1[d].wait_recv()

        def add_a1(z, _):
            total = part_ref[at.pipe, z, rows].astype(f32)
            for d in others_y:
                total = total + in_a1_ref[d - 1, z, rows].astype(f32)
            mid_a_ref[z, rows] = total.astype(bf16)
            return 0

        lax.fori_loop(0, FIRST_Z, add_a1, 0)
        for e in others_x:
            a2[e] = start_remote(
                mid_a_ref.at[first_z, rows, lanes(lax.rem(at.x + e, CHIPS_X))],
                in_a2_ref.at[e - 1, first_z, rows],
                a2_send,
                a2_recv,
                turn * len(others_x) + e - 1,
                at.device(x=e),
            )
        yield
        for d in others_y:
            b2[d].wait_recv()
        for e in others_x:
            a2[e].wait_recv()

        def add_a2(z, _):
            total = mid_a_ref[z, rows, lanes(at.x)].astype(f32)
            for e in others_x:
                total = total + in_a2_ref[e - 1, z, rows].astype(f32)
            small_ref[z, rows] = total.astype(bf16)
            return 0

        def add_b2(z, _):
            total = mid_b_ref[at.pipe, z, rows].astype(f32)
            for d in others_y:
                total = total + in_b2_ref[d - 1, z, rows].astype(f32)
            small_ref[FIRST_Z + z, rows] = total.astype(bf16)
            return 0

        lax.fori_loop(0, FIRST_Z, add_a2, 0)
        lax.fori_loop(0, LAST_Z, add_b2, 0)
        to_z = [
            start_remote(
                small_ref.at[lax.rem(at.z + d, CHIPS_Z), rows],
                in_z_ref.at[d - 1, rows],
                z_send,
                z_recv,
                turn * len(others_z) + d - 1,
                at.device(z=d),
            )
            for d in others_z
        ]
        yield
        for copy in to_z:
            copy.wait_recv()
        total = small_ref[at.z, rows].astype(f32)
        for d in others_z:
            total = total + in_z_ref[d - 1, rows].astype(f32)
        line_ref[at.z, rows] = total.astype(bf16)
        piece = line_ref.at[at.z, rows]
        line = [
            start_remote(
                piece,
                piece,
                line_send,
                line_recv,
                turn * len(others_z) + d - 1,
                at.device(z=d),
            )
            for d in others_z
        ]
        yield
        for copy in line:
            copy.wait_recv()
        column = plane_ref.at[all_z, rows, lanes(at.x)]
        plane = [
            start_remote(
                line_ref.at[all_z, rows],
                column,
                plane_send,
                plane_recv,
                turn * len(others_x) + e - 1,
                at.device(x=e),
            )
            for e in others_x
        ]
        own_column = start_local(line_ref.at[all_z, rows], column, column_sem, turn)
        yield
        own_column.wait()
        for copy in plane:
            copy.wait_recv()
        half = out_ref.at[at.core, all_z, rows]
        last = start_remote(
            plane_ref.at[all_z, rows], half, core_send, core_recv, turn, partner
        )
        own_half = start_local(plane_ref.at[all_z, rows], half, half_sem, turn)
        yield
        own_half.wait()
        last.wait()
        for copies in (paired, a1, b1, a2, b2):
            for copy in copies.values():
                copy.wait_send()
        for copy in to_z + line + plane:
            copy.wait_send()

    running = [stream(turn, *span) for turn, span in enumerate(STREAMS)]
    for turn in TURNS:
        next(running[turn])
    for one in running:
        for _ in one:
            pass


def reduce_grads(grads, sections):
    rows, channels = grads.shape[2:]
    grads = grads.reshape(sections, CORES, CHIPS_Z, CHUNK, channels)
    dma = pltpu.SemaphoreType.DMA
    ys, xs, zs, turns = sections - 1, CHIPS_X - 1, CHIPS_Z - 1, len(STREAMS)

    def vmem(*shape):
        return pltpu.VMEM(shape, jnp.bfloat16)

    out = pl.pallas_call(
        functools.partial(reduce_kernel, sections),
        out_shape=jax.ShapeDtypeStruct((CORES, CHIPS_Z, CHUNK, channels), jnp.bfloat16),
        in_specs=[pl.BlockSpec(memory_space=pltpu.VMEM)],
        out_specs=pl.BlockSpec(memory_space=pl.ANY),
        scratch_shapes=[
            vmem(sections, CHIPS_Z, CHUNK, channels),
            vmem(sections, CHIPS_Z, CHUNK, channels),
            vmem(ys, FIRST_Z, CHUNK, channels),
            vmem(xs, sections, LAST_Z, CHUNK, LANES),
            vmem(FIRST_Z, CHUNK, channels),
            vmem(sections, LAST_Z, CHUNK, LANES),
            vmem(xs, FIRST_Z, CHUNK, LANES),
            vmem(ys, LAST_Z, CHUNK, LANES),
            vmem(CHIPS_Z, CHUNK, LANES),
            vmem(zs, CHUNK, LANES),
            vmem(CHIPS_Z, CHUNK, LANES),
            vmem(CHIPS_Z, CHUNK, channels),
        ]
        + [
            dma((turns * count,))
            for count in (sections, ys, sections * xs, xs, ys, zs, zs, xs, 1)
            for _ in ("send", "receive")
        ]
        + [dma((turns,)), dma((turns,))],
        compiler_params=pltpu.CompilerParams(
            collective_id=1, has_side_effects=True, vmem_limit_bytes=24 * 1024 * 1024
        ),
        name="reduce",
    )(grads)
    return out.reshape(CORES, rows, channels)


def own_taps(block, slot):
    size = 2 * slot + 3
    start = CELLS_MAX * block.shape[-1] // CORES + TAP_STARTS[slot]
    rows = block[TAP_HALVES[slot], start : start + size * size].astype(jnp.float32)
    return rows.reshape(1, size, size, block.shape[-1])


def shards(
    features,
    labels,
    micro_count,
    cells_per_section,
    point_weight,
    depth_three,
    depth_five,
    depth_seven,
    head_weight,
):
    sections = lax.axis_size("pipe")
    channels = point_weight.shape[-1]
    by_position = features.transpose(1, 2, 0, 3).reshape(-1, channels)
    weights, own = gather_weights(
        point_weight[0], depth_three[0], depth_five[0], depth_seven[0], by_position, sections
    )
    grads = run_cells(cells_per_section, labels, micro_count, own, weights, head_weight.T)
    block = reduce_grads(grads, sections)
    span = channels // CORES
    point_rows = CELLS_MAX * span
    loss_start = point_rows + TAP_ROWS
    total_loss = jnp.sum(block[0, loss_start : loss_start + 3].astype(jnp.float32))
    point_sum = block[:, :point_rows].reshape(CORES, CELLS_MAX, span, channels)
    point_sum = point_sum.transpose(1, 0, 2, 3).astype(jnp.float32)
    return (
        total_loss,
        point_sum.reshape(1, CELLS_MAX, channels, channels),
        own_taps(block, 0),
        own_taps(block, 1),
        own_taps(block, 2),
    )


def solution(mesh):
    return jax.shard_map(
        shards,
        mesh=mesh,
        in_specs=(
            P("dp", None, None, None),
            P("dp"),
            P("dp"),
            P(),
            P("pipe", None, None, None),
            P("pipe", None, None, None),
            P("pipe", None, None, None),
            P("pipe", None, None, None),
            P(),
        ),
        out_specs=(
            P(),
            P("pipe", None, None, None),
            P("pipe", None, None, None),
            P("pipe", None, None, None),
            P("pipe", None, None, None),
        ),
        check_vma=False,
    )
```

```python
import functools

import jax
import jax.numpy as jnp
import ml_dtypes
import numpy as np
from jax import lax
from jax.experimental import pallas as pl
from jax.experimental.pallas import tpu as pltpu
from jax.sharding import PartitionSpec as P

SIDE = 12
AREA = SIDE * SIDE
MB_IMG = 2
CELLS_MAX = 3
TAPS = 7
TAP_ROWS = 64
LOGIT_CAP = 30.0
CYCLE = SIDE + TAPS // 2
HALF = 120
IMAGES = 4
GROUP = 16
CHIPS_X = 4
CHIPS_Z = 8
CORES = 2
LANES = 128
MESH = pl.DeviceIdType.MESH
TAP_HALVES = (0, 0, 1)
TAP_STARTS = (0, 16, 0)
TAP_SPANS = (16, 32, 64)
CHUNK = 112
STREAMS = ((0, 32), (32, 32), (64, 32), (96, 16))
X_FIRST = (2,)
FIRST_Z = 4
LAST_Z = CHIPS_Z - FIRST_Z
VIA_Z = 2
HALF_ROWS = CHIPS_Z * CHUNK
LOSS_ROWS = 16
WEIGHT_A = 320
CELLS_MB = 32


def transform_tables():
    slots = [(0, 0)]
    seen = {(0, 0)}
    for u in range(CYCLE):
        for v in range(CYCLE):
            if (u, v) in seen:
                continue
            seen.add((u, v))
            seen.add(((-u) % CYCLE, (-v) % CYCLE))
            slots.append((u, v))
    count = len(slots)
    waves = np.array(slots, np.float64)
    sites = np.array([(i, j) for i in range(SIDE) for j in range(SIDE)], np.float64)
    weight = np.where((waves == 0).all(1), 1.0, 2.0)[:, None] / CYCLE**2
    site_angle = 2 * np.pi * ((waves @ sites.T) % CYCLE) / CYCLE
    into = np.zeros((2 * HALF, AREA))
    into[:count] = np.cos(site_angle)
    into[HALF : HALF + count] = -np.sin(site_angle)
    back = np.zeros((AREA, 2 * HALF))
    back[:, :count] = (np.cos(site_angle) * weight).T
    back[:, HALF : HALF + count] = -(np.sin(site_angle) * weight).T
    tap_into = np.zeros((CELLS_MAX, 2 * HALF, TAP_ROWS))
    tap_back = np.zeros((CELLS_MAX, TAP_ROWS, 2 * HALF))
    for slot in range(CELLS_MAX):
        size = 2 * slot + 3
        reach = size // 2
        shifts = np.array(
            [(u - reach, v - reach) for u in range(size) for v in range(size)], np.float64
        )
        taps = slice(TAP_STARTS[slot], TAP_STARTS[slot] + size * size)
        tap_angle = 2 * np.pi * ((waves @ shifts.T) % CYCLE) / CYCLE
        tap_into[slot, :count, taps] = np.cos(tap_angle)
        tap_into[slot, HALF : HALF + count, taps] = np.sin(tap_angle)
        tap_back[slot, taps, :count] = (np.cos(tap_angle) * weight).T
        tap_back[slot, taps, HALF : HALF + count] = -(np.sin(tap_angle) * weight).T
    return [pair_of(into)[0], pair_of(back)[0], pair_of(tap_into), pair_of(tap_back)]


def pair_of(table):
    high = table.astype(ml_dtypes.bfloat16)
    low = (table - high.astype(np.float64)).astype(ml_dtypes.bfloat16)
    return np.stack([high, low])


def mul(a, b):
    return jnp.dot(a, b, preferred_element_type=jnp.float32)


def halves(values):
    high = values.astype(jnp.bfloat16)
    low = (values - high.astype(jnp.float32)).astype(jnp.bfloat16)
    return high, low


def three_part(left, right_high, right_low, dim):
    rows = left.shape[0]
    dims = (((1,), (dim,)), ((), ()))
    high, low = halves(left)
    both = lax.dot_general(
        jnp.concatenate([high, low], axis=0), right_high, dims, preferred_element_type=jnp.float32
    )
    rest = lax.dot_general(high, right_low, dims, preferred_element_type=jnp.float32)
    return both[:rows] + (both[rows:] + rest)


def cells_kernel(
    cells_ref,
    labels_ref,
    live_count_ref,
    features_ref,
    weight_ref,
    head_ref,
    into_ref,
    back_ref,
    tap_into_ref,
    tap_back_ref,
    grad_ref,
    order_ref,
    acts_ref,
    deep_ref,
    wave_ref,
    cot_ref,
    deep_cot_ref,
    total_ref,
):
    sections, channels = weight_ref.shape[0], weight_ref.shape[-1]
    span = channels // CORES
    point_rows = CELLS_MAX * span
    loss_start = point_rows + TAP_ROWS
    pipe = lax.axis_index("pipe")
    count = jnp.int32(0)
    for section in range(sections):
        held = cells_ref[section]
        for slot in range(CELLS_MAX):
            order_ref[count + slot] = section * CELLS_MAX + slot
        for slot in range(1, CELLS_MAX):

            @pl.when(slot >= held)
            def _(section=section, slot=slot):
                for core in range(CORES):
                    grad_ref[section, core, slot * span : (slot + 1) * span] = jnp.zeros(
                        (span, channels), jnp.bfloat16
                    )
                row = point_rows + TAP_STARTS[slot]
                grad_ref[section, TAP_HALVES[slot], row : row + TAP_SPANS[slot]] = jnp.zeros(
                    (TAP_SPANS[slot], channels), jnp.bfloat16
                )

        count = count + held

    acts_ref[0] = features_ref[...]

    def rows_of(image):
        return pl.ds(image * AREA, AREA)

    def lanes_of(image):
        return slice(image * channels, (image + 1) * channels)

    def abreast(ref):
        return jnp.concatenate([ref[rows_of(image)] for image in range(IMAGES)], axis=1)

    def forward(step, _):
        cell = order_ref[step]
        section = lax.div(cell, CELLS_MAX)
        slot = lax.rem(cell, CELLS_MAX)
        taps = weight_ref[section, lax.div(slot, CELLS_MAX - 1), point_rows:]
        wave = mul(tap_into_ref[0, slot], taps) + mul(tap_into_ref[1, slot], taps)
        wave_ref[step] = wave
        wave_re, wave_im = wave[:HALF], wave[HALF:]
        seen = mul(into_ref[...], jnp.maximum(abreast(acts_ref.at[step]), 0))
        mixed = []
        for image in range(IMAGES):
            lanes = lanes_of(image)
            seen_re, seen_im = seen[:HALF, lanes], seen[HALF:, lanes]
            mixed.append(
                jnp.concatenate(
                    [
                        seen_re * wave_re - seen_im * wave_im,
                        seen_re * wave_im + seen_im * wave_re,
                    ],
                    axis=0,
                ).astype(jnp.bfloat16)
            )
        deep = mul(back_ref[...], jnp.concatenate(mixed, axis=1)).astype(jnp.bfloat16)
        for image in range(IMAGES):
            deep_ref[step, rows_of(image)] = deep[:, lanes_of(image)]
        rows = pl.ds(pl.multiple_of(slot * span, span), span)
        mixed = mul(deep_ref[step, :, :span], weight_ref[section, 0, rows]) + mul(
            deep_ref[step, :, span:], weight_ref[section, 1, rows]
        )
        acts_ref[step + 1] = (acts_ref[step].astype(jnp.float32) + mixed).astype(jnp.bfloat16)
        return 0

    lax.fori_loop(0, count, forward, 0)

    means = [
        jnp.sum(acts_ref[count, rows_of(image)].astype(jnp.float32), axis=0, keepdims=True)
        for image in range(IMAGES)
    ]
    spare = jnp.zeros((8 - IMAGES, channels), jnp.float32)
    pooled = jnp.concatenate(means + [spare], axis=0) / AREA
    head = head_ref[...]
    head_high, head_low = halves(head)
    scores = three_part(pooled, head_high, head_low, 1)
    capped = jnp.tanh(scores / LOGIT_CAP)
    logits = LOGIT_CAP * capped
    exponent = jnp.exp(logits)
    total = jnp.sum(exponent, axis=1, keepdims=True)
    classes = lax.broadcasted_iota(jnp.int32, logits.shape, 1)
    image_row = lax.broadcasted_iota(jnp.int32, (8, 1), 0)
    targets = jnp.zeros((8, 1), jnp.int32)
    live = jnp.zeros((8, 1), jnp.float32)
    for image in range(IMAGES):
        place = pipe + sections * image
        is_live = (lax.div(place, MB_IMG) < live_count_ref[0]).astype(jnp.float32)
        targets = jnp.where(image_row == image, labels_ref[place], targets)
        live = jnp.where(image_row == image, is_live, live)
    onehot = (classes == targets).astype(jnp.float32)
    row_loss = (jnp.log(total) - jnp.sum(logits * onehot, axis=1, keepdims=True)) * live
    score_cot = (exponent / total - onehot) * live * (1.0 - capped * capped)
    pooled_cot = three_part(score_cot, head_high, head_low, 0)
    spread = pooled_cot / AREA
    for image in range(IMAGES):
        cot_ref[rows_of(image)] = jnp.broadcast_to(
            spread[image : image + 1], (AREA, channels)
        ).astype(jnp.bfloat16)

    loss = jnp.broadcast_to(jnp.sum(row_loss, axis=0, keepdims=True), (LOSS_ROWS, channels))
    high = loss.astype(jnp.bfloat16).astype(jnp.float32)
    middle = (loss - high).astype(jnp.bfloat16).astype(jnp.float32)
    low = loss - high - middle
    device = lax.axis_index("dp") * sections + pipe
    part = lax.broadcasted_iota(jnp.int32, loss.shape, 0)
    own = lax.broadcasted_iota(jnp.int32, loss.shape, 1) == device
    parts = jnp.where(part == 0, high, jnp.where(part == 1, middle, low))
    parts = jnp.where(own & (part < 3), parts, 0.0).astype(jnp.bfloat16)
    for section in range(sections):
        for core in range(CORES):
            grad_ref[section, core, loss_start : loss_start + LOSS_ROWS] = parts
            grad_ref[section, core, loss_start + LOSS_ROWS :] = jnp.zeros(
                (HALF_ROWS - loss_start - LOSS_ROWS, channels), jnp.bfloat16
            )

    def backward(turn, _):
        step = count - 1 - turn
        cell = order_ref[step]
        section = lax.div(cell, CELLS_MAX)
        slot = lax.rem(cell, CELLS_MAX)
        rows = pl.ds(pl.multiple_of(slot * span, span), span)
        cot = cot_ref[...]
        for core in range(CORES):
            columns = slice(core * span, (core + 1) * span)
            grad_ref[section, core, rows] = lax.dot_general(
                deep_ref[step, :, columns],
                cot,
                (((0,), (0,)), ((), ())),
                preferred_element_type=jnp.float32,
            ).astype(jnp.bfloat16)
            deep_cot_ref[:, columns] = lax.dot_general(
                cot,
                weight_ref[section, core, rows],
                (((1,), (1,)), ((), ())),
                preferred_element_type=jnp.float32,
            ).astype(jnp.bfloat16)
        wave_re, wave_im = wave_ref[step, :HALF], wave_ref[step, HALF:]
        acts = abreast(acts_ref.at[step])
        seen = mul(into_ref[...], jnp.maximum(acts, 0))
        sent = mul(into_ref[...], abreast(deep_cot_ref))
        mixed = []
        for image in range(IMAGES):
            lanes = lanes_of(image)
            seen_re, seen_im = seen[:HALF, lanes], seen[HALF:, lanes]
            sent_re, sent_im = sent[:HALF, lanes], sent[HALF:, lanes]
            part_re = seen_re * sent_re + seen_im * sent_im
            part_im = seen_im * sent_re - seen_re * sent_im
            if image == 0:
                total_ref[:HALF] = part_re
                total_ref[HALF:] = part_im
            else:
                total_ref[:HALF] += part_re
                total_ref[HALF:] += part_im
            mixed.append(
                jnp.concatenate(
                    [
                        sent_re * wave_re + sent_im * wave_im,
                        sent_im * wave_re - sent_re * wave_im,
                    ],
                    axis=0,
                ).astype(jnp.bfloat16)
            )
        rect_cot = mul(back_ref[...], jnp.concatenate(mixed, axis=1))
        for image in range(IMAGES):
            lanes = lanes_of(image)
            passed = jnp.where(acts[:, lanes].astype(jnp.float32) > 0, rect_cot[:, lanes], 0.0)
            cot_ref[rows_of(image)] = (
                cot_ref[rows_of(image)].astype(jnp.float32) + passed
            ).astype(jnp.bfloat16)
        high, low = halves(total_ref[...])
        taps = (
            mul(tap_back_ref[0, slot], high)
            + mul(tap_back_ref[0, slot], low)
            + mul(tap_back_ref[1, slot], high)
        ).astype(jnp.bfloat16)
        for kind in range(CELLS_MAX):

            @pl.when(slot == kind)
            def _(kind=kind):
                first, last = TAP_STARTS[kind], TAP_STARTS[kind] + TAP_SPANS[kind]
                grad_ref[section, TAP_HALVES[kind], point_rows + first : point_rows + last] = taps[
                    first:last
                ]

        return 0

    lax.fori_loop(0, count, backward, 0)


def run_cells(cells, labels, live_count, features, weights, head):
    sections, channels = weights.shape[0], weights.shape[-1]
    slots = sections * CELLS_MAX
    tables = [jnp.asarray(table) for table in transform_tables()]
    vmem = pl.BlockSpec(memory_space=pltpu.VMEM)
    smem = pl.BlockSpec(memory_space=pltpu.SMEM)
    rows = IMAGES * AREA
    return pl.pallas_call(
        cells_kernel,
        out_shape=jax.ShapeDtypeStruct((sections, CORES, HALF_ROWS, channels), jnp.bfloat16),
        in_specs=[smem] * 3 + [vmem] * 7,
        out_specs=vmem,
        scratch_shapes=[
            pltpu.SMEM((slots + CELLS_MAX,), jnp.int32),
            pltpu.VMEM((slots + 1, rows, channels), jnp.bfloat16),
            pltpu.VMEM((slots, rows, channels), jnp.bfloat16),
            pltpu.VMEM((slots, 2 * HALF, channels), jnp.float32),
            pltpu.VMEM((rows, channels), jnp.bfloat16),
            pltpu.VMEM((rows, channels), jnp.bfloat16),
            pltpu.VMEM((2 * HALF, channels), jnp.float32),
        ],
        compiler_params=pltpu.CompilerParams(vmem_limit_bytes=CELLS_MB * 1024 * 1024),
        name="cells",
    )(cells, labels, live_count, features, weights, head, *tables)


class Place:
    def __init__(self, sections):
        self.sections = sections
        self.pipe = lax.axis_index("pipe")
        place = lax.axis_index("dp")
        self.core = lax.rem(place, CORES)
        self.z = lax.rem(lax.div(place, CORES), CHIPS_Z)
        self.x = lax.div(place, CORES * CHIPS_Z)

    def device(self, pipe=0, x=0, z=0, core=0):
        pipe = lax.rem(self.pipe + pipe, self.sections)
        x = lax.rem(self.x + x, CHIPS_X)
        z = lax.rem(self.z + z, CHIPS_Z)
        core = lax.rem(self.core + core, CORES)
        return (pipe, (x * CHIPS_Z + z) * CORES + core)

    def signal(self, partners):
        barrier = pltpu.get_barrier_semaphore()
        for partner in partners:
            pl.semaphore_signal(barrier, inc=1, device_id=partner, device_id_type=MESH)

    def wait(self, partners):
        pl.semaphore_wait(pltpu.get_barrier_semaphore(), partners)


def start_remote(source, target, send_sems, recv_sems, index, device):
    copy = pltpu.make_async_remote_copy(
        src_ref=source,
        dst_ref=target,
        send_sem=send_sems.at[index],
        recv_sem=recv_sems.at[index],
        device_id=device,
        device_id_type=MESH,
    )
    copy.start()
    return copy


def start_local(source, target, sems, index):
    copy = pltpu.make_async_copy(source, target, sems.at[index])
    copy.start()
    return copy


def gather_kernel(
    sections,
    weight_ref,
    three_ref,
    five_ref,
    seven_ref,
    features_ref,
    weights_ref,
    own_ref,
    taps_ref,
    direct_send,
    direct_recv,
    split_send,
    split_recv,
    spread_send,
    spread_recv,
    core_send,
    core_recv,
    weight_sem,
):
    at = Place(sections)
    others_y = range(1, sections)
    others_x = range(1, CHIPS_X)
    core = at.core
    channels = weights_ref.shape[-1]
    span = channels // CORES
    point_rows = CELLS_MAX * span
    at.signal(
        [at.device(pipe=d) for d in others_y]
        + [at.device(x=d) for d in others_x]
        + [at.device(core=1)]
    )
    loads = []
    for half in (core, lax.rem(core + 1, CORES)):
        for cell in range(CELLS_MAX):
            loads.append(
                start_local(
                    weight_ref.at[cell, half],
                    weights_ref.at[at.pipe, half, pl.ds(cell * span, span)],
                    weight_sem,
                    len(loads),
                )
            )
    taps_ref[...] = jnp.zeros_like(taps_ref)
    for slot, ref in enumerate((three_ref, five_ref, seven_ref)):
        size = 2 * slot + 3
        for u in range(size):
            row = TAP_STARTS[slot] + u * size
            taps_ref[TAP_HALVES[slot], row : row + size] = ref[u].astype(jnp.float32)
    for half in range(CORES):
        weights_ref[at.pipe, half, point_rows:] = taps_ref[half].astype(jnp.bfloat16)
    for copy in loads[:CELLS_MAX]:
        copy.wait()
    at.wait((sections - 1) + (CHIPS_X - 1) + 1)

    near = pl.ds(0, WEIGHT_A)
    far = pl.ds(WEIGHT_A, point_rows + TAP_ROWS - WEIGHT_A)

    def lanes(x):
        return pl.ds(pl.multiple_of(x * LANES, LANES), LANES)

    split, direct = [], []
    for d in others_y:
        piece = weights_ref.at[at.pipe, core, far, lanes(at.x)]
        split.append(
            start_remote(piece, piece, split_send, split_recv, d - 1, at.device(pipe=d))
        )
    for d in others_y:
        piece = weights_ref.at[at.pipe, core, near]
        direct.append(
            start_remote(piece, piece, direct_send, direct_recv, d - 1, at.device(pipe=d))
        )
    per_replica = features_ref.shape[0] // AREA
    group = (GROUP * IMAGES, GROUP * per_replica)
    row = lax.broadcasted_iota(jnp.int32, group, 0)
    column = lax.broadcasted_iota(jnp.int32, group, 1)
    wanted = lax.rem(row, GROUP) * per_replica + lax.div(row, GROUP) * sections + at.pipe
    pick = (column == wanted).astype(jnp.float32).astype(jnp.bfloat16)
    for g in range(AREA // GROUP):
        picked = mul(pick, features_ref[g * group[1] : (g + 1) * group[1]]).astype(jnp.bfloat16)
        for k in range(IMAGES):
            row = k * AREA + g * GROUP
            own_ref[row : row + GROUP] = picked[k * GROUP : (k + 1) * GROUP]

    spread, shared = [], []

    def share(piece):
        k = len(shared)
        shared.append(start_remote(piece, piece, core_send, core_recv, k, at.device(core=1)))

    def source(d):
        return lax.rem(at.pipe + sections - d, sections)

    for d in others_y:
        split[d - 1].wait_recv()
        piece = weights_ref.at[source(d), core, far, lanes(at.x)]
        for e in others_x:
            k = (d - 1) * (CHIPS_X - 1) + e - 1
            spread.append(
                start_remote(piece, piece, spread_send, spread_recv, k, at.device(x=e))
            )
        share(piece)
    for d in others_y:
        direct[d - 1].wait_recv()
        share(weights_ref.at[source(d), core, near])
    for d in others_y:
        for e in others_x:
            spread[(d - 1) * (CHIPS_X - 1) + e - 1].wait_recv()
            x = lax.rem(at.x + CHIPS_X - e, CHIPS_X)
            share(weights_ref.at[source(d), core, far, lanes(x)])
    for copy in loads[CELLS_MAX:]:
        copy.wait()
    for copy in shared:
        copy.wait_recv()
    for copy in shared + split + direct + spread:
        copy.wait_send()


def gather_weights(weight, three, five, seven, features, sections):
    cells, channels = weight.shape[0], weight.shape[-1]
    weight = weight.reshape(cells, CORES, channels // CORES, channels)
    vmem = pl.BlockSpec(memory_space=pltpu.VMEM)
    anywhere = pl.BlockSpec(memory_space=pl.ANY)
    dma = pltpu.SemaphoreType.DMA
    ys, xs = sections - 1, CHIPS_X - 1
    rows = cells * channels // CORES + TAP_ROWS
    return pl.pallas_call(
        functools.partial(gather_kernel, sections),
        out_shape=(
            jax.ShapeDtypeStruct((sections, CORES, rows, channels), weight.dtype),
            jax.ShapeDtypeStruct((IMAGES * AREA, channels), features.dtype),
        ),
        in_specs=[anywhere, vmem, vmem, vmem, vmem],
        out_specs=(vmem, vmem),
        scratch_shapes=[
            pltpu.VMEM((CORES, TAP_ROWS, channels), jnp.float32),
            dma((ys,)),
            dma((ys,)),
            dma((ys,)),
            dma((ys,)),
            dma((ys * xs,)),
            dma((ys * xs,)),
            dma((2 * ys + ys * xs,)),
            dma((2 * ys + ys * xs,)),
            dma((CORES * cells,)),
        ],
        compiler_params=pltpu.CompilerParams(
            collective_id=0, has_side_effects=True, vmem_limit_bytes=24 * 1024 * 1024
        ),
        name="gather",
    )(weight, three, five, seven, features)


def reduce_kernel(
    sections,
    grad_ref,
    out_ref,
    pair_ref,
    part_ref,
    via_a_ref,
    via_b_ref,
    in_a1_ref,
    in_b1_ref,
    mid_a_ref,
    mid_b_ref,
    in_a2_ref,
    in_b2_ref,
    small_ref,
    in_z_ref,
    line_ref,
    plane_ref,
    pair_send,
    pair_recv,
    via_a_send,
    via_a_recv,
    via_b_send,
    via_b_recv,
    a1_send,
    a1_recv,
    b1_send,
    b1_recv,
    a2_send,
    a2_recv,
    b2_send,
    b2_recv,
    z_send,
    z_recv,
    line_send,
    line_recv,
    plane_send,
    plane_recv,
    core_send,
    core_recv,
    column_sem,
    half_sem,
):
    at = Place(sections)
    others_y = range(1, sections)
    others_x = range(1, CHIPS_X)
    others_z = range(1, CHIPS_Z)
    partner = at.device(core=1)
    at.signal(
        [partner]
        + [at.device(pipe=d) for d in others_y]
        + [at.device(x=d) for d in others_x]
        + [at.device(z=d) for d in others_z]
    )
    at.wait(1 + len(others_y) + len(others_x) + len(others_z))
    f32 = jnp.float32
    bf16 = jnp.bfloat16
    order = (2, 1, 3, 0)
    other_core = lax.rem(at.core + 1, CORES)
    all_z = pl.ds(0, CHIPS_Z)
    first_z = pl.ds(0, FIRST_Z)
    last_z = pl.ds(FIRST_Z, LAST_Z)
    last_all = pl.ds(0, LAST_Z)
    via_all = pl.ds(0, VIA_Z)
    sides = (1, 3)

    def lanes(x):
        return pl.ds(pl.multiple_of(x * LANES, LANES), LANES)

    def section_at(d):
        return lax.rem(at.pipe + d, sections)

    def stream(turn, start, size):
        rows = pl.ds(start, size)
        paired, via_a, via_b, a1, b1, a2, b2 = {}, {}, {}, {}, {}, {}, {}
        for k, d in enumerate(order):
            section = section_at(d)
            paired[d] = start_remote(
                grad_ref.at[section, other_core, all_z, rows],
                pair_ref.at[section, all_z, rows],
                pair_send,
                pair_recv,
                turn * sections + k,
                partner,
            )
        yield
        for d in order:
            section = section_at(d)
            paired[d].wait_recv()

            def add_pair(z, _, section=section):
                total = grad_ref[section, at.core, z, rows].astype(f32)
                total = total + pair_ref[section, z, rows].astype(f32)
                part_ref[section, z, rows] = total.astype(bf16)
                return 0

            lax.fori_loop(0, CHIPS_Z, add_pair, 0)
            for n, side in enumerate(sides):
                if d == 2:
                    via_a[side] = start_remote(
                        part_ref.at[section, pl.ds(n * VIA_Z, VIA_Z), rows],
                        via_a_ref.at[n, via_all, rows],
                        via_a_send,
                        via_a_recv,
                        turn * len(sides) + n,
                        at.device(pipe=side),
                    )
                via_b[d, side] = start_remote(
                    part_ref.at[
                        section,
                        pl.ds(FIRST_Z + n * VIA_Z, VIA_Z),
                        rows,
                        lanes(lax.rem(at.x + 2, CHIPS_X)),
                    ],
                    via_b_ref.at[n, section, via_all, rows],
                    via_b_send,
                    via_b_recv,
                    (turn * sections + d) * len(sides) + n,
                    at.device(x=side),
                )
        yield
        for n, side in enumerate(sides):
            section = section_at(side)
            via_a[side].wait_recv()

            def add_via_a(z, _, section=section, n=n):
                total = part_ref[section, n * VIA_Z + z, rows].astype(f32)
                total = total + via_a_ref[n, z, rows].astype(f32)
                part_ref[section, n * VIA_Z + z, rows] = total.astype(bf16)
                return 0

            lax.fori_loop(0, VIA_Z, add_via_a, 0)
            a1[side] = start_remote(
                part_ref.at[section, first_z, rows],
                in_a1_ref.at[n, first_z, rows],
                a1_send,
                a1_recv,
                turn * len(sides) + n,
                at.device(pipe=side),
            )
        for d in order:
            section = section_at(d)
            for n, side in enumerate(sides):
                via_b[d, side].wait_recv()
                place = lanes(lax.rem(at.x + side, CHIPS_X))

                def add_via_b(z, _, section=section, n=n, place=place):
                    row = FIRST_Z + n * VIA_Z + z
                    total = part_ref[section, row, rows, place].astype(f32)
                    total = total + via_b_ref[n, section, z, rows].astype(f32)
                    part_ref[section, row, rows, place] = total.astype(bf16)
                    return 0

                lax.fori_loop(0, VIA_Z, add_via_b, 0)
                b1[d, side] = start_remote(
                    part_ref.at[section, last_z, rows, place],
                    in_b1_ref.at[n, section, last_all, rows],
                    b1_send,
                    b1_recv,
                    (turn * sections + d) * len(sides) + n,
                    at.device(x=side),
                )
        yield
        for d in order:
            section = section_at(d)
            for side in sides:
                b1[d, side].wait_recv()

            def add_b1(z, _, section=section):
                total = part_ref[section, FIRST_Z + z, rows, lanes(at.x)].astype(f32)
                for n in range(len(sides)):
                    total = total + in_b1_ref[n, section, z, rows].astype(f32)
                mid_b_ref[section, z, rows] = total.astype(bf16)
                return 0

            lax.fori_loop(0, LAST_Z, add_b1, 0)
            if d:
                b2[d] = start_remote(
                    mid_b_ref.at[section, last_all, rows],
                    in_b2_ref.at[d - 1, last_all, rows],
                    b2_send,
                    b2_recv,
                    turn * len(others_y) + d - 1,
                    at.device(pipe=d),
                )
        for side in sides:
            a1[side].wait_recv()

        def add_a1(z, _):
            total = part_ref[at.pipe, z, rows].astype(f32)
            for n in range(len(sides)):
                total = total + in_a1_ref[n, z, rows].astype(f32)
            mid_a_ref[z, rows] = total.astype(bf16)
            return 0

        lax.fori_loop(0, FIRST_Z, add_a1, 0)
        for e in others_x:
            a2[e] = start_remote(
                mid_a_ref.at[first_z, rows, lanes(lax.rem(at.x + e, CHIPS_X))],
                in_a2_ref.at[e - 1, first_z, rows],
                a2_send,
                a2_recv,
                turn * len(others_x) + e - 1,
                at.device(x=e),
            )
        yield
        for d in others_y:
            b2[d].wait_recv()
        for e in others_x:
            a2[e].wait_recv()

        def add_a2(z, _):
            total = mid_a_ref[z, rows, lanes(at.x)].astype(f32)
            for e in others_x:
                total = total + in_a2_ref[e - 1, z, rows].astype(f32)
            small_ref[z, rows] = total.astype(bf16)
            return 0

        def add_b2(z, _):
            total = mid_b_ref[at.pipe, z, rows].astype(f32)
            for d in others_y:
                total = total + in_b2_ref[d - 1, z, rows].astype(f32)
            small_ref[FIRST_Z + z, rows] = total.astype(bf16)
            return 0

        lax.fori_loop(0, FIRST_Z, add_a2, 0)
        lax.fori_loop(0, LAST_Z, add_b2, 0)
        to_z = [
            start_remote(
                small_ref.at[lax.rem(at.z + d, CHIPS_Z), rows],
                in_z_ref.at[d - 1, rows],
                z_send,
                z_recv,
                turn * len(others_z) + d - 1,
                at.device(z=d),
            )
            for d in others_z
        ]
        yield
        for copy in to_z:
            copy.wait_recv()
        total = small_ref[at.z, rows].astype(f32)
        for d in others_z:
            total = total + in_z_ref[d - 1, rows].astype(f32)
        if turn in X_FIRST:
            plane_ref[at.z, rows, lanes(at.x)] = total.astype(bf16)
            piece = plane_ref.at[at.z, rows, lanes(at.x)]
            plane = [
                start_remote(
                    piece,
                    piece,
                    plane_send,
                    plane_recv,
                    turn * len(others_x) + e - 1,
                    at.device(x=e),
                )
                for e in others_x
            ]
            yield
            for copy in plane:
                copy.wait_recv()
            piece = plane_ref.at[at.z, rows]
        else:
            line_ref[at.z, rows] = total.astype(bf16)
            piece = line_ref.at[at.z, rows]
        line = [
            start_remote(
                piece,
                piece,
                line_send,
                line_recv,
                turn * len(others_z) + d - 1,
                at.device(z=d),
            )
            for d in others_z
        ]
        yield
        for copy in line:
            copy.wait_recv()
        if turn not in X_FIRST:
            column = plane_ref.at[all_z, rows, lanes(at.x)]
            plane = [
                start_remote(
                    line_ref.at[all_z, rows],
                    column,
                    plane_send,
                    plane_recv,
                    turn * len(others_x) + e - 1,
                    at.device(x=e),
                )
                for e in others_x
            ]
            own_column = start_local(line_ref.at[all_z, rows], column, column_sem, turn)
            yield
            own_column.wait()
            for copy in plane:
                copy.wait_recv()
        half = out_ref.at[at.core, all_z, rows]
        last = start_remote(
            plane_ref.at[all_z, rows], half, core_send, core_recv, turn, partner
        )
        own_half = start_local(plane_ref.at[all_z, rows], half, half_sem, turn)
        yield
        own_half.wait()
        last.wait()
        for copies in (paired, via_a, via_b, a1, b1, a2, b2):
            for copy in copies.values():
                copy.wait_send()
        for copy in to_z + line + plane:
            copy.wait_send()

    running = [stream(turn, *span) for turn, span in enumerate(STREAMS)]
    while running:
        running = [one for one in running if next(one, running) is None]


def reduce_grads(grads, sections):
    rows, channels = grads.shape[2:]
    grads = grads.reshape(sections, CORES, CHIPS_Z, CHUNK, channels)
    dma = pltpu.SemaphoreType.DMA
    ys, xs, zs, turns = sections - 1, CHIPS_X - 1, CHIPS_Z - 1, len(STREAMS)

    def vmem(*shape):
        return pltpu.VMEM(shape, jnp.bfloat16)

    out = pl.pallas_call(
        functools.partial(reduce_kernel, sections),
        out_shape=jax.ShapeDtypeStruct((CORES, CHIPS_Z, CHUNK, channels), jnp.bfloat16),
        in_specs=[pl.BlockSpec(memory_space=pltpu.VMEM)],
        out_specs=pl.BlockSpec(memory_space=pl.ANY),
        scratch_shapes=[
            vmem(sections, CHIPS_Z, CHUNK, channels),
            vmem(sections, CHIPS_Z, CHUNK, channels),
            vmem(2, VIA_Z, CHUNK, channels),
            vmem(2, sections, VIA_Z, CHUNK, LANES),
            vmem(2, FIRST_Z, CHUNK, channels),
            vmem(2, sections, LAST_Z, CHUNK, LANES),
            vmem(FIRST_Z, CHUNK, channels),
            vmem(sections, LAST_Z, CHUNK, LANES),
            vmem(xs, FIRST_Z, CHUNK, LANES),
            vmem(ys, LAST_Z, CHUNK, LANES),
            vmem(CHIPS_Z, CHUNK, LANES),
            vmem(zs, CHUNK, LANES),
            vmem(CHIPS_Z, CHUNK, LANES),
            vmem(CHIPS_Z, CHUNK, channels),
        ]
        + [
            dma((turns * count,))
            for count in (sections, 2, 2 * sections, 2, 2 * sections, xs, ys, zs, zs, xs, 1)
            for _ in ("send", "receive")
        ]
        + [dma((turns,)), dma((turns,))],
        compiler_params=pltpu.CompilerParams(
            collective_id=1, has_side_effects=True, vmem_limit_bytes=24 * 1024 * 1024
        ),
        name="reduce",
    )(grads)
    return out.reshape(CORES, rows, channels)


def own_taps(block, slot):
    size = 2 * slot + 3
    start = CELLS_MAX * block.shape[-1] // CORES + TAP_STARTS[slot]
    rows = block[TAP_HALVES[slot], start : start + size * size].astype(jnp.float32)
    return rows.reshape(1, size, size, block.shape[-1])


def shards(
    features,
    labels,
    micro_count,
    cells_per_section,
    point_weight,
    depth_three,
    depth_five,
    depth_seven,
    head_weight,
):
    sections = lax.axis_size("pipe")
    channels = point_weight.shape[-1]
    by_position = features.transpose(1, 2, 0, 3).reshape(-1, channels)
    weights, own = gather_weights(
        point_weight[0], depth_three[0], depth_five[0], depth_seven[0], by_position, sections
    )
    grads = run_cells(cells_per_section, labels, micro_count, own, weights, head_weight.T)
    block = reduce_grads(grads, sections)
    span = channels // CORES
    point_rows = CELLS_MAX * span
    loss_start = point_rows + TAP_ROWS
    total_loss = jnp.sum(block[0, loss_start : loss_start + 3].astype(jnp.float32))
    point_sum = block[:, :point_rows].reshape(CORES, CELLS_MAX, span, channels)
    point_sum = point_sum.transpose(1, 0, 2, 3).astype(jnp.float32)
    return (
        total_loss,
        point_sum.reshape(1, CELLS_MAX, channels, channels),
        own_taps(block, 0),
        own_taps(block, 1),
        own_taps(block, 2),
    )


def solution(mesh):
    return jax.shard_map(
        shards,
        mesh=mesh,
        in_specs=(
            P("dp", None, None, None),
            P("dp"),
            P("dp"),
            P(),
            P("pipe", None, None, None),
            P("pipe", None, None, None),
            P("pipe", None, None, None),
            P("pipe", None, None, None),
            P(),
        ),
        out_specs=(
            P(),
            P("pipe", None, None, None),
            P("pipe", None, None, None),
            P("pipe", None, None, None),
            P("pipe", None, None, None),
        ),
        check_vma=False,
    )
```

```python
import functools

import jax
import jax.numpy as jnp
import ml_dtypes
import numpy as np
from jax import lax
from jax.experimental import pallas as pl
from jax.experimental.pallas import tpu as pltpu
from jax.sharding import PartitionSpec as P

SIDE = 12
AREA = SIDE * SIDE
MB_IMG = 2
CELLS_MAX = 3
TAPS = 7
TAP_ROWS = 64
LOGIT_CAP = 30.0
CYCLE = SIDE + TAPS // 2
HALF = 120
IMAGES = 4
GROUP = 16
CHIPS_X = 4
CHIPS_Z = 8
CORES = 2
LANES = 128
MESH = pl.DeviceIdType.MESH
TAP_HALVES = (0, 0, 1)
TAP_STARTS = (0, 16, 0)
TAP_SPANS = (16, 32, 64)
CHUNK = 112
STREAMS = ((0, 32), (32, 32), (64, 32), (96, 16))
X_FIRST = (2,)
FIRST_Z = 4
LAST_Z = CHIPS_Z - FIRST_Z
VIA_Z = 2
HALF_ROWS = CHIPS_Z * CHUNK
LOSS_ROWS = 16
WEIGHT_A = 320
CELLS_MB = 32


def transform_tables():
    slots = [(0, 0)]
    seen = {(0, 0)}
    for u in range(CYCLE):
        for v in range(CYCLE):
            if (u, v) in seen:
                continue
            seen.add((u, v))
            seen.add(((-u) % CYCLE, (-v) % CYCLE))
            slots.append((u, v))
    count = len(slots)
    waves = np.array(slots, np.float64)
    sites = np.array([(i, j) for i in range(SIDE) for j in range(SIDE)], np.float64)
    weight = np.where((waves == 0).all(1), 1.0, 2.0)[:, None] / CYCLE**2
    site_angle = 2 * np.pi * ((waves @ sites.T) % CYCLE) / CYCLE
    into = np.zeros((2 * HALF, AREA))
    into[:count] = np.cos(site_angle)
    into[HALF : HALF + count] = -np.sin(site_angle)
    back = np.zeros((AREA, 2 * HALF))
    back[:, :count] = (np.cos(site_angle) * weight).T
    back[:, HALF : HALF + count] = -(np.sin(site_angle) * weight).T
    tap_into = np.zeros((CELLS_MAX, 2 * HALF, TAP_ROWS))
    tap_back = np.zeros((CELLS_MAX, TAP_ROWS, 2 * HALF))
    for slot in range(CELLS_MAX):
        size = 2 * slot + 3
        reach = size // 2
        shifts = np.array(
            [(u - reach, v - reach) for u in range(size) for v in range(size)], np.float64
        )
        taps = slice(TAP_STARTS[slot], TAP_STARTS[slot] + size * size)
        tap_angle = 2 * np.pi * ((waves @ shifts.T) % CYCLE) / CYCLE
        tap_into[slot, :count, taps] = np.cos(tap_angle)
        tap_into[slot, HALF : HALF + count, taps] = np.sin(tap_angle)
        tap_back[slot, taps, :count] = (np.cos(tap_angle) * weight).T
        tap_back[slot, taps, HALF : HALF + count] = -(np.sin(tap_angle) * weight).T
    return [pair_of(into)[0], pair_of(back)[0], pair_of(tap_into), pair_of(tap_back)]


def pair_of(table):
    high = table.astype(ml_dtypes.bfloat16)
    low = (table - high.astype(np.float64)).astype(ml_dtypes.bfloat16)
    return np.stack([high, low])


def mul(a, b):
    return jnp.dot(a, b, preferred_element_type=jnp.float32)


def halves(values):
    high = values.astype(jnp.bfloat16)
    low = (values - high.astype(jnp.float32)).astype(jnp.bfloat16)
    return high, low


def three_part(left, right_high, right_low, dim):
    rows = left.shape[0]
    dims = (((1,), (dim,)), ((), ()))
    high, low = halves(left)
    both = lax.dot_general(
        jnp.concatenate([high, low], axis=0), right_high, dims, preferred_element_type=jnp.float32
    )
    rest = lax.dot_general(high, right_low, dims, preferred_element_type=jnp.float32)
    return both[:rows] + (both[rows:] + rest)


def cells_kernel(
    cells_ref,
    labels_ref,
    live_count_ref,
    features_ref,
    weight_ref,
    head_ref,
    into_ref,
    back_ref,
    tap_into_ref,
    tap_back_ref,
    grad_ref,
    order_ref,
    acts_ref,
    deep_ref,
    wave_ref,
    cot_ref,
    deep_cot_ref,
    total_ref,
):
    sections, channels = weight_ref.shape[0], weight_ref.shape[-1]
    span = channels // CORES
    point_rows = CELLS_MAX * span
    loss_start = point_rows + TAP_ROWS
    pipe = lax.axis_index("pipe")
    count = jnp.int32(0)
    for section in range(sections):
        held = cells_ref[section]
        for slot in range(CELLS_MAX):
            order_ref[count + slot] = section * CELLS_MAX + slot
        for slot in range(1, CELLS_MAX):

            @pl.when(slot >= held)
            def _(section=section, slot=slot):
                for core in range(CORES):
                    grad_ref[section, core, slot * span : (slot + 1) * span] = jnp.zeros(
                        (span, channels), jnp.bfloat16
                    )
                row = point_rows + TAP_STARTS[slot]
                grad_ref[section, TAP_HALVES[slot], row : row + TAP_SPANS[slot]] = jnp.zeros(
                    (TAP_SPANS[slot], channels), jnp.bfloat16
                )

        count = count + held

    acts_ref[0] = features_ref[...]

    def rows_of(image):
        return pl.ds(image * AREA, AREA)

    def lanes_of(image):
        return slice(image * channels, (image + 1) * channels)

    def abreast(ref):
        return jnp.concatenate([ref[rows_of(image)] for image in range(IMAGES)], axis=1)

    def forward(step, _):
        cell = order_ref[step]
        section = lax.div(cell, CELLS_MAX)
        slot = lax.rem(cell, CELLS_MAX)
        taps = weight_ref[section, lax.div(slot, CELLS_MAX - 1), point_rows:]
        wave = mul(tap_into_ref[0, slot], taps) + mul(tap_into_ref[1, slot], taps)
        wave_ref[step] = wave
        wave_re, wave_im = wave[:HALF], wave[HALF:]
        seen = mul(into_ref[...], jnp.maximum(abreast(acts_ref.at[step]), 0))
        mixed = []
        for image in range(IMAGES):
            lanes = lanes_of(image)
            seen_re, seen_im = seen[:HALF, lanes], seen[HALF:, lanes]
            mixed.append(
                jnp.concatenate(
                    [
                        seen_re * wave_re - seen_im * wave_im,
                        seen_re * wave_im + seen_im * wave_re,
                    ],
                    axis=0,
                ).astype(jnp.bfloat16)
            )
        deep = mul(back_ref[...], jnp.concatenate(mixed, axis=1)).astype(jnp.bfloat16)
        for image in range(IMAGES):
            deep_ref[step, rows_of(image)] = deep[:, lanes_of(image)]
        rows = pl.ds(pl.multiple_of(slot * span, span), span)
        mixed = mul(deep_ref[step, :, :span], weight_ref[section, 0, rows]) + mul(
            deep_ref[step, :, span:], weight_ref[section, 1, rows]
        )
        acts_ref[step + 1] = (acts_ref[step].astype(jnp.float32) + mixed).astype(jnp.bfloat16)
        return 0

    lax.fori_loop(0, count, forward, 0)

    means = [
        jnp.sum(acts_ref[count, rows_of(image)].astype(jnp.float32), axis=0, keepdims=True)
        for image in range(IMAGES)
    ]
    spare = jnp.zeros((8 - IMAGES, channels), jnp.float32)
    pooled = jnp.concatenate(means + [spare], axis=0) / AREA
    head = head_ref[...]
    head_high, head_low = halves(head)
    scores = three_part(pooled, head_high, head_low, 1)
    capped = jnp.tanh(scores / LOGIT_CAP)
    logits = LOGIT_CAP * capped
    exponent = jnp.exp(logits)
    total = jnp.sum(exponent, axis=1, keepdims=True)
    classes = lax.broadcasted_iota(jnp.int32, logits.shape, 1)
    image_row = lax.broadcasted_iota(jnp.int32, (8, 1), 0)
    targets = jnp.zeros((8, 1), jnp.int32)
    live = jnp.zeros((8, 1), jnp.float32)
    for image in range(IMAGES):
        place = pipe + sections * image
        is_live = (lax.div(place, MB_IMG) < live_count_ref[0]).astype(jnp.float32)
        targets = jnp.where(image_row == image, labels_ref[place], targets)
        live = jnp.where(image_row == image, is_live, live)
    onehot = (classes == targets).astype(jnp.float32)
    row_loss = (jnp.log(total) - jnp.sum(logits * onehot, axis=1, keepdims=True)) * live
    score_cot = (exponent / total - onehot) * live * (1.0 - capped * capped)
    pooled_cot = three_part(score_cot, head_high, head_low, 0)
    spread = pooled_cot / AREA
    for image in range(IMAGES):
        cot_ref[rows_of(image)] = jnp.broadcast_to(
            spread[image : image + 1], (AREA, channels)
        ).astype(jnp.bfloat16)

    loss = jnp.broadcast_to(jnp.sum(row_loss, axis=0, keepdims=True), (LOSS_ROWS, channels))
    high = loss.astype(jnp.bfloat16).astype(jnp.float32)
    middle = (loss - high).astype(jnp.bfloat16).astype(jnp.float32)
    low = loss - high - middle
    device = lax.axis_index("dp") * sections + pipe
    part = lax.broadcasted_iota(jnp.int32, loss.shape, 0)
    own = lax.broadcasted_iota(jnp.int32, loss.shape, 1) == device
    parts = jnp.where(part == 0, high, jnp.where(part == 1, middle, low))
    parts = jnp.where(own & (part < 3), parts, 0.0).astype(jnp.bfloat16)
    for section in range(sections):
        for core in range(CORES):
            grad_ref[section, core, loss_start : loss_start + LOSS_ROWS] = parts
            grad_ref[section, core, loss_start + LOSS_ROWS :] = jnp.zeros(
                (HALF_ROWS - loss_start - LOSS_ROWS, channels), jnp.bfloat16
            )

    def backward(turn, _):
        step = count - 1 - turn
        cell = order_ref[step]
        section = lax.div(cell, CELLS_MAX)
        slot = lax.rem(cell, CELLS_MAX)
        rows = pl.ds(pl.multiple_of(slot * span, span), span)
        cot = cot_ref[...]
        for core in range(CORES):
            columns = slice(core * span, (core + 1) * span)
            grad_ref[section, core, rows] = lax.dot_general(
                deep_ref[step, :, columns],
                cot,
                (((0,), (0,)), ((), ())),
                preferred_element_type=jnp.float32,
            ).astype(jnp.bfloat16)
            deep_cot_ref[:, columns] = lax.dot_general(
                cot,
                weight_ref[section, core, rows],
                (((1,), (1,)), ((), ())),
                preferred_element_type=jnp.float32,
            ).astype(jnp.bfloat16)
        wave_re, wave_im = wave_ref[step, :HALF], wave_ref[step, HALF:]
        acts = abreast(acts_ref.at[step])
        seen = mul(into_ref[...], jnp.maximum(acts, 0))
        sent = mul(into_ref[...], abreast(deep_cot_ref))
        mixed = []
        for image in range(IMAGES):
            lanes = lanes_of(image)
            seen_re, seen_im = seen[:HALF, lanes], seen[HALF:, lanes]
            sent_re, sent_im = sent[:HALF, lanes], sent[HALF:, lanes]
            part_re = seen_re * sent_re + seen_im * sent_im
            part_im = seen_im * sent_re - seen_re * sent_im
            if image == 0:
                total_ref[:HALF] = part_re
                total_ref[HALF:] = part_im
            else:
                total_ref[:HALF] += part_re
                total_ref[HALF:] += part_im
            mixed.append(
                jnp.concatenate(
                    [
                        sent_re * wave_re + sent_im * wave_im,
                        sent_im * wave_re - sent_re * wave_im,
                    ],
                    axis=0,
                ).astype(jnp.bfloat16)
            )
        rect_cot = mul(back_ref[...], jnp.concatenate(mixed, axis=1))
        for image in range(IMAGES):
            lanes = lanes_of(image)
            passed = jnp.where(acts[:, lanes].astype(jnp.float32) > 0, rect_cot[:, lanes], 0.0)
            cot_ref[rows_of(image)] = (
                cot_ref[rows_of(image)].astype(jnp.float32) + passed
            ).astype(jnp.bfloat16)
        high, low = halves(total_ref[...])
        taps = (
            mul(tap_back_ref[0, slot], high)
            + mul(tap_back_ref[0, slot], low)
            + mul(tap_back_ref[1, slot], high)
        ).astype(jnp.bfloat16)
        for kind in range(CELLS_MAX):

            @pl.when(slot == kind)
            def _(kind=kind):
                first, last = TAP_STARTS[kind], TAP_STARTS[kind] + TAP_SPANS[kind]
                grad_ref[section, TAP_HALVES[kind], point_rows + first : point_rows + last] = taps[
                    first:last
                ]

        return 0

    lax.fori_loop(0, count, backward, 0)


def run_cells(cells, labels, live_count, features, weights, head):
    sections, channels = weights.shape[0], weights.shape[-1]
    slots = sections * CELLS_MAX
    tables = [jnp.asarray(table) for table in transform_tables()]
    vmem = pl.BlockSpec(memory_space=pltpu.VMEM)
    smem = pl.BlockSpec(memory_space=pltpu.SMEM)
    rows = IMAGES * AREA
    return pl.pallas_call(
        cells_kernel,
        out_shape=jax.ShapeDtypeStruct((sections, CORES, HALF_ROWS, channels), jnp.bfloat16),
        in_specs=[smem] * 3 + [vmem] * 7,
        out_specs=vmem,
        scratch_shapes=[
            pltpu.SMEM((slots + CELLS_MAX,), jnp.int32),
            pltpu.VMEM((slots + 1, rows, channels), jnp.bfloat16),
            pltpu.VMEM((slots, rows, channels), jnp.bfloat16),
            pltpu.VMEM((slots, 2 * HALF, channels), jnp.float32),
            pltpu.VMEM((rows, channels), jnp.bfloat16),
            pltpu.VMEM((rows, channels), jnp.bfloat16),
            pltpu.VMEM((2 * HALF, channels), jnp.float32),
        ],
        compiler_params=pltpu.CompilerParams(vmem_limit_bytes=CELLS_MB * 1024 * 1024),
        name="cells",
    )(cells, labels, live_count, features, weights, head, *tables)


class Place:
    def __init__(self, sections):
        self.sections = sections
        self.pipe = lax.axis_index("pipe")
        place = lax.axis_index("dp")
        self.core = lax.rem(place, CORES)
        self.z = lax.rem(lax.div(place, CORES), CHIPS_Z)
        self.x = lax.div(place, CORES * CHIPS_Z)

    def device(self, pipe=0, x=0, z=0, core=0):
        pipe = lax.rem(self.pipe + pipe, self.sections)
        x = lax.rem(self.x + x, CHIPS_X)
        z = lax.rem(self.z + z, CHIPS_Z)
        core = lax.rem(self.core + core, CORES)
        return (pipe, (x * CHIPS_Z + z) * CORES + core)

    def signal(self, partners):
        barrier = pltpu.get_barrier_semaphore()
        for partner in partners:
            pl.semaphore_signal(barrier, inc=1, device_id=partner, device_id_type=MESH)

    def wait(self, partners):
        pl.semaphore_wait(pltpu.get_barrier_semaphore(), partners)


def start_remote(source, target, send_sems, recv_sems, index, device):
    copy = pltpu.make_async_remote_copy(
        src_ref=source,
        dst_ref=target,
        send_sem=send_sems.at[index],
        recv_sem=recv_sems.at[index],
        device_id=device,
        device_id_type=MESH,
    )
    copy.start()
    return copy


def start_local(source, target, sems, index):
    copy = pltpu.make_async_copy(source, target, sems.at[index])
    copy.start()
    return copy


def gather_kernel(
    sections,
    weight_ref,
    three_ref,
    five_ref,
    seven_ref,
    features_ref,
    weights_ref,
    own_ref,
    taps_ref,
    direct_send,
    direct_recv,
    split_send,
    split_recv,
    spread_send,
    spread_recv,
    core_send,
    core_recv,
    weight_sem,
):
    at = Place(sections)
    others_y = range(1, sections)
    others_x = range(1, CHIPS_X)
    core = at.core
    channels = weights_ref.shape[-1]
    span = channels // CORES
    point_rows = CELLS_MAX * span
    at.signal(
        [at.device(pipe=d) for d in others_y]
        + [at.device(x=d) for d in others_x]
        + [at.device(core=1)]
    )
    loads = []
    for half in (core, lax.rem(core + 1, CORES)):
        for cell in range(CELLS_MAX):
            loads.append(
                start_local(
                    weight_ref.at[cell, half],
                    weights_ref.at[at.pipe, half, pl.ds(cell * span, span)],
                    weight_sem,
                    len(loads),
                )
            )
    taps_ref[...] = jnp.zeros_like(taps_ref)
    for slot, ref in enumerate((three_ref, five_ref, seven_ref)):
        size = 2 * slot + 3
        for u in range(size):
            row = TAP_STARTS[slot] + u * size
            taps_ref[TAP_HALVES[slot], row : row + size] = ref[u].astype(jnp.float32)
    for half in range(CORES):
        weights_ref[at.pipe, half, point_rows:] = taps_ref[half].astype(jnp.bfloat16)
    for copy in loads[:CELLS_MAX]:
        copy.wait()
    at.wait((sections - 1) + (CHIPS_X - 1) + 1)

    near = pl.ds(0, WEIGHT_A)
    far = pl.ds(WEIGHT_A, point_rows + TAP_ROWS - WEIGHT_A)

    def lanes(x):
        return pl.ds(pl.multiple_of(x * LANES, LANES), LANES)

    split, direct = [], []
    for d in others_y:
        piece = weights_ref.at[at.pipe, core, far, lanes(at.x)]
        split.append(
            start_remote(piece, piece, split_send, split_recv, d - 1, at.device(pipe=d))
        )
    sides = (1, 3)
    near_halves = [pl.ds(n * WEIGHT_A // 2, WEIGHT_A // 2) for n in range(2)]
    far_rows = point_rows + TAP_ROWS - WEIGHT_A
    far_halves = [pl.ds(WEIGHT_A + n * far_rows // 2, far_rows // 2) for n in range(2)]
    for n, side in enumerate(sides):
        piece = weights_ref.at[at.pipe, core, near]
        direct.append(
            start_remote(piece, piece, direct_send, direct_recv, n, at.device(pipe=side))
        )
    per_replica = features_ref.shape[0] // AREA
    group = (GROUP * IMAGES, GROUP * per_replica)
    row = lax.broadcasted_iota(jnp.int32, group, 0)
    column = lax.broadcasted_iota(jnp.int32, group, 1)
    wanted = lax.rem(row, GROUP) * per_replica + lax.div(row, GROUP) * sections + at.pipe
    pick = (column == wanted).astype(jnp.float32).astype(jnp.bfloat16)
    for g in range(AREA // GROUP):
        picked = mul(pick, features_ref[g * group[1] : (g + 1) * group[1]]).astype(jnp.bfloat16)
        for k in range(IMAGES):
            row = k * AREA + g * GROUP
            own_ref[row : row + GROUP] = picked[k * GROUP : (k + 1) * GROUP]

    spread, shared = [], []

    def share(piece):
        k = len(shared)
        shared.append(start_remote(piece, piece, core_send, core_recv, k, at.device(core=1)))

    def source(d):
        return lax.rem(at.pipe + sections - d, sections)

    for d in others_y:
        split[d - 1].wait_recv()
        piece = weights_ref.at[source(d), core, far, lanes(at.x)]
        for n, side in enumerate(sides):
            k = (d - 1) * len(sides) + n
            spread.append(
                start_remote(piece, piece, spread_send, spread_recv, k, at.device(x=side))
            )
        share(piece)
    near_relays, far_relays = [], []
    for n, side in enumerate(sides):
        direct[n].wait_recv()
        piece = weights_ref.at[source(side), core, near_halves[n]]
        near_relays.append(
            start_remote(piece, piece, direct_send, direct_recv, 2 + n, at.device(pipe=side))
        )
        share(weights_ref.at[source(side), core, near])
    for d in others_y:
        for n, side in enumerate(sides):
            spread[(d - 1) * len(sides) + n].wait_recv()
            x = lanes(lax.rem(at.x + CHIPS_X - side, CHIPS_X))
            piece = weights_ref.at[source(d), core, far_halves[n], x]
            k = (len(others_y) + d - 1) * len(sides) + n
            far_relays.append(
                start_remote(piece, piece, spread_send, spread_recv, k, at.device(x=side))
            )
            share(weights_ref.at[source(d), core, far, x])
    for copy in near_relays:
        copy.wait_recv()
    share(weights_ref.at[source(2), core, near])
    opposite = lanes(lax.rem(at.x + 2, CHIPS_X))
    for d in others_y:
        for n in range(len(sides)):
            far_relays[(d - 1) * len(sides) + n].wait_recv()
        share(weights_ref.at[source(d), core, far, opposite])
    for copy in loads[CELLS_MAX:]:
        copy.wait()
    for copy in shared:
        copy.wait_recv()
    for copy in shared + split + direct + near_relays + spread + far_relays:
        copy.wait_send()


def gather_weights(weight, three, five, seven, features, sections):
    cells, channels = weight.shape[0], weight.shape[-1]
    weight = weight.reshape(cells, CORES, channels // CORES, channels)
    vmem = pl.BlockSpec(memory_space=pltpu.VMEM)
    anywhere = pl.BlockSpec(memory_space=pl.ANY)
    dma = pltpu.SemaphoreType.DMA
    ys, xs = sections - 1, CHIPS_X - 1
    rows = cells * channels // CORES + TAP_ROWS
    return pl.pallas_call(
        functools.partial(gather_kernel, sections),
        out_shape=(
            jax.ShapeDtypeStruct((sections, CORES, rows, channels), weight.dtype),
            jax.ShapeDtypeStruct((IMAGES * AREA, channels), features.dtype),
        ),
        in_specs=[anywhere, vmem, vmem, vmem, vmem],
        out_specs=(vmem, vmem),
        scratch_shapes=[
            pltpu.VMEM((CORES, TAP_ROWS, channels), jnp.float32),
            dma((4,)),
            dma((4,)),
            dma((ys,)),
            dma((ys,)),
            dma((ys * 4,)),
            dma((ys * 4,)),
            dma((2 * ys + ys * xs,)),
            dma((2 * ys + ys * xs,)),
            dma((CORES * cells,)),
        ],
        compiler_params=pltpu.CompilerParams(
            collective_id=0, has_side_effects=True, vmem_limit_bytes=24 * 1024 * 1024
        ),
        name="gather",
    )(weight, three, five, seven, features)


def reduce_kernel(
    sections,
    grad_ref,
    out_ref,
    pair_ref,
    part_ref,
    via_a_ref,
    via_b_ref,
    in_a1_ref,
    in_b1_ref,
    mid_a_ref,
    mid_b_ref,
    in_a2_ref,
    in_b2_ref,
    small_ref,
    in_z_ref,
    line_ref,
    plane_ref,
    pair_send,
    pair_recv,
    via_a_send,
    via_a_recv,
    via_b_send,
    via_b_recv,
    a1_send,
    a1_recv,
    b1_send,
    b1_recv,
    a2_send,
    a2_recv,
    b2_send,
    b2_recv,
    z_send,
    z_recv,
    line_send,
    line_recv,
    plane_send,
    plane_recv,
    core_send,
    core_recv,
    column_sem,
    half_sem,
):
    at = Place(sections)
    others_y = range(1, sections)
    others_x = range(1, CHIPS_X)
    others_z = range(1, CHIPS_Z)
    partner = at.device(core=1)
    at.signal(
        [partner]
        + [at.device(pipe=d) for d in others_y]
        + [at.device(x=d) for d in others_x]
        + [at.device(z=d) for d in others_z]
    )
    at.wait(1 + len(others_y) + len(others_x) + len(others_z))
    f32 = jnp.float32
    bf16 = jnp.bfloat16
    order = (2, 1, 3, 0)
    other_core = lax.rem(at.core + 1, CORES)
    all_z = pl.ds(0, CHIPS_Z)
    first_z = pl.ds(0, FIRST_Z)
    last_z = pl.ds(FIRST_Z, LAST_Z)
    last_all = pl.ds(0, LAST_Z)
    via_all = pl.ds(0, VIA_Z)
    sides = (1, 3)

    def lanes(x):
        return pl.ds(pl.multiple_of(x * LANES, LANES), LANES)

    def section_at(d):
        return lax.rem(at.pipe + d, sections)

    def stream(turn, start, size):
        rows = pl.ds(start, size)
        paired, via_a, via_b, a1, b1, a2, b2 = {}, {}, {}, {}, {}, {}, {}
        for k, d in enumerate(order):
            section = section_at(d)
            paired[d] = start_remote(
                grad_ref.at[section, other_core, all_z, rows],
                pair_ref.at[section, all_z, rows],
                pair_send,
                pair_recv,
                turn * sections + k,
                partner,
            )
        yield
        for d in order:
            section = section_at(d)
            paired[d].wait_recv()

            def add_pair(z, _, section=section):
                total = grad_ref[section, at.core, z, rows].astype(f32)
                total = total + pair_ref[section, z, rows].astype(f32)
                part_ref[section, z, rows] = total.astype(bf16)
                return 0

            lax.fori_loop(0, CHIPS_Z, add_pair, 0)
            for n, side in enumerate(sides):
                if d == 2:
                    via_a[side] = start_remote(
                        part_ref.at[section, pl.ds(n * VIA_Z, VIA_Z), rows],
                        via_a_ref.at[n, via_all, rows],
                        via_a_send,
                        via_a_recv,
                        turn * len(sides) + n,
                        at.device(pipe=side),
                    )
                via_b[d, side] = start_remote(
                    part_ref.at[
                        section,
                        pl.ds(FIRST_Z + n * VIA_Z, VIA_Z),
                        rows,
                        lanes(lax.rem(at.x + 2, CHIPS_X)),
                    ],
                    via_b_ref.at[n, section, via_all, rows],
                    via_b_send,
                    via_b_recv,
                    (turn * sections + d) * len(sides) + n,
                    at.device(x=side),
                )
        yield
        for n, side in enumerate(sides):
            section = section_at(side)
            via_a[side].wait_recv()

            def add_via_a(z, _, section=section, n=n):
                total = part_ref[section, n * VIA_Z + z, rows].astype(f32)
                total = total + via_a_ref[n, z, rows].astype(f32)
                part_ref[section, n * VIA_Z + z, rows] = total.astype(bf16)
                return 0

            lax.fori_loop(0, VIA_Z, add_via_a, 0)
            a1[side] = start_remote(
                part_ref.at[section, first_z, rows],
                in_a1_ref.at[n, first_z, rows],
                a1_send,
                a1_recv,
                turn * len(sides) + n,
                at.device(pipe=side),
            )
        for d in order:
            section = section_at(d)
            for n, side in enumerate(sides):
                via_b[d, side].wait_recv()
                place = lanes(lax.rem(at.x + side, CHIPS_X))

                def add_via_b(z, _, section=section, n=n, place=place):
                    row = FIRST_Z + n * VIA_Z + z
                    total = part_ref[section, row, rows, place].astype(f32)
                    total = total + via_b_ref[n, section, z, rows].astype(f32)
                    part_ref[section, row, rows, place] = total.astype(bf16)
                    return 0

                lax.fori_loop(0, VIA_Z, add_via_b, 0)
                b1[d, side] = start_remote(
                    part_ref.at[section, last_z, rows, place],
                    in_b1_ref.at[n, section, last_all, rows],
                    b1_send,
                    b1_recv,
                    (turn * sections + d) * len(sides) + n,
                    at.device(x=side),
                )
        yield
        for d in order:
            section = section_at(d)
            for side in sides:
                b1[d, side].wait_recv()

            def add_b1(z, _, section=section):
                total = part_ref[section, FIRST_Z + z, rows, lanes(at.x)].astype(f32)
                for n in range(len(sides)):
                    total = total + in_b1_ref[n, section, z, rows].astype(f32)
                mid_b_ref[section, z, rows] = total.astype(bf16)
                return 0

            lax.fori_loop(0, LAST_Z, add_b1, 0)
            if d:
                b2[d] = start_remote(
                    mid_b_ref.at[section, last_all, rows],
                    in_b2_ref.at[d - 1, last_all, rows],
                    b2_send,
                    b2_recv,
                    turn * len(others_y) + d - 1,
                    at.device(pipe=d),
                )
        for side in sides:
            a1[side].wait_recv()

        def add_a1(z, _):
            total = part_ref[at.pipe, z, rows].astype(f32)
            for n in range(len(sides)):
                total = total + in_a1_ref[n, z, rows].astype(f32)
            mid_a_ref[z, rows] = total.astype(bf16)
            return 0

        lax.fori_loop(0, FIRST_Z, add_a1, 0)
        for e in others_x:
            a2[e] = start_remote(
                mid_a_ref.at[first_z, rows, lanes(lax.rem(at.x + e, CHIPS_X))],
                in_a2_ref.at[e - 1, first_z, rows],
                a2_send,
                a2_recv,
                turn * len(others_x) + e - 1,
                at.device(x=e),
            )
        yield
        for d in others_y:
            b2[d].wait_recv()
        for e in others_x:
            a2[e].wait_recv()

        def add_a2(z, _):
            total = mid_a_ref[z, rows, lanes(at.x)].astype(f32)
            for e in others_x:
                total = total + in_a2_ref[e - 1, z, rows].astype(f32)
            small_ref[z, rows] = total.astype(bf16)
            return 0

        def add_b2(z, _):
            total = mid_b_ref[at.pipe, z, rows].astype(f32)
            for d in others_y:
                total = total + in_b2_ref[d - 1, z, rows].astype(f32)
            small_ref[FIRST_Z + z, rows] = total.astype(bf16)
            return 0

        lax.fori_loop(0, FIRST_Z, add_a2, 0)
        lax.fori_loop(0, LAST_Z, add_b2, 0)
        to_z = [
            start_remote(
                small_ref.at[lax.rem(at.z + d, CHIPS_Z), rows],
                in_z_ref.at[d - 1, rows],
                z_send,
                z_recv,
                turn * len(others_z) + d - 1,
                at.device(z=d),
            )
            for d in others_z
        ]
        yield
        for copy in to_z:
            copy.wait_recv()
        total = small_ref[at.z, rows].astype(f32)
        for d in others_z:
            total = total + in_z_ref[d - 1, rows].astype(f32)
        if turn in X_FIRST:
            plane_ref[at.z, rows, lanes(at.x)] = total.astype(bf16)
            piece = plane_ref.at[at.z, rows, lanes(at.x)]
            plane = [
                start_remote(
                    piece,
                    piece,
                    plane_send,
                    plane_recv,
                    turn * len(others_x) + e - 1,
                    at.device(x=e),
                )
                for e in others_x
            ]
            yield
            for copy in plane:
                copy.wait_recv()
            piece = plane_ref.at[at.z, rows]
        else:
            line_ref[at.z, rows] = total.astype(bf16)
            piece = line_ref.at[at.z, rows]
        line = [
            start_remote(
                piece,
                piece,
                line_send,
                line_recv,
                turn * len(others_z) + d - 1,
                at.device(z=d),
            )
            for d in others_z
        ]
        yield
        for copy in line:
            copy.wait_recv()
        if turn not in X_FIRST:
            column = plane_ref.at[all_z, rows, lanes(at.x)]
            plane = [
                start_remote(
                    line_ref.at[all_z, rows],
                    column,
                    plane_send,
                    plane_recv,
                    turn * len(others_x) + e - 1,
                    at.device(x=e),
                )
                for e in others_x
            ]
            own_column = start_local(line_ref.at[all_z, rows], column, column_sem, turn)
            yield
            own_column.wait()
            for copy in plane:
                copy.wait_recv()
        half = out_ref.at[at.core, all_z, rows]
        last = start_remote(
            plane_ref.at[all_z, rows], half, core_send, core_recv, turn, partner
        )
        own_half = start_local(plane_ref.at[all_z, rows], half, half_sem, turn)
        yield
        own_half.wait()
        last.wait()
        for copies in (paired, via_a, via_b, a1, b1, a2, b2):
            for copy in copies.values():
                copy.wait_send()
        for copy in to_z + line + plane:
            copy.wait_send()

    running = [stream(turn, *span) for turn, span in enumerate(STREAMS)]
    while running:
        running = [one for one in running if next(one, running) is None]


def reduce_grads(grads, sections):
    rows, channels = grads.shape[2:]
    grads = grads.reshape(sections, CORES, CHIPS_Z, CHUNK, channels)
    dma = pltpu.SemaphoreType.DMA
    ys, xs, zs, turns = sections - 1, CHIPS_X - 1, CHIPS_Z - 1, len(STREAMS)

    def vmem(*shape):
        return pltpu.VMEM(shape, jnp.bfloat16)

    out = pl.pallas_call(
        functools.partial(reduce_kernel, sections),
        out_shape=jax.ShapeDtypeStruct((CORES, CHIPS_Z, CHUNK, channels), jnp.bfloat16),
        in_specs=[pl.BlockSpec(memory_space=pltpu.VMEM)],
        out_specs=pl.BlockSpec(memory_space=pl.ANY),
        scratch_shapes=[
            vmem(sections, CHIPS_Z, CHUNK, channels),
            vmem(sections, CHIPS_Z, CHUNK, channels),
            vmem(2, VIA_Z, CHUNK, channels),
            vmem(2, sections, VIA_Z, CHUNK, LANES),
            vmem(2, FIRST_Z, CHUNK, channels),
            vmem(2, sections, LAST_Z, CHUNK, LANES),
            vmem(FIRST_Z, CHUNK, channels),
            vmem(sections, LAST_Z, CHUNK, LANES),
            vmem(xs, FIRST_Z, CHUNK, LANES),
            vmem(ys, LAST_Z, CHUNK, LANES),
            vmem(CHIPS_Z, CHUNK, LANES),
            vmem(zs, CHUNK, LANES),
            vmem(CHIPS_Z, CHUNK, LANES),
            vmem(CHIPS_Z, CHUNK, channels),
        ]
        + [
            dma((turns * count,))
            for count in (sections, 2, 2 * sections, 2, 2 * sections, xs, ys, zs, zs, xs, 1)
            for _ in ("send", "receive")
        ]
        + [dma((turns,)), dma((turns,))],
        compiler_params=pltpu.CompilerParams(
            collective_id=1, has_side_effects=True, vmem_limit_bytes=24 * 1024 * 1024
        ),
        name="reduce",
    )(grads)
    return out.reshape(CORES, rows, channels)


def own_taps(block, slot):
    size = 2 * slot + 3
    start = CELLS_MAX * block.shape[-1] // CORES + TAP_STARTS[slot]
    rows = block[TAP_HALVES[slot], start : start + size * size].astype(jnp.float32)
    return rows.reshape(1, size, size, block.shape[-1])


def shards(
    features,
    labels,
    micro_count,
    cells_per_section,
    point_weight,
    depth_three,
    depth_five,
    depth_seven,
    head_weight,
):
    sections = lax.axis_size("pipe")
    channels = point_weight.shape[-1]
    by_position = features.transpose(1, 2, 0, 3).reshape(-1, channels)
    weights, own = gather_weights(
        point_weight[0], depth_three[0], depth_five[0], depth_seven[0], by_position, sections
    )
    grads = run_cells(cells_per_section, labels, micro_count, own, weights, head_weight.T)
    block = reduce_grads(grads, sections)
    span = channels // CORES
    point_rows = CELLS_MAX * span
    loss_start = point_rows + TAP_ROWS
    total_loss = jnp.sum(block[0, loss_start : loss_start + 3].astype(jnp.float32))
    point_sum = block[:, :point_rows].reshape(CORES, CELLS_MAX, span, channels)
    point_sum = point_sum.transpose(1, 0, 2, 3).astype(jnp.float32)
    return (
        total_loss,
        point_sum.reshape(1, CELLS_MAX, channels, channels),
        own_taps(block, 0),
        own_taps(block, 1),
        own_taps(block, 2),
    )


def solution(mesh):
    return jax.shard_map(
        shards,
        mesh=mesh,
        in_specs=(
            P("dp", None, None, None),
            P("dp"),
            P("dp"),
            P(),
            P("pipe", None, None, None),
            P("pipe", None, None, None),
            P("pipe", None, None, None),
            P("pipe", None, None, None),
            P(),
        ),
        out_specs=(
            P(),
            P("pipe", None, None, None),
            P("pipe", None, None, None),
            P("pipe", None, None, None),
            P("pipe", None, None, None),
        ),
        check_vma=False,
    )
```

```python
import functools

import jax
import jax.numpy as jnp
import ml_dtypes
import numpy as np
from jax import lax
from jax.experimental import pallas as pl
from jax.experimental.pallas import tpu as pltpu
from jax.sharding import PartitionSpec as P

SIDE = 12
AREA = SIDE * SIDE
MB_IMG = 2
CELLS_MAX = 3
TAPS = 7
TAP_ROWS = 64
LOGIT_CAP = 30.0
CYCLE = SIDE + TAPS // 2
HALF = 120
IMAGES = 4
GROUP = 16
CHIPS_X = 4
CHIPS_Z = 8
CORES = 2
LANES = 128
MESH = pl.DeviceIdType.MESH
TAP_HALVES = (0, 0, 1)
TAP_STARTS = (0, 16, 0)
TAP_SPANS = (16, 32, 64)
CHUNK = 112
STREAMS = ((0, 32), (32, 32), (64, 32), (96, 16))
X_FIRST = (2,)
FIRST_Z = 4
LAST_Z = CHIPS_Z - FIRST_Z
VIA_Z = 2
HALF_ROWS = CHIPS_Z * CHUNK
LOSS_ROWS = 16
WEIGHT_A = 320
CELLS_MB = 32


def transform_tables():
    slots = [(0, 0)]
    seen = {(0, 0)}
    for u in range(CYCLE):
        for v in range(CYCLE):
            if (u, v) in seen:
                continue
            seen.add((u, v))
            seen.add(((-u) % CYCLE, (-v) % CYCLE))
            slots.append((u, v))
    count = len(slots)
    waves = np.array(slots, np.float64)
    sites = np.array([(i, j) for i in range(SIDE) for j in range(SIDE)], np.float64)
    weight = np.where((waves == 0).all(1), 1.0, 2.0)[:, None] / CYCLE**2
    site_angle = 2 * np.pi * ((waves @ sites.T) % CYCLE) / CYCLE
    into = np.zeros((2 * HALF, AREA))
    into[:count] = np.cos(site_angle)
    into[HALF : HALF + count] = -np.sin(site_angle)
    back = np.zeros((AREA, 2 * HALF))
    back[:, :count] = (np.cos(site_angle) * weight).T
    back[:, HALF : HALF + count] = -(np.sin(site_angle) * weight).T
    tap_into = np.zeros((CELLS_MAX, 2 * HALF, TAP_ROWS))
    tap_back = np.zeros((CELLS_MAX, TAP_ROWS, 2 * HALF))
    for slot in range(CELLS_MAX):
        size = 2 * slot + 3
        reach = size // 2
        shifts = np.array(
            [(u - reach, v - reach) for u in range(size) for v in range(size)], np.float64
        )
        taps = slice(TAP_STARTS[slot], TAP_STARTS[slot] + size * size)
        tap_angle = 2 * np.pi * ((waves @ shifts.T) % CYCLE) / CYCLE
        tap_into[slot, :count, taps] = np.cos(tap_angle)
        tap_into[slot, HALF : HALF + count, taps] = np.sin(tap_angle)
        tap_back[slot, taps, :count] = (np.cos(tap_angle) * weight).T
        tap_back[slot, taps, HALF : HALF + count] = -(np.sin(tap_angle) * weight).T
    return [
        pair_of(into)[0],
        pair_of(back)[0],
        np.concatenate(pair_of(tap_into), axis=2),
        np.concatenate(pair_of(tap_back), axis=1),
    ]


def pair_of(table):
    high = table.astype(ml_dtypes.bfloat16)
    low = (table - high.astype(np.float64)).astype(ml_dtypes.bfloat16)
    return np.stack([high, low])


def mul(a, b):
    return jnp.dot(a, b, preferred_element_type=jnp.float32)


def halves(values):
    high = values.astype(jnp.bfloat16)
    low = (values - high.astype(jnp.float32)).astype(jnp.bfloat16)
    return high, low


def three_part(left, right_high, right_low, dim):
    rows = left.shape[0]
    dims = (((1,), (dim,)), ((), ()))
    high, low = halves(left)
    both = lax.dot_general(
        jnp.concatenate([high, low], axis=0), right_high, dims, preferred_element_type=jnp.float32
    )
    rest = lax.dot_general(high, right_low, dims, preferred_element_type=jnp.float32)
    return both[:rows] + (both[rows:] + rest)


def cells_kernel(
    cells_ref,
    labels_ref,
    live_count_ref,
    features_ref,
    weight_ref,
    head_ref,
    into_ref,
    back_ref,
    tap_into_ref,
    tap_back_ref,
    grad_ref,
    order_ref,
    acts_ref,
    deep_ref,
    wave_ref,
    cot_ref,
    deep_cot_ref,
    total_ref,
):
    sections, channels = weight_ref.shape[0], weight_ref.shape[-1]
    span = channels // CORES
    point_rows = CELLS_MAX * span
    loss_start = point_rows + TAP_ROWS
    pipe = lax.axis_index("pipe")
    count = jnp.int32(0)
    for section in range(sections):
        held = cells_ref[section]
        for slot in range(CELLS_MAX):
            order_ref[count + slot] = section * CELLS_MAX + slot
        for slot in range(1, CELLS_MAX):

            @pl.when(slot >= held)
            def _(section=section, slot=slot):
                for core in range(CORES):
                    grad_ref[section, core, slot * span : (slot + 1) * span] = jnp.zeros(
                        (span, channels), jnp.bfloat16
                    )
                row = point_rows + TAP_STARTS[slot]
                grad_ref[section, TAP_HALVES[slot], row : row + TAP_SPANS[slot]] = jnp.zeros(
                    (TAP_SPANS[slot], channels), jnp.bfloat16
                )

        count = count + held

    acts_ref[0] = features_ref[...]

    def rows_of(image):
        return pl.ds(image * AREA, AREA)

    def lanes_of(image):
        return slice(image * channels, (image + 1) * channels)

    def abreast(ref):
        return jnp.concatenate([ref[rows_of(image)] for image in range(IMAGES)], axis=1)

    def forward(step, _):
        cell = order_ref[step]
        section = lax.div(cell, CELLS_MAX)
        slot = lax.rem(cell, CELLS_MAX)
        taps = weight_ref[section, lax.div(slot, CELLS_MAX - 1), point_rows:]
        wave = mul(tap_into_ref[slot], jnp.concatenate([taps, taps], axis=0))
        wave_ref[step] = wave
        wave_re, wave_im = wave[:HALF], wave[HALF:]
        seen = mul(into_ref[...], jnp.maximum(abreast(acts_ref.at[step]), 0))
        mixed = []
        for image in range(IMAGES):
            lanes = lanes_of(image)
            seen_re, seen_im = seen[:HALF, lanes], seen[HALF:, lanes]
            mixed.append(
                jnp.concatenate(
                    [
                        seen_re * wave_re - seen_im * wave_im,
                        seen_re * wave_im + seen_im * wave_re,
                    ],
                    axis=0,
                ).astype(jnp.bfloat16)
            )
        deep = mul(back_ref[...], jnp.concatenate(mixed, axis=1)).astype(jnp.bfloat16)
        for image in range(IMAGES):
            deep_ref[step, rows_of(image)] = deep[:, lanes_of(image)]
        rows = pl.ds(pl.multiple_of(slot * span, span), span)
        mixed = mul(deep_ref[step, :, :span], weight_ref[section, 0, rows]) + mul(
            deep_ref[step, :, span:], weight_ref[section, 1, rows]
        )
        acts_ref[step + 1] = (acts_ref[step].astype(jnp.float32) + mixed).astype(jnp.bfloat16)
        return 0

    lax.fori_loop(0, count, forward, 0)

    means = [
        jnp.sum(acts_ref[count, rows_of(image)].astype(jnp.float32), axis=0, keepdims=True)
        for image in range(IMAGES)
    ]
    spare = jnp.zeros((8 - IMAGES, channels), jnp.float32)
    pooled = jnp.concatenate(means + [spare], axis=0) / AREA
    head = head_ref[...]
    head_high, head_low = halves(head)
    scores = three_part(pooled, head_high, head_low, 1)
    capped = jnp.tanh(scores / LOGIT_CAP)
    logits = LOGIT_CAP * capped
    exponent = jnp.exp(logits)
    total = jnp.sum(exponent, axis=1, keepdims=True)
    classes = lax.broadcasted_iota(jnp.int32, logits.shape, 1)
    image_row = lax.broadcasted_iota(jnp.int32, (8, 1), 0)
    targets = jnp.zeros((8, 1), jnp.int32)
    live = jnp.zeros((8, 1), jnp.float32)
    for image in range(IMAGES):
        place = pipe + sections * image
        is_live = (lax.div(place, MB_IMG) < live_count_ref[0]).astype(jnp.float32)
        targets = jnp.where(image_row == image, labels_ref[place], targets)
        live = jnp.where(image_row == image, is_live, live)
    onehot = (classes == targets).astype(jnp.float32)
    row_loss = (jnp.log(total) - jnp.sum(logits * onehot, axis=1, keepdims=True)) * live
    score_cot = (exponent / total - onehot) * live * (1.0 - capped * capped)
    pooled_cot = three_part(score_cot, head_high, head_low, 0)
    spread = pooled_cot / AREA
    for image in range(IMAGES):
        cot_ref[rows_of(image)] = jnp.broadcast_to(
            spread[image : image + 1], (AREA, channels)
        ).astype(jnp.bfloat16)

    loss = jnp.broadcast_to(jnp.sum(row_loss, axis=0, keepdims=True), (LOSS_ROWS, channels))
    high = loss.astype(jnp.bfloat16).astype(jnp.float32)
    middle = (loss - high).astype(jnp.bfloat16).astype(jnp.float32)
    low = loss - high - middle
    device = lax.axis_index("dp") * sections + pipe
    part = lax.broadcasted_iota(jnp.int32, loss.shape, 0)
    own = lax.broadcasted_iota(jnp.int32, loss.shape, 1) == device
    parts = jnp.where(part == 0, high, jnp.where(part == 1, middle, low))
    parts = jnp.where(own & (part < 3), parts, 0.0).astype(jnp.bfloat16)
    for section in range(sections):
        for core in range(CORES):
            grad_ref[section, core, loss_start : loss_start + LOSS_ROWS] = parts
            grad_ref[section, core, loss_start + LOSS_ROWS :] = jnp.zeros(
                (HALF_ROWS - loss_start - LOSS_ROWS, channels), jnp.bfloat16
            )

    def backward(turn, _):
        step = count - 1 - turn
        cell = order_ref[step]
        section = lax.div(cell, CELLS_MAX)
        slot = lax.rem(cell, CELLS_MAX)
        rows = pl.ds(pl.multiple_of(slot * span, span), span)
        cot = cot_ref[...]
        for core in range(CORES):
            columns = slice(core * span, (core + 1) * span)
            grad_ref[section, core, rows] = lax.dot_general(
                deep_ref[step, :, columns],
                cot,
                (((0,), (0,)), ((), ())),
                preferred_element_type=jnp.float32,
            ).astype(jnp.bfloat16)
            deep_cot_ref[:, columns] = lax.dot_general(
                cot,
                weight_ref[section, core, rows],
                (((1,), (1,)), ((), ())),
                preferred_element_type=jnp.float32,
            ).astype(jnp.bfloat16)
        wave_re, wave_im = wave_ref[step, :HALF], wave_ref[step, HALF:]
        acts = abreast(acts_ref.at[step])
        seen = mul(into_ref[...], jnp.maximum(acts, 0))
        sent = mul(into_ref[...], abreast(deep_cot_ref))
        mixed = []
        for image in range(IMAGES):
            lanes = lanes_of(image)
            seen_re, seen_im = seen[:HALF, lanes], seen[HALF:, lanes]
            sent_re, sent_im = sent[:HALF, lanes], sent[HALF:, lanes]
            part_re = seen_re * sent_re + seen_im * sent_im
            part_im = seen_im * sent_re - seen_re * sent_im
            if image == 0:
                total_ref[:HALF] = part_re
                total_ref[HALF:] = part_im
            else:
                total_ref[:HALF] += part_re
                total_ref[HALF:] += part_im
            mixed.append(
                jnp.concatenate(
                    [
                        sent_re * wave_re + sent_im * wave_im,
                        sent_im * wave_re - sent_re * wave_im,
                    ],
                    axis=0,
                ).astype(jnp.bfloat16)
            )
        rect_cot = mul(back_ref[...], jnp.concatenate(mixed, axis=1))
        for image in range(IMAGES):
            lanes = lanes_of(image)
            passed = jnp.where(acts[:, lanes].astype(jnp.float32) > 0, rect_cot[:, lanes], 0.0)
            cot_ref[rows_of(image)] = (
                cot_ref[rows_of(image)].astype(jnp.float32) + passed
            ).astype(jnp.bfloat16)
        high, low = halves(total_ref[...])
        both = mul(tap_back_ref[slot], high)
        rest = mul(tap_back_ref[slot, :TAP_ROWS], low)
        taps = (both[:TAP_ROWS] + (both[TAP_ROWS:] + rest)).astype(jnp.bfloat16)
        for kind in range(CELLS_MAX):

            @pl.when(slot == kind)
            def _(kind=kind):
                first, last = TAP_STARTS[kind], TAP_STARTS[kind] + TAP_SPANS[kind]
                grad_ref[section, TAP_HALVES[kind], point_rows + first : point_rows + last] = taps[
                    first:last
                ]

        return 0

    lax.fori_loop(0, count, backward, 0)


def run_cells(cells, labels, live_count, features, weights, head):
    sections, channels = weights.shape[0], weights.shape[-1]
    slots = sections * CELLS_MAX
    tables = [jnp.asarray(table) for table in transform_tables()]
    vmem = pl.BlockSpec(memory_space=pltpu.VMEM)
    smem = pl.BlockSpec(memory_space=pltpu.SMEM)
    rows = IMAGES * AREA
    return pl.pallas_call(
        cells_kernel,
        out_shape=jax.ShapeDtypeStruct((sections, CORES, HALF_ROWS, channels), jnp.bfloat16),
        in_specs=[smem] * 3 + [vmem] * 7,
        out_specs=vmem,
        scratch_shapes=[
            pltpu.SMEM((slots + CELLS_MAX,), jnp.int32),
            pltpu.VMEM((slots + 1, rows, channels), jnp.bfloat16),
            pltpu.VMEM((slots, rows, channels), jnp.bfloat16),
            pltpu.VMEM((slots, 2 * HALF, channels), jnp.float32),
            pltpu.VMEM((rows, channels), jnp.bfloat16),
            pltpu.VMEM((rows, channels), jnp.bfloat16),
            pltpu.VMEM((2 * HALF, channels), jnp.float32),
        ],
        compiler_params=pltpu.CompilerParams(vmem_limit_bytes=CELLS_MB * 1024 * 1024),
        name="cells",
    )(cells, labels, live_count, features, weights, head, *tables)


class Place:
    def __init__(self, sections):
        self.sections = sections
        self.pipe = lax.axis_index("pipe")
        place = lax.axis_index("dp")
        self.core = lax.rem(place, CORES)
        self.z = lax.rem(lax.div(place, CORES), CHIPS_Z)
        self.x = lax.div(place, CORES * CHIPS_Z)

    def device(self, pipe=0, x=0, z=0, core=0):
        pipe = lax.rem(self.pipe + pipe, self.sections)
        x = lax.rem(self.x + x, CHIPS_X)
        z = lax.rem(self.z + z, CHIPS_Z)
        core = lax.rem(self.core + core, CORES)
        return (pipe, (x * CHIPS_Z + z) * CORES + core)

    def signal(self, partners):
        barrier = pltpu.get_barrier_semaphore()
        for partner in partners:
            pl.semaphore_signal(barrier, inc=1, device_id=partner, device_id_type=MESH)

    def wait(self, partners):
        pl.semaphore_wait(pltpu.get_barrier_semaphore(), partners)


def start_remote(source, target, send_sems, recv_sems, index, device):
    copy = pltpu.make_async_remote_copy(
        src_ref=source,
        dst_ref=target,
        send_sem=send_sems.at[index],
        recv_sem=recv_sems.at[index],
        device_id=device,
        device_id_type=MESH,
    )
    copy.start()
    return copy


def start_local(source, target, sems, index):
    copy = pltpu.make_async_copy(source, target, sems.at[index])
    copy.start()
    return copy


def gather_kernel(
    sections,
    weight_ref,
    three_ref,
    five_ref,
    seven_ref,
    features_ref,
    weights_ref,
    own_ref,
    taps_ref,
    direct_send,
    direct_recv,
    split_send,
    split_recv,
    spread_send,
    spread_recv,
    core_send,
    core_recv,
    weight_sem,
):
    at = Place(sections)
    others_y = range(1, sections)
    others_x = range(1, CHIPS_X)
    core = at.core
    channels = weights_ref.shape[-1]
    span = channels // CORES
    point_rows = CELLS_MAX * span
    at.signal(
        [at.device(pipe=d) for d in others_y]
        + [at.device(x=d) for d in others_x]
        + [at.device(core=1)]
    )
    loads = []
    for half in (core, lax.rem(core + 1, CORES)):
        for cell in range(CELLS_MAX):
            loads.append(
                start_local(
                    weight_ref.at[cell, half],
                    weights_ref.at[at.pipe, half, pl.ds(cell * span, span)],
                    weight_sem,
                    len(loads),
                )
            )
    taps_ref[...] = jnp.zeros_like(taps_ref)
    for slot, ref in enumerate((three_ref, five_ref, seven_ref)):
        size = 2 * slot + 3
        for u in range(size):
            row = TAP_STARTS[slot] + u * size
            taps_ref[TAP_HALVES[slot], row : row + size] = ref[u].astype(jnp.float32)
    for half in range(CORES):
        weights_ref[at.pipe, half, point_rows:] = taps_ref[half].astype(jnp.bfloat16)
    for copy in loads[:CELLS_MAX]:
        copy.wait()
    at.wait((sections - 1) + (CHIPS_X - 1) + 1)

    near = pl.ds(0, WEIGHT_A)
    far = pl.ds(WEIGHT_A, point_rows + TAP_ROWS - WEIGHT_A)

    def lanes(x):
        return pl.ds(pl.multiple_of(x * LANES, LANES), LANES)

    split, direct = [], []
    for d in others_y:
        piece = weights_ref.at[at.pipe, core, far, lanes(at.x)]
        split.append(
            start_remote(piece, piece, split_send, split_recv, d - 1, at.device(pipe=d))
        )
    sides = (1, 3)
    near_halves = [pl.ds(n * WEIGHT_A // 2, WEIGHT_A // 2) for n in range(2)]
    far_rows = point_rows + TAP_ROWS - WEIGHT_A
    far_halves = [pl.ds(WEIGHT_A + n * far_rows // 2, far_rows // 2) for n in range(2)]
    for n, side in enumerate(sides):
        piece = weights_ref.at[at.pipe, core, near]
        direct.append(
            start_remote(piece, piece, direct_send, direct_recv, n, at.device(pipe=side))
        )
    per_replica = features_ref.shape[0] // AREA
    group = (GROUP * IMAGES, GROUP * per_replica)
    row = lax.broadcasted_iota(jnp.int32, group, 0)
    column = lax.broadcasted_iota(jnp.int32, group, 1)
    wanted = lax.rem(row, GROUP) * per_replica + lax.div(row, GROUP) * sections + at.pipe
    pick = (column == wanted).astype(jnp.float32).astype(jnp.bfloat16)
    for g in range(AREA // GROUP):
        picked = mul(pick, features_ref[g * group[1] : (g + 1) * group[1]]).astype(jnp.bfloat16)
        for k in range(IMAGES):
            row = k * AREA + g * GROUP
            own_ref[row : row + GROUP] = picked[k * GROUP : (k + 1) * GROUP]

    spread, shared = [], []

    def share(piece):
        k = len(shared)
        shared.append(start_remote(piece, piece, core_send, core_recv, k, at.device(core=1)))

    def source(d):
        return lax.rem(at.pipe + sections - d, sections)

    for d in others_y:
        split[d - 1].wait_recv()
        piece = weights_ref.at[source(d), core, far, lanes(at.x)]
        for n, side in enumerate(sides):
            k = (d - 1) * len(sides) + n
            spread.append(
                start_remote(piece, piece, spread_send, spread_recv, k, at.device(x=side))
            )
        share(piece)
    near_relays, far_relays = [], []
    for n, side in enumerate(sides):
        direct[n].wait_recv()
        piece = weights_ref.at[source(side), core, near_halves[n]]
        near_relays.append(
            start_remote(piece, piece, direct_send, direct_recv, 2 + n, at.device(pipe=side))
        )
        share(weights_ref.at[source(side), core, near])
    for d in others_y:
        for n, side in enumerate(sides):
            spread[(d - 1) * len(sides) + n].wait_recv()
            x = lanes(lax.rem(at.x + CHIPS_X - side, CHIPS_X))
            piece = weights_ref.at[source(d), core, far_halves[n], x]
            k = (len(others_y) + d - 1) * len(sides) + n
            far_relays.append(
                start_remote(piece, piece, spread_send, spread_recv, k, at.device(x=side))
            )
            share(weights_ref.at[source(d), core, far, x])
    for copy in near_relays:
        copy.wait_recv()
    share(weights_ref.at[source(2), core, near])
    opposite = lanes(lax.rem(at.x + 2, CHIPS_X))
    for d in others_y:
        for n in range(len(sides)):
            far_relays[(d - 1) * len(sides) + n].wait_recv()
        share(weights_ref.at[source(d), core, far, opposite])
    for copy in loads[CELLS_MAX:]:
        copy.wait()
    for copy in shared:
        copy.wait_recv()
    for copy in shared + split + direct + near_relays + spread + far_relays:
        copy.wait_send()


def gather_weights(weight, three, five, seven, features, sections):
    cells, channels = weight.shape[0], weight.shape[-1]
    weight = weight.reshape(cells, CORES, channels // CORES, channels)
    vmem = pl.BlockSpec(memory_space=pltpu.VMEM)
    anywhere = pl.BlockSpec(memory_space=pl.ANY)
    dma = pltpu.SemaphoreType.DMA
    ys, xs = sections - 1, CHIPS_X - 1
    rows = cells * channels // CORES + TAP_ROWS
    return pl.pallas_call(
        functools.partial(gather_kernel, sections),
        out_shape=(
            jax.ShapeDtypeStruct((sections, CORES, rows, channels), weight.dtype),
            jax.ShapeDtypeStruct((IMAGES * AREA, channels), features.dtype),
        ),
        in_specs=[anywhere, vmem, vmem, vmem, vmem],
        out_specs=(vmem, vmem),
        scratch_shapes=[
            pltpu.VMEM((CORES, TAP_ROWS, channels), jnp.float32),
            dma((4,)),
            dma((4,)),
            dma((ys,)),
            dma((ys,)),
            dma((ys * 4,)),
            dma((ys * 4,)),
            dma((2 * ys + ys * xs,)),
            dma((2 * ys + ys * xs,)),
            dma((CORES * cells,)),
        ],
        compiler_params=pltpu.CompilerParams(
            collective_id=0, has_side_effects=True, vmem_limit_bytes=24 * 1024 * 1024
        ),
        name="gather",
    )(weight, three, five, seven, features)


def reduce_kernel(
    sections,
    grad_ref,
    out_ref,
    pair_ref,
    part_ref,
    via_a_ref,
    via_b_ref,
    in_a1_ref,
    in_b1_ref,
    mid_a_ref,
    mid_b_ref,
    in_a2_ref,
    in_b2_ref,
    small_ref,
    in_z_ref,
    line_ref,
    plane_ref,
    pair_send,
    pair_recv,
    via_a_send,
    via_a_recv,
    via_b_send,
    via_b_recv,
    a1_send,
    a1_recv,
    b1_send,
    b1_recv,
    a2_send,
    a2_recv,
    b2_send,
    b2_recv,
    z_send,
    z_recv,
    line_send,
    line_recv,
    plane_send,
    plane_recv,
    core_send,
    core_recv,
    column_sem,
    half_sem,
):
    at = Place(sections)
    others_y = range(1, sections)
    others_x = range(1, CHIPS_X)
    others_z = range(1, CHIPS_Z)
    partner = at.device(core=1)
    at.signal(
        [partner]
        + [at.device(pipe=d) for d in others_y]
        + [at.device(x=d) for d in others_x]
        + [at.device(z=d) for d in others_z]
    )
    at.wait(1 + len(others_y) + len(others_x) + len(others_z))
    f32 = jnp.float32
    bf16 = jnp.bfloat16
    order = (2, 1, 3, 0)
    other_core = lax.rem(at.core + 1, CORES)
    all_z = pl.ds(0, CHIPS_Z)
    first_z = pl.ds(0, FIRST_Z)
    last_z = pl.ds(FIRST_Z, LAST_Z)
    last_all = pl.ds(0, LAST_Z)
    via_all = pl.ds(0, VIA_Z)
    sides = (1, 3)

    def lanes(x):
        return pl.ds(pl.multiple_of(x * LANES, LANES), LANES)

    def section_at(d):
        return lax.rem(at.pipe + d, sections)

    def stream(turn, start, size):
        rows = pl.ds(start, size)
        paired, via_a, via_b, a1, b1, a2, b2 = {}, {}, {}, {}, {}, {}, {}
        for k, d in enumerate(order):
            section = section_at(d)
            paired[d] = start_remote(
                grad_ref.at[section, other_core, all_z, rows],
                pair_ref.at[section, all_z, rows],
                pair_send,
                pair_recv,
                turn * sections + k,
                partner,
            )
        yield
        for d in order:
            section = section_at(d)
            paired[d].wait_recv()

            def add_pair(z, _, section=section):
                total = grad_ref[section, at.core, z, rows].astype(f32)
                total = total + pair_ref[section, z, rows].astype(f32)
                part_ref[section, z, rows] = total.astype(bf16)
                return 0

            lax.fori_loop(0, CHIPS_Z, add_pair, 0)
            for n, side in enumerate(sides):
                if d == 2:
                    via_a[side] = start_remote(
                        part_ref.at[section, pl.ds(n * VIA_Z, VIA_Z), rows],
                        via_a_ref.at[n, via_all, rows],
                        via_a_send,
                        via_a_recv,
                        turn * len(sides) + n,
                        at.device(pipe=side),
                    )
                via_b[d, side] = start_remote(
                    part_ref.at[
                        section,
                        pl.ds(FIRST_Z + n * VIA_Z, VIA_Z),
                        rows,
                        lanes(lax.rem(at.x + 2, CHIPS_X)),
                    ],
                    via_b_ref.at[n, section, via_all, rows],
                    via_b_send,
                    via_b_recv,
                    (turn * sections + d) * len(sides) + n,
                    at.device(x=side),
                )
        yield
        for n, side in enumerate(sides):
            section = section_at(side)
            via_a[side].wait_recv()

            def add_via_a(z, _, section=section, n=n):
                total = part_ref[section, n * VIA_Z + z, rows].astype(f32)
                total = total + via_a_ref[n, z, rows].astype(f32)
                part_ref[section, n * VIA_Z + z, rows] = total.astype(bf16)
                return 0

            lax.fori_loop(0, VIA_Z, add_via_a, 0)
            a1[side] = start_remote(
                part_ref.at[section, first_z, rows],
                in_a1_ref.at[n, first_z, rows],
                a1_send,
                a1_recv,
                turn * len(sides) + n,
                at.device(pipe=side),
            )
        for d in order:
            section = section_at(d)
            for n, side in enumerate(sides):
                via_b[d, side].wait_recv()
                place = lanes(lax.rem(at.x + side, CHIPS_X))

                def add_via_b(z, _, section=section, n=n, place=place):
                    row = FIRST_Z + n * VIA_Z + z
                    total = part_ref[section, row, rows, place].astype(f32)
                    total = total + via_b_ref[n, section, z, rows].astype(f32)
                    part_ref[section, row, rows, place] = total.astype(bf16)
                    return 0

                lax.fori_loop(0, VIA_Z, add_via_b, 0)
                b1[d, side] = start_remote(
                    part_ref.at[section, last_z, rows, place],
                    in_b1_ref.at[n, section, last_all, rows],
                    b1_send,
                    b1_recv,
                    (turn * sections + d) * len(sides) + n,
                    at.device(x=side),
                )
        yield
        for d in order:
            section = section_at(d)
            for side in sides:
                b1[d, side].wait_recv()

            def add_b1(z, _, section=section):
                total = part_ref[section, FIRST_Z + z, rows, lanes(at.x)].astype(f32)
                for n in range(len(sides)):
                    total = total + in_b1_ref[n, section, z, rows].astype(f32)
                mid_b_ref[section, z, rows] = total.astype(bf16)
                return 0

            lax.fori_loop(0, LAST_Z, add_b1, 0)
            if d:
                b2[d] = start_remote(
                    mid_b_ref.at[section, last_all, rows],
                    in_b2_ref.at[d - 1, last_all, rows],
                    b2_send,
                    b2_recv,
                    turn * len(others_y) + d - 1,
                    at.device(pipe=d),
                )
        for side in sides:
            a1[side].wait_recv()

        def add_a1(z, _):
            total = part_ref[at.pipe, z, rows].astype(f32)
            for n in range(len(sides)):
                total = total + in_a1_ref[n, z, rows].astype(f32)
            mid_a_ref[z, rows] = total.astype(bf16)
            return 0

        lax.fori_loop(0, FIRST_Z, add_a1, 0)
        for e in others_x:
            a2[e] = start_remote(
                mid_a_ref.at[first_z, rows, lanes(lax.rem(at.x + e, CHIPS_X))],
                in_a2_ref.at[e - 1, first_z, rows],
                a2_send,
                a2_recv,
                turn * len(others_x) + e - 1,
                at.device(x=e),
            )
        yield
        for d in others_y:
            b2[d].wait_recv()
        for e in others_x:
            a2[e].wait_recv()

        def add_a2(z, _):
            total = mid_a_ref[z, rows, lanes(at.x)].astype(f32)
            for e in others_x:
                total = total + in_a2_ref[e - 1, z, rows].astype(f32)
            small_ref[z, rows] = total.astype(bf16)
            return 0

        def add_b2(z, _):
            total = mid_b_ref[at.pipe, z, rows].astype(f32)
            for d in others_y:
                total = total + in_b2_ref[d - 1, z, rows].astype(f32)
            small_ref[FIRST_Z + z, rows] = total.astype(bf16)
            return 0

        lax.fori_loop(0, FIRST_Z, add_a2, 0)
        lax.fori_loop(0, LAST_Z, add_b2, 0)
        to_z = [
            start_remote(
                small_ref.at[lax.rem(at.z + d, CHIPS_Z), rows],
                in_z_ref.at[d - 1, rows],
                z_send,
                z_recv,
                turn * len(others_z) + d - 1,
                at.device(z=d),
            )
            for d in others_z
        ]
        yield
        for copy in to_z:
            copy.wait_recv()
        total = small_ref[at.z, rows].astype(f32)
        for d in others_z:
            total = total + in_z_ref[d - 1, rows].astype(f32)
        if turn in X_FIRST:
            plane_ref[at.z, rows, lanes(at.x)] = total.astype(bf16)
            piece = plane_ref.at[at.z, rows, lanes(at.x)]
            plane = [
                start_remote(
                    piece,
                    piece,
                    plane_send,
                    plane_recv,
                    turn * len(others_x) + e - 1,
                    at.device(x=e),
                )
                for e in others_x
            ]
            yield
            for copy in plane:
                copy.wait_recv()
            piece = plane_ref.at[at.z, rows]
        else:
            line_ref[at.z, rows] = total.astype(bf16)
            piece = line_ref.at[at.z, rows]
        line = [
            start_remote(
                piece,
                piece,
                line_send,
                line_recv,
                turn * len(others_z) + d - 1,
                at.device(z=d),
            )
            for d in others_z
        ]
        yield
        for copy in line:
            copy.wait_recv()
        if turn not in X_FIRST:
            column = plane_ref.at[all_z, rows, lanes(at.x)]
            plane = [
                start_remote(
                    line_ref.at[all_z, rows],
                    column,
                    plane_send,
                    plane_recv,
                    turn * len(others_x) + e - 1,
                    at.device(x=e),
                )
                for e in others_x
            ]
            own_column = start_local(line_ref.at[all_z, rows], column, column_sem, turn)
            yield
            own_column.wait()
            for copy in plane:
                copy.wait_recv()
        half = out_ref.at[at.core, all_z, rows]
        last = start_remote(
            plane_ref.at[all_z, rows], half, core_send, core_recv, turn, partner
        )
        own_half = start_local(plane_ref.at[all_z, rows], half, half_sem, turn)
        yield
        own_half.wait()
        last.wait()
        for copies in (paired, via_a, via_b, a1, b1, a2, b2):
            for copy in copies.values():
                copy.wait_send()
        for copy in to_z + line + plane:
            copy.wait_send()

    running = [stream(turn, *span) for turn, span in enumerate(STREAMS)]
    while running:
        running = [one for one in running if next(one, running) is None]


def reduce_grads(grads, sections):
    rows, channels = grads.shape[2:]
    grads = grads.reshape(sections, CORES, CHIPS_Z, CHUNK, channels)
    dma = pltpu.SemaphoreType.DMA
    ys, xs, zs, turns = sections - 1, CHIPS_X - 1, CHIPS_Z - 1, len(STREAMS)

    def vmem(*shape):
        return pltpu.VMEM(shape, jnp.bfloat16)

    out = pl.pallas_call(
        functools.partial(reduce_kernel, sections),
        out_shape=jax.ShapeDtypeStruct((CORES, CHIPS_Z, CHUNK, channels), jnp.bfloat16),
        in_specs=[pl.BlockSpec(memory_space=pltpu.VMEM)],
        out_specs=pl.BlockSpec(memory_space=pl.ANY),
        scratch_shapes=[
            vmem(sections, CHIPS_Z, CHUNK, channels),
            vmem(sections, CHIPS_Z, CHUNK, channels),
            vmem(2, VIA_Z, CHUNK, channels),
            vmem(2, sections, VIA_Z, CHUNK, LANES),
            vmem(2, FIRST_Z, CHUNK, channels),
            vmem(2, sections, LAST_Z, CHUNK, LANES),
            vmem(FIRST_Z, CHUNK, channels),
            vmem(sections, LAST_Z, CHUNK, LANES),
            vmem(xs, FIRST_Z, CHUNK, LANES),
            vmem(ys, LAST_Z, CHUNK, LANES),
            vmem(CHIPS_Z, CHUNK, LANES),
            vmem(zs, CHUNK, LANES),
            vmem(CHIPS_Z, CHUNK, LANES),
            vmem(CHIPS_Z, CHUNK, channels),
        ]
        + [
            dma((turns * count,))
            for count in (sections, 2, 2 * sections, 2, 2 * sections, xs, ys, zs, zs, xs, 1)
            for _ in ("send", "receive")
        ]
        + [dma((turns,)), dma((turns,))],
        compiler_params=pltpu.CompilerParams(
            collective_id=1, has_side_effects=True, vmem_limit_bytes=24 * 1024 * 1024
        ),
        name="reduce",
    )(grads)
    return out.reshape(CORES, rows, channels)


def own_taps(block, slot):
    size = 2 * slot + 3
    start = CELLS_MAX * block.shape[-1] // CORES + TAP_STARTS[slot]
    rows = block[TAP_HALVES[slot], start : start + size * size].astype(jnp.float32)
    return rows.reshape(1, size, size, block.shape[-1])


def shards(
    features,
    labels,
    micro_count,
    cells_per_section,
    point_weight,
    depth_three,
    depth_five,
    depth_seven,
    head_weight,
):
    sections = lax.axis_size("pipe")
    channels = point_weight.shape[-1]
    by_position = features.transpose(1, 2, 0, 3).reshape(-1, channels)
    weights, own = gather_weights(
        point_weight[0], depth_three[0], depth_five[0], depth_seven[0], by_position, sections
    )
    grads = run_cells(cells_per_section, labels, micro_count, own, weights, head_weight.T)
    block = reduce_grads(grads, sections)
    span = channels // CORES
    point_rows = CELLS_MAX * span
    loss_start = point_rows + TAP_ROWS
    total_loss = jnp.sum(block[0, loss_start : loss_start + 3].astype(jnp.float32))
    point_sum = block[:, :point_rows].reshape(CORES, CELLS_MAX, span, channels)
    point_sum = point_sum.transpose(1, 0, 2, 3).astype(jnp.float32)
    return (
        total_loss,
        point_sum.reshape(1, CELLS_MAX, channels, channels),
        own_taps(block, 0),
        own_taps(block, 1),
        own_taps(block, 2),
    )


def solution(mesh):
    return jax.shard_map(
        shards,
        mesh=mesh,
        in_specs=(
            P("dp", None, None, None),
            P("dp"),
            P("dp"),
            P(),
            P("pipe", None, None, None),
            P("pipe", None, None, None),
            P("pipe", None, None, None),
            P("pipe", None, None, None),
            P(),
        ),
        out_specs=(
            P(),
            P("pipe", None, None, None),
            P("pipe", None, None, None),
            P("pipe", None, None, None),
            P("pipe", None, None, None),
        ),
        check_vma=False,
    )
```
